32 devices in a mesh: groups: 2 (over y), lat: 4 (over z), lev: 2 (over x), tr: 2 (over core).
Axes of the slice: x: 2, y: 2, z: 4, core: 2. Of those that a mesh axis runs over, the one named last changes fastest.
Arguments:
- adjoint_in: float32 [4, 24, 32, 512], P(('groups', 'tr'), 'lev', 'lat'), parts along dimension 0, may hold values from -6 to 6
- courant: float32 [2, 24, 32, 512], P(None, 'lev', 'lat'), may hold values from -0.45 to 0.45
- diffusion: float32 [23, 32, 512], P(None, 'lat', 'lev'), may hold values from 0.3 to 6
- tile_values: float32 [4, 24, 256, 128], P(('groups', 'tr'), 'lev', 'lat'), parts along dimension 0, may hold values from -6 to 6
- tile_region: int32 [512, 1], P(('groups', 'lat')), parts along dimension 0, may hold values from 0 to 3; in each aligned block of 64 rows (0 to 63, 64 to 127, ...) at most 16 rows name the same one
- tile_cell: int32 [512], P(('groups', 'lat')), parts along dimension 0, may hold values from 0 to 31
Outputs:
- adjoint_out: float32 [4, 24, 32, 512], P(('groups', 'tr'), 'lev', 'lat'), parts along dimension 0
- flux_gradient: float32 [4, 32, 512], P(('groups', 'tr'), 'lat', 'lev'), parts along dimension 0
The draws below stay inside these ranges and needn't reach their ends.
There are 2 independent parts, one for each index of `groups`. The reference program is written for one: setup_inputs(seed, part) draws one part's arguments, and reference() takes and returns one part's arrays. A program takes and returns all parts, laid end to end along the dimension named above; an argument that names none is the same for every part. Nothing has to cross between parts.
Inputs may be any that keep to these rules, and one draw needn't show every extreme that they name: `tile_region`: among the tiles of one index of lat (aligned blocks of 64 tiles) at most 16 name any one band, a bound that some block reaches of them.
All inputs are finite; a program needn't handle non-finite values.
Results may differ from the reference program's by a relative error of at most 0.0001.
Values sent between devices are 32-bit elements; how exact they have to be, the bound alone decides.
No kernel may reach another device: no remote copies, remote signals or barrier semaphores. Data moves between devices by JAX's collectives and lax.ppermute only.
A program may use at most 64 MiB of HBM per device.

```python
import math
import jax
import jax.numpy as jnp
import numpy as np
from jax import lax

TR = 2
LEV = 24
LAT_DEV = 8
NLON = 512
TILE_W = 128
TILE_DEV = 64
STEPS = 6
NLAT = 32
REGIONS = 4
TILES = 256
CAP = 16
NBLK = 4


def place_ends(entries, rng, least, top_value):
    longest = entries.shape.index(max(entries.shape))
    spots = []
    for shift in (0, 1):
        where = [jax.random.randint(jax.random.fold_in(rng, axis), (), 0, length) for axis, length in enumerate(entries.shape)]
        where[longest] = (where[longest] + shift) % entries.shape[longest]
        spots.append(tuple(where))
    return entries.at[spots[0]].set(least).at[spots[1]].set(top_value)


def steps_of(stream_key, extent, cuts, least, high):
    def one(position, parts):
        heights = jax.random.uniform(jax.random.fold_in(jax.random.fold_in(stream_key, 6), position), (parts,), jnp.float32, least / len(cuts), high / len(cuts))
        return jnp.repeat(jnp.exp(heights), extent[position] // parts).reshape((-1,) + (1,) * (len(extent) - position - 1))

    level = one(*cuts[0])
    for cut in cuts[1:]:
        level = level * one(*cut)
    return level


def assign_block(own_key, own, number, rows, amount, top, most, skew):
    ranking = jax.random.permutation(own_key, amount)
    heavy_load, common = portions_of(amount, rows * top, most, skew, True), portions_of(amount, rows * top, most, skew, False)
    places = jnp.arange(amount)

    def named(lengths, turn):
        used = int((lengths > 0).sum())
        fixed = max(1, used // 4)
        passed = fixed + (places - fixed + turn * (used - fixed)) % max(1, amount - fixed)
        return jnp.zeros((amount,), jnp.int32).at[ranking[jnp.where(places < fixed, places, passed)]].set(jnp.asarray(lengths, jnp.int32))

    lengths = jnp.where(number % 4 == 0, named(heavy_load, number // 4), named(common, number - number // 4 - 1))
    mixed = jax.random.permutation(jax.random.fold_in(own, 3), amount)
    donor, taker = mixed[0:amount // 2 * 2:2], mixed[1:amount // 2 * 2:2]
    slack = jnp.minimum(lengths[donor] - 1, most - lengths[taker]) // 2
    slack = jnp.where((donor == ranking[0]) | (taker == ranking[0]) | (lengths[taker] == 0), 0, jnp.maximum(slack, 0))
    passed = jax.random.randint(jax.random.fold_in(own, 4), (amount // 2,), 0, 1 << 20) % (slack + 1)
    lengths = lengths.at[donor].add(-passed).at[taker].add(passed)
    labels = jnp.searchsorted(jnp.cumsum(lengths), jnp.arange(rows * top), side="right").astype(jnp.int32)
    listing = labels.reshape(top, rows).T
    listing = listing[jax.random.permutation(jax.random.fold_in(own, 1), rows)]
    turn = jax.random.randint(jax.random.fold_in(own, 2), (rows, 1), 0, top)
    return jnp.take_along_axis(listing, (jnp.arange(top)[None, :] + turn) % top, axis=1)


def portions_of(amount, total, most, skew, full):
    loads = [(1 << 20) // math.isqrt(rank ** skew) + 1 for rank in range(1, amount + 1)]
    largest = most if full else min(most, max(-(-total // amount), total * loads[0] // sum(loads)))
    least = 1 if total - largest >= amount - 1 else 0
    holding, surplus = [largest] + [least] * (amount - 1), total - largest - least * (amount - 1)
    while surplus > 0:
        candidates = [i for i in range(1, amount) if holding[i] < largest] or [i for i in range(1, amount) if holding[i] < most]
        mass, left = sum([loads[i] for i in candidates]), surplus
        for i in candidates:
            extra = min(most - holding[i], max(1, left * loads[i] // mass), surplus)
            holding[i] = holding[i] + extra
            surplus = surplus - extra
    return np.array(holding)


def noise(rng, dims, spread, reach, shards=(), kind=jnp.bfloat16):
    gain = steps_of(rng, dims, shards, -0.22, 0.18) if shards else 1.0
    entries = jax.random.normal(rng, dims, jnp.float32) * spread * gain
    return jnp.minimum(jnp.maximum(entries, -reach), reach).astype(kind)


def setup_inputs(seed: int = 0, part: int = 0) -> dict:
    keys = jax.random.split(jax.random.key(seed), 7)
    own_keys = jax.random.split(jax.random.fold_in(keys[6], part), 7)
    adjoint_in = noise(own_keys[0], (TR, LEV, NLAT, NLON), 1.0, 6.0, ((0, 2), (1, 2), (2, 4)), jnp.float32)
    courant = jnp.clip(jax.random.uniform(keys[1], (2, LEV, NLAT, NLON), jnp.float32, -0.45, 0.45) * steps_of(keys[1], (2, LEV, NLAT, NLON), ((1, 2), (2, 4)), -0.4, 0.0), -0.45, 0.45)
    diffusion = jnp.clip(jnp.exp(math.log(6.0) - 2.9957322 * jax.random.uniform(keys[2], (LEV - 1, NLAT, NLON), jnp.float32) ** steps_of(keys[2], (LEV - 1, NLAT, NLON), ((1, 4), (2, 2)), -0.2, 0.2)), 0.3, 6.0)
    tile_values = noise(own_keys[3], (TR, LEV, TILES, TILE_W), 1.0, 6.0, ((0, 2), (1, 2), (2, 4)), jnp.float32)
    tile_region_keys = jax.random.split(jax.random.fold_in(own_keys[4], 1), TILES // TILE_DEV)
    tile_region_turns = jax.random.permutation(jax.random.fold_in(own_keys[4], 3), TILES // TILE_DEV)
    tile_region = jax.vmap(lambda own, number: assign_block(jax.random.fold_in(own_keys[4], 2), own, number, TILE_DEV, REGIONS, 1, CAP, 2))(tile_region_keys, tile_region_turns).reshape((TILES, 1))
    tile_cell = place_ends(jax.random.randint(own_keys[5], (TILES,), 0, LAT_DEV * NBLK), jax.random.fold_in(own_keys[5], 1), 0, (LAT_DEV * NBLK) - 1).astype(jnp.int32)
    return dict(adjoint_in=adjoint_in, courant=courant, diffusion=diffusion, tile_values=tile_values, tile_region=tile_region, tile_cell=tile_cell)


def periodic_pad(field, dim):
    count = field.shape[dim]
    first = lax.slice_in_dim(field, 0, 1, axis=dim)
    last = lax.slice_in_dim(field, count - 1, count, axis=dim)
    return jnp.concatenate([last, field, first], axis=dim)


def zero_pad(field, dim):
    widths = [(0, 0)] * field.ndim
    widths[dim] = (1, 1)
    return jnp.pad(field, widths)


def advect_adjoint(padded, faces, dim):
    count = padded.shape[dim] - 2
    center = lax.slice_in_dim(padded, 1, count + 1, axis=dim)
    upper = lax.slice_in_dim(padded, 2, count + 2, axis=dim)
    lower = lax.slice_in_dim(padded, 0, count, axis=dim)
    east = jnp.maximum(lax.slice_in_dim(faces, 2, count + 2, axis=dim), 0.0)
    west = jnp.minimum(lax.slice_in_dim(faces, 1, count + 1, axis=dim), 0.0)
    return center + east * (upper - center) + west * (center - lower)


def column_factors(diffusion):
    levels = diffusion.shape[0] + 1
    gains = []
    inverses = []
    for level in range(levels):
        if level < levels - 1:
            pivot = 1.0 + diffusion[level]
        else:
            pivot = jnp.ones_like(diffusion[0])
        if level > 0:
            pivot = pivot + diffusion[level - 1] - diffusion[level - 1] * gains[level - 1]
        inverse = 1.0 / pivot
        inverses.append(inverse)
        if level < levels - 1:
            gains.append(diffusion[level] * inverse)
    return gains, inverses


def column_solve(field, diffusion, gains, inverses):
    levels = len(inverses)
    forward = [field[:, 0] * inverses[0]]
    for level in range(1, levels):
        forward.append((field[:, level] + diffusion[level - 1] * forward[level - 1]) * inverses[level])
    result = [forward[levels - 1]]
    for level in range(levels - 2, -1, -1):
        result.append(forward[level] + gains[level] * result[-1])
    return jnp.stack(list(reversed(result)), axis=1)


def reference(adjoint_in, courant, diffusion, tile_values, tile_region, tile_cell):
    rows = lax.broadcasted_iota(jnp.int32, (1, 1, NLAT, 1), 2)
    faces_lat = courant[1:2] * (rows != 0).astype(jnp.float32)
    faces_lon = courant[0:1]
    lat_faces = zero_pad(faces_lat, 2)
    lon_faces = periodic_pad(faces_lon, 3)
    gains, inverses = column_factors(diffusion)
    field = adjoint_in
    flux = jnp.zeros((TR, NLAT, NLON), jnp.float32)
    for step in range(STEPS):
        field = column_solve(field, diffusion, gains, inverses)
        flux = flux + field[:, 0]
        field = advect_adjoint(zero_pad(field, 2), lat_faces, 2)
        field = advect_adjoint(periodic_pad(field, 3), lon_faces, 3)
    cells = (tile_region[:, 0] * (LAT_DEV * NBLK) + tile_cell).astype(jnp.int32)
    flat = field.reshape(TR, LEV, NLAT * NBLK, TILE_W)
    flat = flat.at[:, :, cells, :].add(tile_values)
    return flat.reshape(TR, LEV, NLAT, NLON), flux / STEPS
```

```python
import functools

import jax
import jax.numpy as jnp
from jax import lax
from jax.experimental import pallas as pl
from jax.experimental.pallas import tpu as pltpu
from jax.sharding import PartitionSpec as P

STEPS = 6
F32 = jnp.float32


def call(body, out_shapes, *args):
    spec = pl.BlockSpec(memory_space=pltpu.VMEM)
    return pl.pallas_call(
        body,
        out_shape=[jax.ShapeDtypeStruct(shape, F32) for shape in out_shapes],
        in_specs=[spec] * len(args),
        out_specs=[spec] * len(out_shapes),
        compiler_params=pltpu.CompilerParams(vmem_limit_bytes=24 * 1024 * 1024),
    )(*args)


def order(i, count, upper):
    return jnp.where(upper, i, count - 1 - i)


def upper_half(devices):
    return lax.axis_index("lev") < devices // 2


def prepare_body(devices, field, window, courant, face_north, gain_in, y_in, *outs):
    r_out, a_out, g_out, me_out, mw_out, ze_out, zw_out, y_out, ends_out = outs
    count, rows, width = field.shape
    upper = upper_half(devices)
    row = lax.broadcasted_iota(jnp.int32, (rows, width), 0)
    first_row = (row == 0) & (lax.axis_index("lat") == 0)
    gain, y = gain_in[...], y_in[...]
    for i in range(count):
        level = order(i, count, upper)
        k_prev = window[jnp.where(upper, i, count - i)]
        k_next = window[jnp.where(upper, i + 1, count - 1 - i)]
        inverse = 1.0 / (1.0 + k_prev + k_next - k_prev * gain)
        gain = k_next * inverse
        a = k_prev * inverse
        r_out[i], a_out[i], g_out[i] = inverse, a, gain
        y = field[level] * inverse + a * y
        y_out[i] = y
        south = courant[1, level]
        north = pltpu.roll(south, rows - 1, 0)
        north = jnp.where(row == rows - 1, face_north[pl.ds(level, 1), :], north)
        me_out[i] = jnp.maximum(north, 0.0)
        mw_out[i] = jnp.where(first_row, 0.0, jnp.minimum(south, 0.0))
        west = courant[0, level]
        ze_out[i] = jnp.maximum(pltpu.roll(west, width - 1, 1), 0.0)
        zw_out[i] = jnp.minimum(west, 0.0)
    ends_out[0] = y
    ends_out[1] = gain


def back_body(devices, first, *refs):
    if first:
        y, other, g, lam, south, north, flux, scale_out = refs
    else:
        y, other, g, scale, flux_in, lam, south, north, flux = refs
    count, rows, _ = y.shape
    last = count - 1
    if first:
        at = lax.axis_index("lev")
        middle = (at == devices // 2) | (at == devices // 2 - 1)
        scale = jnp.where(middle, 1.0 / (1.0 - g[last] * other[1]), 1.0)
        scale_out[...] = scale
        met = other[0]
    else:
        scale = scale[...]
        met = other[...]
    w = (y[last] + g[last] * met) * scale
    for i in range(last, -1, -1):
        if i < last:
            w = y[i] + g[i] * w
        lam[i] = w
        south[pl.ds(i, 1), :] = w[0:1, :]
        north[pl.ds(i, 1), :] = w[rows - 1 : rows, :]
    flux[...] = w if first else flux_in[...] + w


def advect(i, lam, below, above, me, mw, ze, zw):
    _, rows, width = lam.shape
    row = lax.broadcasted_iota(jnp.int32, (rows, width), 0)
    v = lam[i]
    up = jnp.where(row == rows - 1, above[pl.ds(i, 1), :], pltpu.roll(v, rows - 1, 0))
    down = jnp.where(row == 0, below[pl.ds(i, 1), :], pltpu.roll(v, 1, 0))
    v = v + me[i] * (up - v) + mw[i] * (v - down)
    east = pltpu.roll(v, width - 1, 1)
    west = pltpu.roll(v, 1, 1)
    return v + ze[i] * (east - v) + zw[i] * (v - west)


def forward_body(lam, below, above, me, mw, ze, zw, r, a, y_in, y_out, end_out):
    y = y_in[...]
    for i in range(lam.shape[0]):
        y = advect(i, lam, below, above, me, mw, ze, zw) * r[i] + a[i] * y
        y_out[i] = y
    end_out[...] = y


def finish_body(devices, lam, below, above, me, mw, ze, zw, *rest):
    buckets, out = rest[:-1], rest[-1]
    count, rows, width = lam.shape
    upper = upper_half(devices)
    cells = jnp.concatenate([bucket[count] for bucket in buckets], axis=0)
    tile = cells.shape[1]
    blocks = width // tile
    lane = lax.broadcasted_iota(jnp.int32, cells.shape, 1)
    place = (lane % rows * blocks + lane // rows).astype(F32)
    hits = jnp.where((cells == place) & (lane < rows * blocks), 1.0, 0.0)
    hits = hits.T[: rows * blocks]
    for i in range(count):
        level = order(i, count, upper)
        v = advect(i, lam, below, above, me, mw, ze, zw)
        values = jnp.concatenate([bucket[level] for bucket in buckets], axis=0)
        added = lax.dot_general(
            hits, values, (((1,), (0,)), ((), ())), precision=lax.Precision.HIGHEST, preferred_element_type=F32
        )
        for block in range(blocks):
            out[level, :, block * tile : (block + 1) * tile] = (
                v[:, block * tile : (block + 1) * tile] + added[block * rows : (block + 1) * rows]
            )


def bucket_body(regions, values, region_column, region_row, cell_column, *outs):
    count, tiles, tile = values.shape
    capacity = outs[0].shape[1]
    band = lax.axis_index("lat")
    earlier = lax.broadcasted_iota(jnp.int32, (tiles, tiles), 0) < lax.broadcasted_iota(jnp.int32, (tiles, tiles), 1)
    same = (region_column[...] == region_row[...]) & earlier
    rank = jnp.sum(jnp.where(same, 1.0, 0.0), axis=0, keepdims=True).astype(jnp.int32)
    slot = lax.broadcasted_iota(jnp.int32, (capacity, tiles), 0)
    cells = jnp.broadcast_to(cell_column[...].astype(F32), (tiles, tile))
    picks = [
        jnp.where((slot == rank) & (region_row[...] == lax.rem(band + s, regions)), 1.0, 0.0) for s in range(regions)
    ]
    picks = jnp.concatenate(picks, axis=0)
    for level in range(count + 1):
        got = lax.dot_general(
            picks,
            cells if level == count else values[level],
            (((1,), (0,)), ((), ())),
            precision=lax.Precision.HIGHEST,
            preferred_element_type=F32,
        )
        for s in range(regions):
            outs[s][level] = got[s * capacity : (s + 1) * capacity]


def route_tiles(tile_values, tile_region, tile_cell):
    regions = lax.axis_size("lat")
    count, tiles, tile = tile_values.shape
    outs = call(
        functools.partial(bucket_body, regions),
        [(count + 1, tiles // 4, tile)] * regions,
        tile_values,
        tile_region,
        tile_region.reshape(1, tiles),
        tile_cell.reshape(tiles, 1),
    )
    got = [outs[0]]
    for s in range(1, regions):
        got.append(lax.ppermute(outs[s], "lat", [(b, (b + s) % regions) for b in range(regions)]))
    return got


def diffusion_window(diffusion, count):
    devices = lax.axis_size("lev")
    at = lax.axis_index("lev")
    chunk = diffusion.shape[2]
    padded = jnp.pad(diffusion, ((1, 1), (0, 0), (0, 0)))
    parts = []
    for shift in range(devices):
        target = lax.rem(at + shift, devices)
        part = lax.dynamic_slice_in_dim(padded, target * count, count + 1, axis=0)
        if shift:
            part = lax.ppermute(part, "lev", [(p, (p + shift) % devices) for p in range(devices)])
        parts.append(part)
    parts = jnp.stack(parts)
    return jnp.concatenate([parts[(at - p) % devices] for p in range(devices)], axis=2)


def local(adjoint_in, courant, diffusion, tile_values, tile_region, tile_cell):
    field = adjoint_in[0]
    count, rows, width = field.shape
    devices = lax.axis_size("lev")
    bands = lax.axis_size("lat")
    half = devices // 2
    at = lax.axis_index("lev")
    outermost = (at == 0) | (at == devices - 1)
    innermost = (at == half) | (at == half - 1)
    inward = [(p, p + 1) for p in range(half - 1)] + [(p, p - 1) for p in range(half + 1, devices)]
    outward = [(b, a) for a, b in inward]
    meet = [(half - 1, half), (half, half - 1)]
    northward = [(b, b + 1) for b in range(bands - 1)]
    southward = [(b + 1, b) for b in range(bands - 1)]

    buckets = route_tiles(tile_values[0], tile_region, tile_cell)
    window = diffusion_window(diffusion, count)
    face_north = lax.ppermute(courant[1, :, 0, :], "lat", southward)

    whole, plane, edge = (count, rows, width), (rows, width), (count, width)
    zero = jnp.zeros(plane, F32)
    gain_in, y_in = zero, zero
    for turn in range(half):
        r, a, g, me, mw, ze, zw, y, ends = call(
            functools.partial(prepare_body, devices),
            [whole] * 8 + [(2,) + plane],
            field,
            window,
            courant,
            face_north,
            gain_in,
            y_in,
        )
        if turn < half - 1:
            passed = jnp.where(outermost, 0.0, lax.ppermute(ends, "lev", inward))
            y_in, gain_in = passed[0], passed[1]

    for step in range(STEPS):
        met = lax.ppermute(ends, "lev", meet)
        for turn in range(half):
            if step == 0:
                lam, south, north, new_flux, scale = call(
                    functools.partial(back_body, devices, True), [whole, edge, edge, plane, plane], y, met, g
                )
            else:
                lam, south, north, new_flux = call(
                    functools.partial(back_body, devices, False),
                    [whole, edge, edge, plane],
                    y,
                    met,
                    g,
                    scale,
                    flux,
                )
            if turn < half - 1:
                passed = lax.ppermute(lam[0], "lev", outward)
                if step == 0:
                    passed = jnp.stack([passed, jnp.zeros_like(passed)])
                met = jnp.where(innermost, met, passed)
        flux = new_flux
        below = lax.ppermute(north, "lat", northward)
        above = lax.ppermute(south, "lat", southward)
        args = (lam, below, above, me, mw, ze, zw)
        if step == STEPS - 1:
            (out,) = call(functools.partial(finish_body, devices), [whole], *args, *buckets)
            break
        y_in = zero
        for turn in range(half):
            y, ends = call(forward_body, [whole, plane], *args, r, a, y_in)
            if turn < half - 1:
                y_in = jnp.where(outermost, 0.0, lax.ppermute(ends, "lev", inward))

    flux = flux / STEPS
    chunk = width // devices
    share = flux[:, :chunk]
    for p in range(1, devices):
        sent = lax.ppermute(flux[:, p * chunk : (p + 1) * chunk], "lev", [(0, p)])
        share = jnp.where(at == p, sent, share)
    return out[None], share[None]


def solution(mesh):
    return jax.shard_map(
        local,
        mesh=mesh,
        in_specs=(
            P(("groups", "tr"), "lev", "lat", None),
            P(None, "lev", "lat", None),
            P(None, "lat", "lev"),
            P(("groups", "tr"), "lev", "lat", None),
            P(("groups", "lat"), None),
            P(("groups", "lat")),
        ),
        out_specs=(P(("groups", "tr"), "lev", "lat", None), P(("groups", "tr"), "lat", "lev")),
        check_vma=False,
    )
```

```python
import functools

import jax
import jax.numpy as jnp
from jax import lax
from jax.experimental import pallas as pl
from jax.experimental.pallas import tpu as pltpu
from jax.sharding import PartitionSpec as P

STEPS = 6
F32 = jnp.float32


def call(body, out_shapes, *args):
    spec = pl.BlockSpec(memory_space=pltpu.VMEM)
    return pl.pallas_call(
        body,
        out_shape=[jax.ShapeDtypeStruct(shape, F32) for shape in out_shapes],
        in_specs=[spec] * len(args),
        out_specs=[spec] * len(out_shapes),
        compiler_params=pltpu.CompilerParams(vmem_limit_bytes=24 * 1024 * 1024),
    )(*args)


def order(i, count, upper):
    return jnp.where(upper, i, count - 1 - i)


def upper_half(devices):
    return lax.axis_index("lev") < devices // 2


def even_band():
    return lax.rem(lax.axis_index("lat"), 2) == 0


def band_swaps(bands, first):
    swaps = []
    for b in range(bands):
        partner = b + 1 if (b - first) % 2 == 0 else b - 1
        swaps.append((b, partner if 0 <= partner < bands else b))
    return swaps


def partner_of(band, shift, bands):
    if bands & (bands - 1) == 0:
        return band ^ shift
    return (band + shift) % bands


def prepare_body(devices, bands, field, window, courant, face_north, gain_in, y_in, *outs):
    r_out, a_out, g_out, me_out, mw_out, ze_out, zw_out, y_out, ends_out = outs
    count, rows, width = field.shape
    upper = upper_half(devices)
    row = lax.broadcasted_iota(jnp.int32, (rows, width), 0)
    first_row = (row == 0) & (lax.axis_index("lat") == 0)
    last_row = (row == rows - 1) & (lax.axis_index("lat") == bands - 1)
    gain, y = gain_in[...], y_in[...]
    for i in range(count):
        level = order(i, count, upper)
        k_prev = window[jnp.where(upper, i, count - i)]
        k_next = window[jnp.where(upper, i + 1, count - 1 - i)]
        inverse = 1.0 / (1.0 + k_prev + k_next - k_prev * gain)
        gain = k_next * inverse
        a = k_prev * inverse
        r_out[i], a_out[i], g_out[i] = inverse, a, gain
        y = field[level] * inverse + a * y
        y_out[i] = y
        south = courant[1, level]
        north = pltpu.roll(south, rows - 1, 0)
        north = jnp.where(row == rows - 1, face_north[pl.ds(level, 1), :], north)
        me_out[i] = jnp.where(last_row, 0.0, jnp.maximum(north, 0.0))
        mw_out[i] = jnp.where(first_row, 0.0, jnp.minimum(south, 0.0))
        west = courant[0, level]
        ze_out[i] = jnp.maximum(pltpu.roll(west, width - 1, 1), 0.0)
        zw_out[i] = jnp.minimum(west, 0.0)
    ends_out[0] = y
    ends_out[1] = gain


def back_body(devices, first, *refs):
    if first:
        y, other, g, lam, edge_a, edge_b, flux, scale_out = refs
    else:
        y, other, g, scale, flux_in, lam, edge_a, edge_b, flux = refs
    count, rows, _ = y.shape
    last = count - 1
    if first:
        at = lax.axis_index("lev")
        middle = (at == devices // 2) | (at == devices // 2 - 1)
        scale = jnp.where(middle, 1.0 / (1.0 - g[last] * other[1]), 1.0)
        scale_out[...] = scale
        met = other[0]
    else:
        scale = scale[...]
        met = other[...]
    w = (y[last] + g[last] * met) * scale
    even = even_band()
    for i in range(last, -1, -1):
        if i < last:
            w = y[i] + g[i] * w
        lam[i] = w
        south, north = w[0:1, :], w[rows - 1 : rows, :]
        edge_a[pl.ds(i, 1), :] = jnp.where(even, north, south)
        edge_b[pl.ds(i, 1), :] = jnp.where(even, south, north)
    flux[...] = w if first else flux_in[...] + w


def advect(i, lam, edge_a, edge_b, me, mw, ze, zw):
    _, rows, width = lam.shape
    row = lax.broadcasted_iota(jnp.int32, (rows, width), 0)
    v = lam[i]
    even = even_band()
    a, b = edge_a[pl.ds(i, 1), :], edge_b[pl.ds(i, 1), :]
    up = jnp.where(row == rows - 1, jnp.where(even, a, b), pltpu.roll(v, rows - 1, 0))
    down = jnp.where(row == 0, jnp.where(even, b, a), pltpu.roll(v, 1, 0))
    v = v + me[i] * (up - v) + mw[i] * (v - down)
    east = pltpu.roll(v, width - 1, 1)
    west = pltpu.roll(v, 1, 1)
    return v + ze[i] * (east - v) + zw[i] * (v - west)


def forward_body(lam, edge_a, edge_b, me, mw, ze, zw, r, a, y_in, y_out, end_out):
    y = y_in[...]
    for i in range(lam.shape[0]):
        y = advect(i, lam, edge_a, edge_b, me, mw, ze, zw) * r[i] + a[i] * y
        y_out[i] = y
    end_out[...] = y


def finish_body(devices, lam, edge_a, edge_b, me, mw, ze, zw, *rest):
    buckets, out = rest[:-1], rest[-1]
    count, rows, width = lam.shape
    upper = upper_half(devices)
    cells = jnp.concatenate([bucket[count] for bucket in buckets], axis=0)
    tile = cells.shape[1]
    blocks = width // tile
    lane = lax.broadcasted_iota(jnp.int32, cells.shape, 1)
    place = (lane % rows * blocks + lane // rows).astype(F32)
    hits = jnp.where((cells == place) & (lane < rows * blocks), 1.0, 0.0)
    hits = hits.T[: rows * blocks]
    for i in range(count):
        level = order(i, count, upper)
        v = advect(i, lam, edge_a, edge_b, me, mw, ze, zw)
        values = jnp.concatenate([bucket[level] for bucket in buckets], axis=0)
        added = lax.dot_general(
            hits, values, (((1,), (0,)), ((), ())), precision=lax.Precision.HIGHEST, preferred_element_type=F32
        )
        for block in range(blocks):
            out[level, :, block * tile : (block + 1) * tile] = (
                v[:, block * tile : (block + 1) * tile] + added[block * rows : (block + 1) * rows]
            )


def bucket_body(regions, values, region_column, region_row, cell_column, *outs):
    count, tiles, tile = values.shape
    capacity = outs[0].shape[1]
    band = lax.axis_index("lat")
    earlier = lax.broadcasted_iota(jnp.int32, (tiles, tiles), 0) < lax.broadcasted_iota(jnp.int32, (tiles, tiles), 1)
    same = (region_column[...] == region_row[...]) & earlier
    rank = jnp.sum(jnp.where(same, 1.0, 0.0), axis=0, keepdims=True).astype(jnp.int32)
    slot = lax.broadcasted_iota(jnp.int32, (capacity, tiles), 0)
    cells = jnp.broadcast_to(cell_column[...].astype(F32), (tiles, tile))
    picks = [
        jnp.where((slot == rank) & (region_row[...] == partner_of(band, s, regions)), 1.0, 0.0) for s in range(regions)
    ]
    picks = jnp.concatenate(picks, axis=0)
    for level in range(count + 1):
        got = lax.dot_general(
            picks,
            cells if level == count else values[level],
            (((1,), (0,)), ((), ())),
            precision=lax.Precision.HIGHEST,
            preferred_element_type=F32,
        )
        for s in range(regions):
            outs[s][level] = got[s * capacity : (s + 1) * capacity]


def route_tiles(tile_values, tile_region, tile_cell):
    regions = lax.axis_size("lat")
    count, tiles, tile = tile_values.shape
    outs = call(
        functools.partial(bucket_body, regions),
        [(count + 1, tiles // 4, tile)] * regions,
        tile_values,
        tile_region,
        tile_region.reshape(1, tiles),
        tile_cell.reshape(tiles, 1),
    )
    got = [outs[0]]
    for s in range(1, regions):
        got.append(lax.ppermute(outs[s], "lat", [(b, partner_of(b, s, regions)) for b in range(regions)]))
    return got


def diffusion_window(diffusion, count):
    devices = lax.axis_size("lev")
    at = lax.axis_index("lev")
    chunk = diffusion.shape[2]
    padded = jnp.pad(diffusion, ((1, 1), (0, 0), (0, 0)))
    parts = []
    for shift in range(devices):
        target = lax.rem(at + shift, devices)
        part = lax.dynamic_slice_in_dim(padded, target * count, count + 1, axis=0)
        if shift:
            part = lax.ppermute(part, "lev", [(p, (p + shift) % devices) for p in range(devices)])
        parts.append(part)
    parts = jnp.stack(parts)
    return jnp.concatenate([parts[(at - p) % devices] for p in range(devices)], axis=2)


def local(adjoint_in, courant, diffusion, tile_values, tile_region, tile_cell):
    field = adjoint_in[0]
    count, rows, width = field.shape
    devices = lax.axis_size("lev")
    bands = lax.axis_size("lat")
    half = devices // 2
    at = lax.axis_index("lev")
    outermost = (at == 0) | (at == devices - 1)
    innermost = (at == half) | (at == half - 1)
    inward = [(p, p + 1) for p in range(half - 1)] + [(p, p - 1) for p in range(half + 1, devices)]
    outward = [(b, a) for a, b in inward]
    meet = [(half - 1, half), (half, half - 1)]
    swaps_a, swaps_b = band_swaps(bands, 0), band_swaps(bands, 1)

    buckets = route_tiles(tile_values[0], tile_region, tile_cell)
    window = diffusion_window(diffusion, count)
    face_north = lax.ppermute(courant[1, :, 0, :], "lat", [(b, (b - 1) % bands) for b in range(bands)])

    whole, plane, edge = (count, rows, width), (rows, width), (count, width)
    zero = jnp.zeros(plane, F32)
    gain_in, y_in = zero, zero
    for turn in range(half):
        r, a, g, me, mw, ze, zw, y, ends = call(
            functools.partial(prepare_body, devices, bands),
            [whole] * 8 + [(2,) + plane],
            field,
            window,
            courant,
            face_north,
            gain_in,
            y_in,
        )
        if turn < half - 1:
            passed = jnp.where(outermost, 0.0, lax.ppermute(ends, "lev", inward))
            y_in, gain_in = passed[0], passed[1]

    for step in range(STEPS):
        met = lax.ppermute(ends, "lev", meet)
        for turn in range(half):
            if step == 0:
                lam, edge_a, edge_b, new_flux, scale = call(
                    functools.partial(back_body, devices, True), [whole, edge, edge, plane, plane], y, met, g
                )
            else:
                lam, edge_a, edge_b, new_flux = call(
                    functools.partial(back_body, devices, False),
                    [whole, edge, edge, plane],
                    y,
                    met,
                    g,
                    scale,
                    flux,
                )
            if turn < half - 1:
                passed = lax.ppermute(lam[0], "lev", outward)
                if step == 0:
                    passed = jnp.stack([passed, jnp.zeros_like(passed)])
                met = jnp.where(innermost, met, passed)
        flux = new_flux
        edge_a = lax.ppermute(edge_a, "lat", swaps_a)
        edge_b = lax.ppermute(edge_b, "lat", swaps_b)
        args = (lam, edge_a, edge_b, me, mw, ze, zw)
        if step == STEPS - 1:
            (out,) = call(functools.partial(finish_body, devices), [whole], *args, *buckets)
            break
        y_in = zero
        for turn in range(half):
            y, ends = call(forward_body, [whole, plane], *args, r, a, y_in)
            if turn < half - 1:
                y_in = jnp.where(outermost, 0.0, lax.ppermute(ends, "lev", inward))

    flux = flux / STEPS
    chunk = width // devices
    share = flux[:, :chunk]
    for p in range(1, devices):
        sent = lax.ppermute(flux[:, p * chunk : (p + 1) * chunk], "lev", [(0, p), (p, 0)])
        share = jnp.where(at == p, sent, share)
    return out[None], share[None]


def solution(mesh):
    return jax.shard_map(
        local,
        mesh=mesh,
        in_specs=(
            P(("groups", "tr"), "lev", "lat", None),
            P(None, "lev", "lat", None),
            P(None, "lat", "lev"),
            P(("groups", "tr"), "lev", "lat", None),
            P(("groups", "lat"), None),
            P(("groups", "lat")),
        ),
        out_specs=(P(("groups", "tr"), "lev", "lat", None), P(("groups", "tr"), "lat", "lev")),
        check_vma=False,
    )
```

```python
import functools

import jax
import jax.numpy as jnp
from jax import lax
from jax.experimental import pallas as pl
from jax.experimental.pallas import tpu as pltpu
from jax.sharding import PartitionSpec as P

STEPS = 6
HALO = STEPS
LANES = 128
F32 = jnp.float32


def call(body, out_shapes, *args, scratch=()):
    spec = pl.BlockSpec(memory_space=pltpu.VMEM)
    return pl.pallas_call(
        body,
        out_shape=[jax.ShapeDtypeStruct(shape, F32) for shape in out_shapes],
        in_specs=[spec] * len(args),
        out_specs=[spec] * len(out_shapes),
        scratch_shapes=[pltpu.VMEM(shape, F32) for shape in scratch],
        compiler_params=pltpu.CompilerParams(vmem_limit_bytes=32 * 1024 * 1024),
    )(*args)


def partner_of(index, turn, count):
    if count & (count - 1) == 0:
        return index ^ turn
    return (index + turn) % count


def source_of(index, turn, count):
    if count & (count - 1) == 0:
        return index ^ turn
    return (index - turn) % count


def rounds(count):
    return [[(b, partner_of(b, turn, count)) for b in range(count)] for turn in range(1, count)]


def band_swaps(bands, first):
    swaps = []
    for b in range(bands):
        partner = b + 1 if (b - first) % 2 == 0 else b - 1
        swaps.append((b, partner if 0 <= partner < bands else b))
    return swaps


class Plan:
    def __init__(self, count, rows, width, devices):
        self.count, self.rows, self.width, self.devices = count, rows, width, devices
        self.levels = count * devices
        self.chunk = width // devices
        self.full = self.chunk // LANES
        self.rest = self.chunk % LANES
        self.window = (self.full + 1) * LANES
        assert self.rest + 2 * HALO <= LANES
        self.middle = (self.rest + LANES) // 2
        self.pitch = -(-(self.rest + 2 * HALO) // 16) * 16
        self.slots = LANES // self.pitch
        self.edge_slots = LANES // 16
        fields = 3 * count
        self.rests_at = fields * self.full
        self.diffusion_at = self.rests_at + -(-fields // self.slots)
        self.diffusion_tiles = -(-self.chunk // LANES)
        self.own_size = self.diffusion_at + (self.levels - 1) * self.diffusion_tiles
        self.sent_size = self.diffusion_at + -(-(self.levels - 1) // self.edge_slots)

    def packed(self, size):
        return size - size // 4 if 4 * HALO == 3 * self.rows else size


def lane_of(rows=8):
    return lax.broadcasted_iota(jnp.int32, (rows, LANES), 1)


def row_of(rows=8):
    return lax.broadcasted_iota(jnp.int32, (rows, LANES), 0)


def turn_lanes(tile, shift):
    return pltpu.roll(tile, shift % LANES, 1) if shift % LANES else tile


def turn_rows(tile, shift):
    rows = tile.shape[0]
    return pltpu.roll(tile, shift % rows, 0) if shift % rows else tile


def pack_lanes(tiles, slots, pitch):
    packed = []
    lane = lane_of(tiles[0].shape[0])
    for begin in range(0, len(tiles), slots):
        total = jnp.zeros_like(tiles[0])
        for slot, tile in enumerate(tiles[begin : begin + slots]):
            moved = turn_lanes(tile, HALO + slot * pitch)
            if slots > 1:
                moved = jnp.where((lane >= slot * pitch) & (lane < (slot + 1) * pitch), moved, total)
            total = moved
        packed.append(total)
    return packed


def unpack_lanes(tile, slot, pitch):
    return turn_lanes(tile, -HALO - slot * pitch)


def window_tiles(plan, ref, index, target):
    if plan.rest == 0:
        def at(column):
            return ref[index + (slice(None), pl.ds(pl.multiple_of(column, LANES), LANES))]

        full = [at(target * plan.chunk + t * LANES) for t in range(plan.full)]
        east = at(lax.rem(target + 1, plan.devices) * plan.chunk)
        west = at(lax.rem(target + plan.devices - 1, plan.devices) * plan.chunk + plan.chunk - LANES)
    else:
        line = pltpu.roll(ref[index], lax.rem(plan.width - target * plan.chunk, plan.width), 1)
        full = [line[:, t * LANES : (t + 1) * LANES] for t in range(plan.full)]
        east = line[:, plan.full * LANES : (plan.full + 1) * LANES]
        west = line[:, plan.width - LANES :]
    return full, jnp.where(lane_of(plan.rows) < plan.middle, east, west)


def field_tiles(plan, field, courant, target):
    tiles, rests = [], []
    for ref, lead in ((field, ()), (courant, (0,)), (courant, (1,))):
        for level in range(plan.count):
            full, rest = window_tiles(plan, ref, lead + (level,), target)
            tiles += full
            rests.append(rest)
    return tiles + pack_lanes(rests, plan.slots, plan.pitch)


def diffusion_tile(plan, diffusion, level, t):
    width = min(LANES, plan.chunk - t * LANES)
    tile = diffusion[level, :, t * LANES : t * LANES + width]
    if width < LANES:
        tile = jnp.concatenate([tile, jnp.zeros((plan.rows, LANES - width), F32)], axis=1)
    return tile


def pack_rows(plan, get, size, north, store):
    first = plan.rows - HALO if north else 0
    row = row_of(plan.rows)
    place = 0
    fours = size // 4 if plan.packed(size) < size else 0
    for four in range(fours):
        tiles = [get(4 * four + j) for j in range(4)]
        for j in range(3):
            extra = turn_rows(tiles[3], HALO - first - 2 * j)
            store(place, jnp.where(row < HALO, turn_rows(tiles[j], -first), extra))
            place += 1
    for index in range(4 * fours, size):
        store(place, turn_rows(get(index), -first))
        place += 1


def unpack_rows(plan, get, size, north, store):
    first = plan.rows - HALO if north else 0
    row = row_of(plan.rows)
    place = 0
    fours = size // 4 if plan.packed(size) < size else 0
    for four in range(fours):
        tiles = [get(place + j) for j in range(3)]
        place += 3
        last = jnp.zeros_like(tiles[0])
        for j in range(3):
            store(4 * four + j, turn_rows(tiles[j], first))
            moved = turn_rows(tiles[j], first + 2 * j - HALO)
            last = jnp.where((row >= first + 2 * j) & (row < first + 2 * j + 2), moved, last)
        store(4 * four + 3, last)
    for index in range(4 * fours, size):
        store(index, turn_rows(get(place), first))
        place += 1


def by_parity(body):
    even = lax.rem(lax.axis_index("lat"), 2) == 0

    @pl.when(even)
    def _():
        body(True)

    @pl.when(jnp.logical_not(even))
    def _():
        body(False)


def pack_body(plan, field, courant, diffusion, own, swap_a, swap_b, *sent):
    me = lax.axis_index("lev")
    tiles = field_tiles(plan, field, courant, me)
    for level in range(plan.levels - 1):
        tiles += [diffusion_tile(plan, diffusion, level, t) for t in range(plan.diffusion_tiles)]
    for index, tile in enumerate(tiles):
        own[index] = tile
    edges = []
    for level in range(plan.levels - 1):
        first = diffusion_tile(plan, diffusion, level, 0)
        last = turn_lanes(diffusion_tile(plan, diffusion, level, plan.diffusion_tiles - 1), -plan.rest)
        edges.append(jnp.where(lane_of(plan.rows) < LANES // 2, first, last))
    edges = pack_lanes(edges, plan.edge_slots, 16)
    for turn in range(1, plan.devices):
        target = partner_of(me, turn, plan.devices)
        for index, tile in enumerate(field_tiles(plan, field, courant, target) + edges):
            sent[turn - 1][index] = tile

    def rows(even):
        for north, swap in ((even, swap_a), (not even, swap_b)):
            pack_rows(plan, lambda i: own[i], plan.own_size, north, swap.__setitem__)

    by_parity(rows)


def forward_rows_body(plan, *refs):
    turns = plan.devices - 1
    got, swap_a, swap_b = refs[:turns], refs[turns], refs[turns + 1]
    size = plan.packed(plan.sent_size)

    def rows(even):
        for north, swap in ((even, swap_a), (not even, swap_b)):
            for turn in range(turns):
                def store(index, tile, base=turn * size, swap=swap):
                    swap[base + index] = tile

                pack_rows(plan, lambda i, turn=turn: got[turn][i], plan.sent_size, north, store)

    by_parity(rows)


def steps_body(plan, bands, *refs):
    turns = plan.devices - 1
    own, early_a, early_b, late_a, late_b = refs[:5]
    got = refs[5 : 5 + turns]
    outs = refs[5 + turns : 5 + turns + plan.devices]
    flux = refs[5 + turns + plan.devices]
    lists, lam, face_e, face_w, lat_e, lat_w, r, a, g = refs[6 + turns + plan.devices :]
    me, band = lax.axis_index("lev"), lax.axis_index("lat")
    rows, levels = plan.rows, plan.levels

    late_size = plan.packed(plan.sent_size)

    def unpack(even):
        for side, from_north in ((1, True), (2, False)):
            early, late = (early_a, late_a) if even == from_north else (early_b, late_b)

            def store(index, tile, base=0, side=side):
                lists[side - 1, base + index] = tile

            unpack_rows(plan, lambda i, e=early: e[i], plan.own_size, not from_north, store)
            for turn in range(turns):
                base = plan.own_size + turn * plan.sent_size
                unpack_rows(
                    plan,
                    lambda i, l=late, t=turn: l[t * late_size + i],
                    plan.sent_size,
                    not from_north,
                    functools.partial(store, base=base),
                )

    by_parity(unpack)

    def tile_of(side, turn, index):
        if side:
            return lists[side - 1, index if turn == 0 else plan.own_size + (turn - 1) * plan.sent_size + index]
        return own[index] if turn == 0 else got[turn - 1][index]

    lane = lane_of(rows)
    for side in range(3):
        at = pl.ds(side * rows, rows)
        for turn in range(plan.devices):
            base = source_of(me, turn, plan.devices) * plan.count if turn else me * plan.count
            for kind, target in enumerate((lam, face_w, lat_w)):
                for level in range(plan.count):
                    item = kind * plan.count + level
                    for t in range(plan.full):
                        target[base + level, at, t * LANES : (t + 1) * LANES] = tile_of(side, turn, item * plan.full + t)
                    rest = tile_of(side, turn, plan.rests_at + item // plan.slots)
                    target[base + level, at, plan.full * LANES :] = unpack_lanes(rest, item % plan.slots, plan.pitch)
        for level in range(levels - 1):
            for t in range(plan.full):
                g[level, at, t * LANES : (t + 1) * LANES] = tile_of(
                    side, 0, plan.diffusion_at + level * plan.diffusion_tiles + t
                )
            east = west = jnp.zeros((rows, LANES), F32)
            for turn in range(1, plan.devices):
                edge = tile_of(side, turn, plan.diffusion_at + level // plan.edge_slots)
                edge = unpack_lanes(edge, level % plan.edge_slots, 16)
                if turns == 1:
                    east = west = edge
                else:
                    source = source_of(me, turn, plan.devices)
                    east = jnp.where(source == lax.rem(me + 1, plan.devices), edge, east)
                    west = jnp.where(source == lax.rem(me + plan.devices - 1, plan.devices), edge, west)
            rest = jnp.where(lane < plan.middle, turn_lanes(east, plan.rest), west)
            if plan.rest:
                mine = tile_of(side, 0, plan.diffusion_at + level * plan.diffusion_tiles + plan.full)
                rest = jnp.where(lane < plan.rest, mine, rest)
            g[level, at, plan.full * LANES :] = rest

    row = lax.broadcasted_iota(jnp.int32, (3 * rows, plan.window), 0)
    closed = ((row == 0) & (band == 0)) | ((row == rows) & (band == bands - 1))
    zero = jnp.zeros((3 * rows, plan.window), F32)
    k_prev = gain = zero
    for level in range(levels):
        south = jnp.where(closed, 0.0, lat_w[level])
        lat_e[level] = jnp.maximum(pltpu.roll(south, 3 * rows - 1, 0), 0.0)
        lat_w[level] = jnp.minimum(south, 0.0)
        west = face_w[level]
        face_e[level] = jnp.maximum(pltpu.roll(west, plan.window - 1, 1), 0.0)
        face_w[level] = jnp.minimum(west, 0.0)
        k_next = g[level] if level < levels - 1 else zero
        inverse = 1.0 / (1.0 + k_prev + k_next - k_prev * gain)
        gain = k_next * inverse
        r[level], a[level], g[level] = inverse, k_prev * inverse, gain
        k_prev = k_next

    flux[...] = jnp.zeros_like(flux)

    def step(_, carry):
        y = zero
        for level in range(levels):
            y = lam[level] * r[level] + a[level] * y
            lam[level] = y
        w = zero
        for level in range(levels - 1, -1, -1):
            w = lam[level] + g[level] * w
            up, down = pltpu.roll(w, 3 * rows - 1, 0), pltpu.roll(w, 1, 0)
            v = w + lat_e[level] * (up - w) + lat_w[level] * (w - down)
            east, west = pltpu.roll(v, plan.window - 1, 1), pltpu.roll(v, 1, 1)
            lam[level] = v + face_e[level] * (east - v) + face_w[level] * (v - west)
        flux[...] += w[:rows, : plan.chunk]
        return carry

    lax.fori_loop(0, STEPS, step, 0)
    flux[...] = flux[...] / STEPS
    for turn in range(plan.devices):
        base = (partner_of(me, turn, plan.devices) if turn else me) * plan.count
        for level in range(plan.count):
            outs[turn][level] = lam[base + level, :rows, : plan.chunk]


def finish_body(plan, regions, *refs):
    parts, buckets, out = refs[: plan.devices], refs[plan.devices : -1], refs[-1]
    count, rows, width = plan.count, plan.rows, plan.width
    me = lax.axis_index("lev")
    cells = jnp.concatenate([bucket[count] for bucket in buckets], axis=0)
    tile = cells.shape[1]
    blocks = width // tile
    lane = lax.broadcasted_iota(jnp.int32, cells.shape, 1)
    place = (lane % rows * blocks + lane // rows).astype(F32)
    hits = jnp.where((cells == place) & (lane < rows * blocks), 1.0, 0.0)
    hits = hits.T[: rows * blocks]
    for level in range(count):
        values = jnp.concatenate([bucket[level] for bucket in buckets], axis=0)
        added = lax.dot_general(
            hits, values, (((1,), (0,)), ((), ())), precision=lax.Precision.HIGHEST, preferred_element_type=F32
        )
        chunks = []
        for q in range(plan.devices):
            piece = parts[0][level]
            for turn in range(1, plan.devices):
                piece = jnp.where(source_of(me, turn, plan.devices) == q, parts[turn][level], piece)
            chunks.append(piece)
        v = jnp.concatenate(chunks, axis=1)
        for block in range(blocks):
            out[level, :, block * tile : (block + 1) * tile] = (
                v[:, block * tile : (block + 1) * tile] + added[block * rows : (block + 1) * rows]
            )


def bucket_body(regions, values, region_column, region_row, cell_column, *outs):
    count, tiles, tile = values.shape
    capacity = outs[0].shape[1]
    band = lax.axis_index("lat")
    earlier = lax.broadcasted_iota(jnp.int32, (tiles, tiles), 0) < lax.broadcasted_iota(jnp.int32, (tiles, tiles), 1)
    same = (region_column[...] == region_row[...]) & earlier
    rank = jnp.sum(jnp.where(same, 1.0, 0.0), axis=0, keepdims=True).astype(jnp.int32)
    slot = lax.broadcasted_iota(jnp.int32, (capacity, tiles), 0)
    cells = jnp.broadcast_to(cell_column[...].astype(F32), (tiles, tile))
    picks = [
        jnp.where((slot == rank) & (region_row[...] == partner_of(band, s, regions)), 1.0, 0.0) for s in range(regions)
    ]
    picks = jnp.concatenate(picks, axis=0)
    for level in range(count + 1):
        got = lax.dot_general(
            picks,
            cells if level == count else values[level],
            (((1,), (0,)), ((), ())),
            precision=lax.Precision.HIGHEST,
            preferred_element_type=F32,
        )
        for s in range(regions):
            outs[s][level] = got[s * capacity : (s + 1) * capacity]


def route_tiles(tile_values, tile_region, tile_cell):
    regions = lax.axis_size("lat")
    count, tiles, tile = tile_values.shape
    outs = call(
        functools.partial(bucket_body, regions),
        [(count + 1, tiles // 4, tile)] * regions,
        tile_values,
        tile_region,
        tile_region.reshape(1, tiles),
        tile_cell.reshape(tiles, 1),
    )
    return [outs[0]] + [lax.ppermute(out, "lat", pairs) for out, pairs in zip(outs[1:], rounds(regions))]


def local(adjoint_in, courant, diffusion, tile_values, tile_region, tile_cell):
    field = adjoint_in[0]
    count, rows, width = field.shape
    devices = lax.axis_size("lev")
    bands = lax.axis_size("lat")
    plan = Plan(count, rows, width, devices)
    swaps_a, swaps_b = band_swaps(bands, 0), band_swaps(bands, 1)
    tile = (rows, LANES)

    early = plan.packed(plan.own_size)
    late = plan.packed(plan.sent_size) * (devices - 1)
    own, early_a, early_b, *sent = call(
        functools.partial(pack_body, plan),
        [(plan.own_size,) + tile] + [(early,) + tile] * 2 + [(plan.sent_size,) + tile] * (devices - 1),
        field,
        courant,
        diffusion,
    )
    got = [lax.ppermute(part, "lev", pairs) for part, pairs in zip(sent, rounds(devices))]
    early_a = lax.ppermute(early_a, "lat", swaps_a)
    early_b = lax.ppermute(early_b, "lat", swaps_b)
    late_a, late_b = call(functools.partial(forward_rows_body, plan), [(late,) + tile] * 2, *got)
    late_a = lax.ppermute(late_a, "lat", swaps_a)
    late_b = lax.ppermute(late_b, "lat", swaps_b)

    whole = (plan.levels, 3 * rows, plan.window)
    lists = (2, plan.own_size + (devices - 1) * plan.sent_size) + tile
    *outs, flux = call(
        functools.partial(steps_body, plan, bands),
        [(count, rows, plan.chunk)] * devices + [(rows, plan.chunk)],
        own,
        early_a,
        early_b,
        late_a,
        late_b,
        *got,
        scratch=[lists] + [whole] * 8,
    )
    parts = [outs[0]] + [lax.ppermute(part, "lev", pairs) for part, pairs in zip(outs[1:], rounds(devices))]
    buckets = route_tiles(tile_values[0], tile_region, tile_cell)
    (out,) = call(functools.partial(finish_body, plan, bands), [(count, rows, width)], *parts, *buckets)
    return out[None], flux[None]


def solution(mesh):
    return jax.shard_map(
        local,
        mesh=mesh,
        in_specs=(
            P(("groups", "tr"), "lev", "lat", None),
            P(None, "lev", "lat", None),
            P(None, "lat", "lev"),
            P(("groups", "tr"), "lev", "lat", None),
            P(("groups", "lat"), None),
            P(("groups", "lat")),
        ),
        out_specs=(P(("groups", "tr"), "lev", "lat", None), P(("groups", "tr"), "lat", "lev")),
        check_vma=False,
    )
```

```python
import functools

import jax
import jax.numpy as jnp
from jax import lax
from jax.experimental import pallas as pl
from jax.experimental.pallas import tpu as pltpu
from jax.sharding import PartitionSpec as P

STEPS = 6
HALO = STEPS
LANES = 128
F32 = jnp.float32


def call(body, out_shapes, *args, scratch=(), semaphores=0, inputs=pltpu.VMEM):
    spec = pl.BlockSpec(memory_space=pltpu.VMEM)
    shapes = [pltpu.VMEM(shape, F32) for shape in scratch]
    if semaphores:
        shapes.append(pltpu.SemaphoreType.DMA((semaphores,)))
    return pl.pallas_call(
        body,
        out_shape=[jax.ShapeDtypeStruct(shape, F32) for shape in out_shapes],
        in_specs=[pl.BlockSpec(memory_space=inputs)] * len(args),
        out_specs=[spec] * len(out_shapes),
        scratch_shapes=shapes,
        compiler_params=pltpu.CompilerParams(vmem_limit_bytes=32 * 1024 * 1024),
    )(*args)


def partner_of(index, turn, count):
    if count & (count - 1) == 0:
        return index ^ turn
    return (index + turn) % count


def source_of(index, turn, count):
    if count & (count - 1) == 0:
        return index ^ turn
    return (index - turn) % count


def rounds(count):
    return [[(b, partner_of(b, turn, count)) for b in range(count)] for turn in range(1, count)]


def band_swaps(bands, first):
    swaps = []
    for b in range(bands):
        partner = b + 1 if (b - first) % 2 == 0 else b - 1
        swaps.append((b, partner if 0 <= partner < bands else b))
    return swaps


class Plan:
    def __init__(self, count, rows, width, devices):
        self.count, self.rows, self.width, self.devices = count, rows, width, devices
        self.levels = count * devices
        self.chunk = width // devices
        self.full = self.chunk // LANES
        self.rest = self.chunk % LANES
        self.window = (self.full + 1) * LANES
        assert self.rest + 2 * HALO <= LANES
        self.middle = (self.rest + LANES) // 2
        self.pitch = -(-(self.rest + 2 * HALO) // 16) * 16
        self.slots = LANES // self.pitch
        self.edge_slots = LANES // 16
        fields = 3 * count
        self.rests_at = fields * self.full
        self.diffusion_at = self.rests_at + -(-fields // self.slots)
        self.diffusion_tiles = -(-self.chunk // LANES)
        self.own_size = self.diffusion_at + (self.levels - 1) * self.diffusion_tiles
        self.sent_size = self.diffusion_at + -(-(self.levels - 1) // self.edge_slots)

    def packed(self, size):
        return size - size // 4 if 4 * HALO == 3 * self.rows else size


def lane_of(rows=8):
    return lax.broadcasted_iota(jnp.int32, (rows, LANES), 1)


def row_of(rows=8):
    return lax.broadcasted_iota(jnp.int32, (rows, LANES), 0)


def turn_lanes(tile, shift):
    return pltpu.roll(tile, shift % LANES, 1) if shift % LANES else tile


def turn_rows(tile, shift):
    rows = tile.shape[0]
    return pltpu.roll(tile, shift % rows, 0) if shift % rows else tile


def pack_lanes(tiles, slots, pitch):
    packed = []
    lane = lane_of(tiles[0].shape[0])
    for begin in range(0, len(tiles), slots):
        total = jnp.zeros_like(tiles[0])
        for slot, tile in enumerate(tiles[begin : begin + slots]):
            moved = turn_lanes(tile, HALO + slot * pitch)
            if slots > 1:
                moved = jnp.where((lane >= slot * pitch) & (lane < (slot + 1) * pitch), moved, total)
            total = moved
        packed.append(total)
    return packed


def unpack_lanes(tile, slot, pitch):
    return turn_lanes(tile, -HALO - slot * pitch)


def window_tiles(plan, ref, index, target):
    if plan.rest == 0:
        def at(column):
            return ref[index + (slice(None), pl.ds(pl.multiple_of(column, LANES), LANES))]

        full = [at(target * plan.chunk + t * LANES) for t in range(plan.full)]
        east = at(lax.rem(target + 1, plan.devices) * plan.chunk)
        west = at(lax.rem(target + plan.devices - 1, plan.devices) * plan.chunk + plan.chunk - LANES)
    else:
        line = pltpu.roll(ref[index], lax.rem(plan.width - target * plan.chunk, plan.width), 1)
        full = [line[:, t * LANES : (t + 1) * LANES] for t in range(plan.full)]
        east = line[:, plan.full * LANES : (plan.full + 1) * LANES]
        west = line[:, plan.width - LANES :]
    return full, jnp.where(lane_of(plan.rows) < plan.middle, east, west)


def field_tiles(plan, field, courant, target):
    tiles, rests = [], []
    for ref, lead in ((field, ()), (courant, (0,)), (courant, (1,))):
        for level in range(plan.count):
            full, rest = window_tiles(plan, ref, lead + (level,), target)
            tiles += full
            rests.append(rest)
    return tiles + pack_lanes(rests, plan.slots, plan.pitch)


def diffusion_tile(plan, diffusion, level, t):
    width = min(LANES, plan.chunk - t * LANES)
    tile = diffusion[level, :, t * LANES : t * LANES + width]
    if width < LANES:
        tile = jnp.concatenate([tile, jnp.zeros((plan.rows, LANES - width), F32)], axis=1)
    return tile


def pack_rows(plan, get, size, north, store):
    first = plan.rows - HALO if north else 0
    row = row_of(plan.rows)
    place = 0
    fours = size // 4 if plan.packed(size) < size else 0
    for four in range(fours):
        tiles = [get(4 * four + j) for j in range(4)]
        for j in range(3):
            extra = turn_rows(tiles[3], HALO - first - 2 * j)
            store(place, jnp.where(row < HALO, turn_rows(tiles[j], -first), extra))
            place += 1
    for index in range(4 * fours, size):
        store(place, turn_rows(get(index), -first))
        place += 1


def unpack_rows(plan, get, size, north, store):
    first = plan.rows - HALO if north else 0
    row = row_of(plan.rows)
    place = 0
    fours = size // 4 if plan.packed(size) < size else 0
    for four in range(fours):
        tiles = [get(place + j) for j in range(3)]
        place += 3
        last = jnp.zeros_like(tiles[0])
        for j in range(3):
            store(4 * four + j, turn_rows(tiles[j], first))
            moved = turn_rows(tiles[j], first + 2 * j - HALO)
            last = jnp.where((row >= first + 2 * j) & (row < first + 2 * j + 2), moved, last)
        store(4 * four + 3, last)
    for index in range(4 * fours, size):
        store(index, turn_rows(get(place), first))
        place += 1


def by_parity(body):
    even = lax.rem(lax.axis_index("lat"), 2) == 0

    @pl.when(even)
    def _():
        body(True)

    @pl.when(jnp.logical_not(even))
    def _():
        body(False)


def pack_body(plan, *refs):
    sources, (own, swap_a, swap_b), sent = refs[:3], refs[3:6], refs[6:-4]
    field, courant, diffusion, arrived = refs[-4:]
    copies = [
        pltpu.make_async_copy(source, target, arrived.at[i])
        for i, (source, target) in enumerate(zip(sources, (field, courant, diffusion)))
    ]
    for copy in copies:
        copy.start()
    for copy in copies:
        copy.wait()
    me = lax.axis_index("lev")
    tiles = field_tiles(plan, field, courant, me)
    for level in range(plan.levels - 1):
        tiles += [diffusion_tile(plan, diffusion, level, t) for t in range(plan.diffusion_tiles)]
    for index, tile in enumerate(tiles):
        own[index] = tile
    edges = []
    for level in range(plan.levels - 1):
        first = diffusion_tile(plan, diffusion, level, 0)
        last = turn_lanes(diffusion_tile(plan, diffusion, level, plan.diffusion_tiles - 1), -plan.rest)
        edges.append(jnp.where(lane_of(plan.rows) < LANES // 2, first, last))
    edges = pack_lanes(edges, plan.edge_slots, 16)
    for turn in range(1, plan.devices):
        target = partner_of(me, turn, plan.devices)
        for index, tile in enumerate(field_tiles(plan, field, courant, target) + edges):
            sent[turn - 1][index] = tile

    def rows(even):
        for north, swap in ((even, swap_a), (not even, swap_b)):
            pack_rows(plan, lambda i: own[i], plan.own_size, north, swap.__setitem__)

    by_parity(rows)


def forward_rows_body(plan, *refs):
    turns = plan.devices - 1
    got, swap_a, swap_b = refs[:turns], refs[turns], refs[turns + 1]
    size = plan.packed(plan.sent_size)

    def rows(even):
        for north, swap in ((even, swap_a), (not even, swap_b)):
            for turn in range(turns):
                def store(index, tile, base=turn * size, swap=swap):
                    swap[base + index] = tile

                pack_rows(plan, lambda i, turn=turn: got[turn][i], plan.sent_size, north, store)

    by_parity(rows)


def steps_body(plan, bands, *refs):
    turns = plan.devices - 1
    own, early_a, early_b, late_a, late_b = refs[:5]
    got = refs[5 : 5 + turns]
    outs = refs[5 + turns : 5 + turns + plan.devices]
    flux = refs[5 + turns + plan.devices]
    lists, lam, face_e, face_w, lat_e, lat_w, r, a, g = refs[6 + turns + plan.devices :]
    me, band = lax.axis_index("lev"), lax.axis_index("lat")
    rows, levels = plan.rows, plan.levels

    late_size = plan.packed(plan.sent_size)

    def unpack(even):
        for side, from_north in ((1, True), (2, False)):
            early, late = (early_a, late_a) if even == from_north else (early_b, late_b)

            def store(index, tile, base=0, side=side):
                lists[side - 1, base + index] = tile

            unpack_rows(plan, lambda i, e=early: e[i], plan.own_size, not from_north, store)
            for turn in range(turns):
                base = plan.own_size + turn * plan.sent_size
                unpack_rows(
                    plan,
                    lambda i, l=late, t=turn: l[t * late_size + i],
                    plan.sent_size,
                    not from_north,
                    functools.partial(store, base=base),
                )

    by_parity(unpack)

    def tile_of(side, turn, index):
        if side:
            return lists[side - 1, index if turn == 0 else plan.own_size + (turn - 1) * plan.sent_size + index]
        return own[index] if turn == 0 else got[turn - 1][index]

    lane = lane_of(rows)
    for side in range(3):
        at = pl.ds(side * rows, rows)
        for turn in range(plan.devices):
            base = source_of(me, turn, plan.devices) * plan.count if turn else me * plan.count
            for kind, target in enumerate((lam, face_w, lat_w)):
                for level in range(plan.count):
                    item = kind * plan.count + level
                    for t in range(plan.full):
                        target[base + level, at, t * LANES : (t + 1) * LANES] = tile_of(side, turn, item * plan.full + t)
                    rest = tile_of(side, turn, plan.rests_at + item // plan.slots)
                    target[base + level, at, plan.full * LANES :] = unpack_lanes(rest, item % plan.slots, plan.pitch)
        for level in range(levels - 1):
            for t in range(plan.full):
                g[level, at, t * LANES : (t + 1) * LANES] = tile_of(
                    side, 0, plan.diffusion_at + level * plan.diffusion_tiles + t
                )
            east = west = jnp.zeros((rows, LANES), F32)
            for turn in range(1, plan.devices):
                edge = tile_of(side, turn, plan.diffusion_at + level // plan.edge_slots)
                edge = unpack_lanes(edge, level % plan.edge_slots, 16)
                if turns == 1:
                    east = west = edge
                else:
                    source = source_of(me, turn, plan.devices)
                    east = jnp.where(source == lax.rem(me + 1, plan.devices), edge, east)
                    west = jnp.where(source == lax.rem(me + plan.devices - 1, plan.devices), edge, west)
            rest = jnp.where(lane < plan.middle, turn_lanes(east, plan.rest), west)
            if plan.rest:
                mine = tile_of(side, 0, plan.diffusion_at + level * plan.diffusion_tiles + plan.full)
                rest = jnp.where(lane < plan.rest, mine, rest)
            g[level, at, plan.full * LANES :] = rest

    row = lax.broadcasted_iota(jnp.int32, (3 * rows, plan.window), 0)
    closed = ((row == 0) & (band == 0)) | ((row == rows) & (band == bands - 1))
    zero = jnp.zeros((3 * rows, plan.window), F32)
    k_prev = gain = zero
    for level in range(levels):
        south = jnp.where(closed, 0.0, lat_w[level])
        lat_e[level] = jnp.maximum(pltpu.roll(south, 3 * rows - 1, 0), 0.0)
        lat_w[level] = jnp.minimum(south, 0.0)
        west = face_w[level]
        face_e[level] = jnp.maximum(pltpu.roll(west, plan.window - 1, 1), 0.0)
        face_w[level] = jnp.minimum(west, 0.0)
        k_next = g[level] if level < levels - 1 else zero
        inverse = 1.0 / (1.0 + k_prev + k_next - k_prev * gain)
        gain = k_next * inverse
        r[level], a[level], g[level] = inverse, k_prev * inverse, gain
        k_prev = k_next

    flux[...] = jnp.zeros_like(flux)

    def step(_, carry):
        y = zero
        for level in range(levels):
            y = lam[level] * r[level] + a[level] * y
            lam[level] = y
        w = zero
        for level in range(levels - 1, -1, -1):
            w = lam[level] + g[level] * w
            up, down = pltpu.roll(w, 3 * rows - 1, 0), pltpu.roll(w, 1, 0)
            v = w + lat_e[level] * (up - w) + lat_w[level] * (w - down)
            east, west = pltpu.roll(v, plan.window - 1, 1), pltpu.roll(v, 1, 1)
            lam[level] = v + face_e[level] * (east - v) + face_w[level] * (v - west)
        flux[...] += w[:rows, : plan.chunk]
        return carry

    lax.fori_loop(0, STEPS, step, 0)
    flux[...] = flux[...] / STEPS
    for turn in range(plan.devices):
        base = (partner_of(me, turn, plan.devices) if turn else me) * plan.count
        for level in range(plan.count):
            outs[turn][level] = lam[base + level, :rows, : plan.chunk]


def sum_body(plan, *refs):
    buckets, out = refs[:-1], refs[-1]
    count, rows, width = plan.count, plan.rows, plan.width
    cells = jnp.concatenate([bucket[count] for bucket in buckets], axis=0)
    tile = cells.shape[1]
    blocks = width // tile
    lane = lax.broadcasted_iota(jnp.int32, cells.shape, 1)
    place = (lane % rows * blocks + lane // rows).astype(F32)
    hits = jnp.where((cells == place) & (lane < rows * blocks), 1.0, 0.0)
    hits = hits.T[: rows * blocks]
    for level in range(count):
        values = jnp.concatenate([bucket[level] for bucket in buckets], axis=0)
        added = lax.dot_general(
            hits, values, (((1,), (0,)), ((), ())), precision=lax.Precision.HIGHEST, preferred_element_type=F32
        )
        for block in range(blocks):
            out[level, :, block * tile : (block + 1) * tile] = added[block * rows : (block + 1) * rows]


def finish_body(plan, *refs):
    parts, added, out = refs[: plan.devices], refs[plan.devices], refs[-1]
    me = lax.axis_index("lev")
    for level in range(plan.count):
        for q in range(plan.devices):
            piece = parts[0][level]
            for turn in range(1, plan.devices):
                piece = jnp.where(source_of(me, turn, plan.devices) == q, parts[turn][level], piece)
            at = slice(q * plan.chunk, (q + 1) * plan.chunk)
            out[level, :, at] = piece + added[level, :, at]


def bucket_body(regions, values, region_column, region_row, cell_column, *outs):
    count, tiles, tile = values.shape
    capacity = outs[0].shape[1]
    band = lax.axis_index("lat")
    earlier = lax.broadcasted_iota(jnp.int32, (tiles, tiles), 0) < lax.broadcasted_iota(jnp.int32, (tiles, tiles), 1)
    same = (region_column[...] == region_row[...]) & earlier
    rank = jnp.sum(jnp.where(same, 1.0, 0.0), axis=0, keepdims=True).astype(jnp.int32)
    slot = lax.broadcasted_iota(jnp.int32, (capacity, tiles), 0)
    cells = jnp.broadcast_to(cell_column[...].astype(F32), (tiles, tile))
    picks = [
        jnp.where((slot == rank) & (region_row[...] == partner_of(band, s, regions)), 1.0, 0.0) for s in range(regions)
    ]
    picks = jnp.concatenate(picks, axis=0)
    for level in range(count + 1):
        got = lax.dot_general(
            picks,
            cells if level == count else values[level],
            (((1,), (0,)), ((), ())),
            precision=lax.Precision.HIGHEST,
            preferred_element_type=F32,
        )
        for s in range(regions):
            outs[s][level] = got[s * capacity : (s + 1) * capacity]


def bucket_tiles(tile_values, tile_region, tile_cell):
    regions = lax.axis_size("lat")
    count, tiles, tile = tile_values.shape
    return call(
        functools.partial(bucket_body, regions),
        [(count + 1, tiles // 4, tile)] * regions,
        tile_values,
        tile_region,
        tile_region.reshape(1, tiles),
        tile_cell.reshape(tiles, 1),
    )

def local(adjoint_in, courant, diffusion, tile_values, tile_region, tile_cell):
    field = adjoint_in[0]
    count, rows, width = field.shape
    devices = lax.axis_size("lev")
    bands = lax.axis_size("lat")
    plan = Plan(count, rows, width, devices)
    swaps_a, swaps_b = band_swaps(bands, 0), band_swaps(bands, 1)
    tile = (rows, LANES)

    early = plan.packed(plan.own_size)
    late = plan.packed(plan.sent_size) * (devices - 1)
    own, early_a, early_b, *sent = call(
        functools.partial(pack_body, plan),
        [(plan.own_size,) + tile] + [(early,) + tile] * 2 + [(plan.sent_size,) + tile] * (devices - 1),
        field,
        courant,
        diffusion,
        scratch=[field.shape, courant.shape, diffusion.shape],
        semaphores=3,
        inputs=pltpu.HBM,
    )
    got = [lax.ppermute(part, "lev", pairs) for part, pairs in zip(sent, rounds(devices))]
    early_a = lax.ppermute(early_a, "lat", swaps_a)
    early_b = lax.ppermute(early_b, "lat", swaps_b)
    late_a, late_b = call(functools.partial(forward_rows_body, plan), [(late,) + tile] * 2, *got)
    late_a = lax.ppermute(late_a, "lat", swaps_a)
    late_b = lax.ppermute(late_b, "lat", swaps_b)
    buckets = bucket_tiles(tile_values[0], tile_region, tile_cell)
    late_a, late_b, *buckets = lax.optimization_barrier((late_a, late_b, *buckets))
    buckets = [buckets[0]] + [lax.ppermute(part, "lat", pairs) for part, pairs in zip(buckets[1:], rounds(bands))]

    whole = (plan.levels, 3 * rows, plan.window)
    lists = (2, plan.own_size + (devices - 1) * plan.sent_size) + tile
    *outs, flux = call(
        functools.partial(steps_body, plan, bands),
        [(count, rows, plan.chunk)] * devices + [(rows, plan.chunk)],
        own,
        early_a,
        early_b,
        late_a,
        late_b,
        *got,
        scratch=[lists] + [whole] * 8,
    )
    parts = [outs[0]] + [lax.ppermute(part, "lev", pairs) for part, pairs in zip(outs[1:], rounds(devices))]
    (added,) = call(functools.partial(sum_body, plan), [(count, rows, width)], *buckets)
    (out,) = call(functools.partial(finish_body, plan), [(count, rows, width)], *parts, added)
    return out[None], flux[None]


def solution(mesh):
    return jax.shard_map(
        local,
        mesh=mesh,
        in_specs=(
            P(("groups", "tr"), "lev", "lat", None),
            P(None, "lev", "lat", None),
            P(None, "lat", "lev"),
            P(("groups", "tr"), "lev", "lat", None),
            P(("groups", "lat"), None),
            P(("groups", "lat")),
        ),
        out_specs=(P(("groups", "tr"), "lev", "lat", None), P(("groups", "tr"), "lat", "lev")),
        check_vma=False,
    )
```

```python
import functools

import jax
import jax.numpy as jnp
from jax import lax
from jax.experimental import pallas as pl
from jax.experimental.pallas import tpu as pltpu
from jax.sharding import PartitionSpec as P

STEPS = 6
HALO = STEPS
LANES = 128
F32 = jnp.float32


def call(body, out_shapes, *args, scratch=(), semaphores=0, inputs=pltpu.VMEM):
    spec = pl.BlockSpec(memory_space=pltpu.VMEM)
    if inputs == pltpu.HBM:
        args = [pltpu.with_memory_space_constraint(arg, pltpu.HBM) for arg in args]
    shapes = [pltpu.VMEM(shape, F32) for shape in scratch]
    if semaphores:
        shapes.append(pltpu.SemaphoreType.DMA((semaphores,)))
    return pl.pallas_call(
        body,
        out_shape=[jax.ShapeDtypeStruct(shape, F32) for shape in out_shapes],
        in_specs=[pl.BlockSpec(memory_space=inputs)] * len(args),
        out_specs=[spec] * len(out_shapes),
        scratch_shapes=shapes,
        compiler_params=pltpu.CompilerParams(vmem_limit_bytes=32 * 1024 * 1024),
    )(*args)


def partner_of(index, turn, count):
    if count & (count - 1) == 0:
        return index ^ turn
    return (index + turn) % count


def source_of(index, turn, count):
    if count & (count - 1) == 0:
        return index ^ turn
    return (index - turn) % count


def rounds(count):
    return [[(b, partner_of(b, turn, count)) for b in range(count)] for turn in range(1, count)]


def band_swaps(bands, first):
    pairs = [(b, b + 1) for b in range(first, bands - 1, 2)]
    return pairs + [(b, a) for a, b in pairs]


class Plan:
    def __init__(self, count, rows, width, devices):
        self.count, self.rows, self.width, self.devices = count, rows, width, devices
        self.levels = count * devices
        self.chunk = width // devices
        self.full = self.chunk // LANES
        self.rest = self.chunk % LANES
        self.window = (self.full + 1) * LANES
        assert self.rest + 2 * HALO <= LANES
        self.middle = (self.rest + LANES) // 2
        self.pitch = -(-(self.rest + 2 * HALO) // 16) * 16
        self.slots = LANES // self.pitch
        self.edge_slots = LANES // 16
        fields = 3 * count
        self.rests_at = fields * self.full
        self.diffusion_at = self.rests_at + -(-fields // self.slots)
        self.diffusion_tiles = -(-self.chunk // LANES)
        self.own_size = self.diffusion_at + (self.levels - 1) * self.diffusion_tiles
        self.sent_size = self.diffusion_at + -(-(self.levels - 1) // self.edge_slots)

    def packed(self, size):
        return size - size // 4 if 4 * HALO == 3 * self.rows else size


def lane_of(rows=8):
    return lax.broadcasted_iota(jnp.int32, (rows, LANES), 1)


def row_of(rows=8):
    return lax.broadcasted_iota(jnp.int32, (rows, LANES), 0)


def turn_lanes(tile, shift):
    return pltpu.roll(tile, shift % LANES, 1) if shift % LANES else tile


def turn_rows(tile, shift):
    rows = tile.shape[0]
    return pltpu.roll(tile, shift % rows, 0) if shift % rows else tile


def pack_lanes(tiles, slots, pitch):
    packed = []
    lane = lane_of(tiles[0].shape[0])
    for begin in range(0, len(tiles), slots):
        total = jnp.zeros_like(tiles[0])
        for slot, tile in enumerate(tiles[begin : begin + slots]):
            moved = turn_lanes(tile, HALO + slot * pitch)
            if slots > 1:
                moved = jnp.where((lane >= slot * pitch) & (lane < (slot + 1) * pitch), moved, total)
            total = moved
        packed.append(total)
    return packed


def unpack_lanes(tile, slot, pitch):
    return turn_lanes(tile, -HALO - slot * pitch)


def window_tiles(plan, ref, index, target):
    if plan.rest == 0:
        def at(column):
            return ref[index + (slice(None), pl.ds(pl.multiple_of(column, LANES), LANES))]

        full = [at(target * plan.chunk + t * LANES) for t in range(plan.full)]
        east = at(lax.rem(target + 1, plan.devices) * plan.chunk)
        west = at(lax.rem(target + plan.devices - 1, plan.devices) * plan.chunk + plan.chunk - LANES)
    else:
        line = pltpu.roll(ref[index], lax.rem(plan.width - target * plan.chunk, plan.width), 1)
        full = [line[:, t * LANES : (t + 1) * LANES] for t in range(plan.full)]
        east = line[:, plan.full * LANES : (plan.full + 1) * LANES]
        west = line[:, plan.width - LANES :]
    return full, jnp.where(lane_of(plan.rows) < plan.middle, east, west)


def field_tiles(plan, field, courant, target):
    tiles, rests = [], []
    for ref, lead in ((field, ()), (courant, (0,)), (courant, (1,))):
        for level in range(plan.count):
            full, rest = window_tiles(plan, ref, lead + (level,), target)
            tiles += full
            rests.append(rest)
    return tiles + pack_lanes(rests, plan.slots, plan.pitch)


def diffusion_tile(plan, diffusion, level, t):
    width = min(LANES, plan.chunk - t * LANES)
    tile = diffusion[level, :, t * LANES : t * LANES + width]
    if width < LANES:
        tile = jnp.concatenate([tile, jnp.zeros((plan.rows, LANES - width), F32)], axis=1)
    return tile


def pack_rows(plan, get, size, north, store):
    first = plan.rows - HALO if north else 0
    row = row_of(plan.rows)
    place = 0
    fours = size // 4 if plan.packed(size) < size else 0
    for four in range(fours):
        tiles = [get(4 * four + j) for j in range(4)]
        for j in range(3):
            extra = turn_rows(tiles[3], HALO - first - 2 * j)
            store(place, jnp.where(row < HALO, turn_rows(tiles[j], -first), extra))
            place += 1
    for index in range(4 * fours, size):
        store(place, turn_rows(get(index), -first))
        place += 1


def unpack_rows(plan, get, size, north, store):
    first = plan.rows - HALO if north else 0
    row = row_of(plan.rows)
    place = 0
    fours = size // 4 if plan.packed(size) < size else 0
    for four in range(fours):
        tiles = [get(place + j) for j in range(3)]
        place += 3
        last = jnp.zeros_like(tiles[0])
        for j in range(3):
            store(4 * four + j, turn_rows(tiles[j], first))
            moved = turn_rows(tiles[j], first + 2 * j - HALO)
            last = jnp.where((row >= first + 2 * j) & (row < first + 2 * j + 2), moved, last)
        store(4 * four + 3, last)
    for index in range(4 * fours, size):
        store(index, turn_rows(get(place), first))
        place += 1


def by_parity(body):
    even = lax.rem(lax.axis_index("lat"), 2) == 0

    @pl.when(even)
    def _():
        body(True)

    @pl.when(jnp.logical_not(even))
    def _():
        body(False)


def pack_body(plan, *refs):
    sources, (own, swap_a, swap_b), sent = refs[:3], refs[3:6], refs[6:-4]
    field, courant, diffusion, arrived = refs[-4:]
    copies = [
        pltpu.make_async_copy(source, target, arrived.at[i])
        for i, (source, target) in enumerate(zip(sources, (field, courant, diffusion)))
    ]
    for copy in copies:
        copy.start()
    for copy in copies:
        copy.wait()
    me = lax.axis_index("lev")
    tiles = field_tiles(plan, field, courant, me)
    for level in range(plan.levels - 1):
        tiles += [diffusion_tile(plan, diffusion, level, t) for t in range(plan.diffusion_tiles)]
    for index, tile in enumerate(tiles):
        own[index] = tile
    edges = []
    for level in range(plan.levels - 1):
        first = diffusion_tile(plan, diffusion, level, 0)
        last = turn_lanes(diffusion_tile(plan, diffusion, level, plan.diffusion_tiles - 1), -plan.rest)
        edges.append(jnp.where(lane_of(plan.rows) < LANES // 2, first, last))
    edges = pack_lanes(edges, plan.edge_slots, 16)
    for turn in range(1, plan.devices):
        target = partner_of(me, turn, plan.devices)
        for index, tile in enumerate(field_tiles(plan, field, courant, target) + edges):
            sent[turn - 1][index] = tile

    def rows(even):
        for north, swap in ((even, swap_a), (not even, swap_b)):
            pack_rows(plan, lambda i: own[i], plan.own_size, north, swap.__setitem__)

    by_parity(rows)


def forward_rows_body(plan, *refs):
    turns = plan.devices - 1
    got, swap_a, swap_b = refs[:turns], refs[turns], refs[turns + 1]
    size = plan.packed(plan.sent_size)

    def rows(even):
        for north, swap in ((even, swap_a), (not even, swap_b)):
            for turn in range(turns):
                def store(index, tile, base=turn * size, swap=swap):
                    swap[base + index] = tile

                pack_rows(plan, lambda i, turn=turn: got[turn][i], plan.sent_size, north, store)

    by_parity(rows)


def steps_body(plan, bands, *refs):
    turns = plan.devices - 1
    own, early_a, early_b, late_a, late_b = refs[:5]
    got = refs[5 : 5 + turns]
    outs = refs[5 + turns : 5 + turns + plan.devices]
    flux = refs[5 + turns + plan.devices]
    lists, lam, face_e, face_w, lat_e, lat_w, r, a, g = refs[6 + turns + plan.devices :]
    me, band = lax.axis_index("lev"), lax.axis_index("lat")
    rows, levels = plan.rows, plan.levels

    late_size = plan.packed(plan.sent_size)

    def unpack(even):
        for side, from_north in ((1, True), (2, False)):
            early, late = (early_a, late_a) if even == from_north else (early_b, late_b)

            def store(index, tile, base=0, side=side):
                lists[side - 1, base + index] = tile

            unpack_rows(plan, lambda i, e=early: e[i], plan.own_size, not from_north, store)
            for turn in range(turns):
                base = plan.own_size + turn * plan.sent_size
                unpack_rows(
                    plan,
                    lambda i, l=late, t=turn: l[t * late_size + i],
                    plan.sent_size,
                    not from_north,
                    functools.partial(store, base=base),
                )

    by_parity(unpack)

    def tile_of(side, turn, index):
        if side:
            return lists[side - 1, index if turn == 0 else plan.own_size + (turn - 1) * plan.sent_size + index]
        return own[index] if turn == 0 else got[turn - 1][index]

    lane = lane_of(rows)
    for side in range(3):
        at = pl.ds(side * rows, rows)
        for turn in range(plan.devices):
            base = source_of(me, turn, plan.devices) * plan.count if turn else me * plan.count
            for kind, target in enumerate((lam, face_w, lat_w)):
                for level in range(plan.count):
                    item = kind * plan.count + level
                    for t in range(plan.full):
                        target[base + level, at, t * LANES : (t + 1) * LANES] = tile_of(side, turn, item * plan.full + t)
                    rest = tile_of(side, turn, plan.rests_at + item // plan.slots)
                    target[base + level, at, plan.full * LANES :] = unpack_lanes(rest, item % plan.slots, plan.pitch)
        for level in range(levels - 1):
            for t in range(plan.full):
                g[level, at, t * LANES : (t + 1) * LANES] = tile_of(
                    side, 0, plan.diffusion_at + level * plan.diffusion_tiles + t
                )
            east = west = jnp.zeros((rows, LANES), F32)
            for turn in range(1, plan.devices):
                edge = tile_of(side, turn, plan.diffusion_at + level // plan.edge_slots)
                edge = unpack_lanes(edge, level % plan.edge_slots, 16)
                if turns == 1:
                    east = west = edge
                else:
                    source = source_of(me, turn, plan.devices)
                    east = jnp.where(source == lax.rem(me + 1, plan.devices), edge, east)
                    west = jnp.where(source == lax.rem(me + plan.devices - 1, plan.devices), edge, west)
            rest = jnp.where(lane < plan.middle, turn_lanes(east, plan.rest), west)
            if plan.rest:
                mine = tile_of(side, 0, plan.diffusion_at + level * plan.diffusion_tiles + plan.full)
                rest = jnp.where(lane < plan.rest, mine, rest)
            g[level, at, plan.full * LANES :] = rest

    row = lax.broadcasted_iota(jnp.int32, (3 * rows, plan.window), 0)
    closed = ((row == 0) & (band == 0)) | ((row == rows) & (band == bands - 1))
    zero = jnp.zeros((3 * rows, plan.window), F32)
    k_prev = gain = zero
    for level in range(levels):
        south = jnp.where(closed, 0.0, lat_w[level])
        lat_e[level] = jnp.maximum(pltpu.roll(south, 3 * rows - 1, 0), 0.0)
        lat_w[level] = jnp.minimum(south, 0.0)
        west = face_w[level]
        face_e[level] = jnp.maximum(pltpu.roll(west, plan.window - 1, 1), 0.0)
        face_w[level] = jnp.minimum(west, 0.0)
        k_next = g[level] if level < levels - 1 else zero
        inverse = 1.0 / (1.0 + k_prev + k_next - k_prev * gain)
        gain = k_next * inverse
        r[level], a[level], g[level] = inverse, k_prev * inverse, gain
        k_prev = k_next

    flux[...] = jnp.zeros_like(flux)

    def step(_, carry):
        y = zero
        for level in range(levels):
            y = lam[level] * r[level] + a[level] * y
            lam[level] = y
        w = zero
        for level in range(levels - 1, -1, -1):
            w = lam[level] + g[level] * w
            up, down = pltpu.roll(w, 3 * rows - 1, 0), pltpu.roll(w, 1, 0)
            v = w + lat_e[level] * (up - w) + lat_w[level] * (w - down)
            east, west = pltpu.roll(v, plan.window - 1, 1), pltpu.roll(v, 1, 1)
            lam[level] = v + face_e[level] * (east - v) + face_w[level] * (v - west)
        flux[...] += w[:rows, : plan.chunk]
        return carry

    lax.fori_loop(0, STEPS, step, 0)
    flux[...] = flux[...] / STEPS
    for turn in range(plan.devices):
        base = (partner_of(me, turn, plan.devices) if turn else me) * plan.count
        for level in range(plan.count):
            outs[turn][level] = lam[base + level, :rows, : plan.chunk]


def sum_body(plan, *refs):
    buckets, out = refs[:-1], refs[-1]
    count, rows, width = plan.count, plan.rows, plan.width
    cells = jnp.concatenate([bucket[count] for bucket in buckets], axis=0)
    tile = cells.shape[1]
    blocks = width // tile
    lane = lax.broadcasted_iota(jnp.int32, cells.shape, 1)
    place = (lane % rows * blocks + lane // rows).astype(F32)
    hits = jnp.where((cells == place) & (lane < rows * blocks), 1.0, 0.0)
    hits = hits.T[: rows * blocks]
    for level in range(count):
        values = jnp.concatenate([bucket[level] for bucket in buckets], axis=0)
        added = lax.dot_general(
            hits, values, (((1,), (0,)), ((), ())), precision=lax.Precision.HIGHEST, preferred_element_type=F32
        )
        for block in range(blocks):
            out[level, :, block * tile : (block + 1) * tile] = added[block * rows : (block + 1) * rows]


def finish_body(plan, *refs):
    parts, added, out = refs[: plan.devices], refs[plan.devices], refs[-1]
    me = lax.axis_index("lev")
    for level in range(plan.count):
        for q in range(plan.devices):
            piece = parts[0][level]
            for turn in range(1, plan.devices):
                piece = jnp.where(source_of(me, turn, plan.devices) == q, parts[turn][level], piece)
            at = slice(q * plan.chunk, (q + 1) * plan.chunk)
            out[level, :, at] = piece + added[level, :, at]


def bucket_body(regions, values, region_column, region_row, cell_column, *outs):
    count, tiles, tile = values.shape
    capacity = outs[0].shape[1]
    band = lax.axis_index("lat")
    earlier = lax.broadcasted_iota(jnp.int32, (tiles, tiles), 0) < lax.broadcasted_iota(jnp.int32, (tiles, tiles), 1)
    same = (region_column[...] == region_row[...]) & earlier
    rank = jnp.sum(jnp.where(same, 1.0, 0.0), axis=0, keepdims=True).astype(jnp.int32)
    slot = lax.broadcasted_iota(jnp.int32, (capacity, tiles), 0)
    cells = jnp.broadcast_to(cell_column[...].astype(F32), (tiles, tile))
    picks = [
        jnp.where((slot == rank) & (region_row[...] == partner_of(band, s, regions)), 1.0, 0.0) for s in range(regions)
    ]
    picks = jnp.concatenate(picks, axis=0)
    for level in range(count + 1):
        got = lax.dot_general(
            picks,
            cells if level == count else values[level],
            (((1,), (0,)), ((), ())),
            precision=lax.Precision.HIGHEST,
            preferred_element_type=F32,
        )
        for s in range(regions):
            outs[s][level] = got[s * capacity : (s + 1) * capacity]


def bucket_tiles(tile_values, tile_region, tile_cell):
    regions = lax.axis_size("lat")
    count, tiles, tile = tile_values.shape
    return call(
        functools.partial(bucket_body, regions),
        [(count + 1, tiles // 4, tile)] * regions,
        tile_values,
        tile_region,
        tile_region.reshape(1, tiles),
        tile_cell.reshape(tiles, 1),
    )

def local(adjoint_in, courant, diffusion, tile_values, tile_region, tile_cell):
    field = adjoint_in[0]
    count, rows, width = field.shape
    devices = lax.axis_size("lev")
    bands = lax.axis_size("lat")
    plan = Plan(count, rows, width, devices)
    swaps_a, swaps_b = band_swaps(bands, 0), band_swaps(bands, 1)
    tile = (rows, LANES)

    early = plan.packed(plan.own_size)
    late = plan.packed(plan.sent_size) * (devices - 1)
    own, early_a, early_b, *sent = call(
        functools.partial(pack_body, plan),
        [(plan.own_size,) + tile] + [(early,) + tile] * 2 + [(plan.sent_size,) + tile] * (devices - 1),
        field,
        courant,
        diffusion,
        scratch=[field.shape, courant.shape, diffusion.shape],
        semaphores=3,
        inputs=pltpu.HBM,
    )
    got = [lax.ppermute(part, "lev", pairs) for part, pairs in zip(sent, rounds(devices))]
    early_b = lax.ppermute(early_b, "lat", swaps_b)
    early_a = lax.ppermute(early_a, "lat", swaps_a)
    late_a, late_b = call(functools.partial(forward_rows_body, plan), [(late,) + tile] * 2, *got)
    late_b = lax.ppermute(late_b, "lat", swaps_b)
    late_a = lax.ppermute(late_a, "lat", swaps_a)
    buckets = bucket_tiles(tile_values[0], tile_region, tile_cell)
    late_a, late_b, *buckets = lax.optimization_barrier((late_a, late_b, *buckets))
    buckets = [buckets[0]] + [lax.ppermute(part, "lat", pairs) for part, pairs in zip(buckets[1:], rounds(bands))]

    whole = (plan.levels, 3 * rows, plan.window)
    lists = (2, plan.own_size + (devices - 1) * plan.sent_size) + tile
    *outs, flux = call(
        functools.partial(steps_body, plan, bands),
        [(count, rows, plan.chunk)] * devices + [(rows, plan.chunk)],
        own,
        early_a,
        early_b,
        late_a,
        late_b,
        *got,
        scratch=[lists] + [whole] * 8,
    )
    parts = [outs[0]] + [lax.ppermute(part, "lev", pairs) for part, pairs in zip(outs[1:], rounds(devices))]
    (added,) = call(functools.partial(sum_body, plan), [(count, rows, width)], *buckets)
    (out,) = call(functools.partial(finish_body, plan), [(count, rows, width)], *parts, added)
    return out[None], flux[None]


def solution(mesh):
    return jax.shard_map(
        local,
        mesh=mesh,
        in_specs=(
            P(("groups", "tr"), "lev", "lat", None),
            P(None, "lev", "lat", None),
            P(None, "lat", "lev"),
            P(("groups", "tr"), "lev", "lat", None),
            P(("groups", "lat"), None),
            P(("groups", "lat")),
        ),
        out_specs=(P(("groups", "tr"), "lev", "lat", None), P(("groups", "tr"), "lat", "lev")),
        check_vma=False,
    )
```

```python
import functools

import jax
import jax.numpy as jnp
from jax import lax
from jax.experimental import pallas as pl
from jax.experimental.pallas import tpu as pltpu
from jax.sharding import PartitionSpec as P

STEPS = 6
HALO = STEPS
LANES = 128
F32 = jnp.float32


def call(body, out_shapes, *args, scratch=(), semaphores=0, inputs=pltpu.VMEM):
    spec = pl.BlockSpec(memory_space=pltpu.VMEM)
    if inputs == pltpu.HBM:
        args = [pltpu.with_memory_space_constraint(arg, pltpu.HBM) for arg in args]
    shapes = [pltpu.VMEM(shape, F32) for shape in scratch]
    if semaphores:
        shapes.append(pltpu.SemaphoreType.DMA((semaphores,)))
    return pl.pallas_call(
        body,
        out_shape=[jax.ShapeDtypeStruct(shape, F32) for shape in out_shapes],
        in_specs=[pl.BlockSpec(memory_space=inputs)] * len(args),
        out_specs=[spec] * len(out_shapes),
        scratch_shapes=shapes,
        compiler_params=pltpu.CompilerParams(vmem_limit_bytes=16 * 1024 * 1024),
    )(*args)


def partner_of(index, turn, count):
    if count & (count - 1) == 0:
        return index ^ turn
    return (index + turn) % count


def source_of(index, turn, count):
    if count & (count - 1) == 0:
        return index ^ turn
    return (index - turn) % count


def rounds(count):
    return [[(b, partner_of(b, turn, count)) for b in range(count)] for turn in range(1, count)]


def band_swaps(bands, tracers, first):
    swaps = []
    for b in range(bands):
        partner = b + 1 if (b - first) % 2 == 0 else b - 1
        for t in range(tracers):
            if 0 <= partner < bands:
                swaps.append((b * tracers + t, partner * tracers + t))
            else:
                swaps.append((b * tracers + t, b * tracers + (t ^ 1 if tracers % 2 == 0 else t)))
    return swaps


class Plan:
    def __init__(self, count, rows, width, devices):
        self.count, self.rows, self.width, self.devices = count, rows, width, devices
        self.levels = count * devices
        self.chunk = width // devices
        self.full = self.chunk // LANES
        self.rest = self.chunk % LANES
        self.window = (self.full + 1) * LANES
        assert self.rest + 2 * HALO <= LANES
        self.middle = (self.rest + LANES) // 2
        self.pitch = -(-(self.rest + 2 * HALO) // 16) * 16
        self.slots = LANES // self.pitch
        self.edge_slots = LANES // 16
        fields = 3 * count
        self.rests_at = fields * self.full
        self.diffusion_at = self.rests_at + -(-fields // self.slots)
        self.diffusion_tiles = -(-self.chunk // LANES)
        self.own_size = self.diffusion_at + (self.levels - 1) * self.diffusion_tiles
        self.sent_size = self.diffusion_at + -(-(self.levels - 1) // self.edge_slots)

    def packed(self, size):
        return size - size // 4 if 4 * HALO == 3 * self.rows else size


def lane_of(rows=8):
    return lax.broadcasted_iota(jnp.int32, (rows, LANES), 1)


def row_of(rows=8):
    return lax.broadcasted_iota(jnp.int32, (rows, LANES), 0)


def turn_lanes(tile, shift):
    return pltpu.roll(tile, shift % LANES, 1) if shift % LANES else tile


def turn_rows(tile, shift):
    rows = tile.shape[0]
    return pltpu.roll(tile, shift % rows, 0) if shift % rows else tile


def pack_lanes(tiles, slots, pitch):
    packed = []
    lane = lane_of(tiles[0].shape[0])
    for begin in range(0, len(tiles), slots):
        total = jnp.zeros_like(tiles[0])
        for slot, tile in enumerate(tiles[begin : begin + slots]):
            moved = turn_lanes(tile, HALO + slot * pitch)
            if slots > 1:
                moved = jnp.where((lane >= slot * pitch) & (lane < (slot + 1) * pitch), moved, total)
            total = moved
        packed.append(total)
    return packed


def unpack_lanes(tile, slot, pitch):
    return turn_lanes(tile, -HALO - slot * pitch)


def window_tiles(plan, ref, index, target):
    if plan.rest == 0:
        def at(column):
            return ref[index + (slice(None), pl.ds(pl.multiple_of(column, LANES), LANES))]

        full = [at(target * plan.chunk + t * LANES) for t in range(plan.full)]
        east = at(lax.rem(target + 1, plan.devices) * plan.chunk)
        west = at(lax.rem(target + plan.devices - 1, plan.devices) * plan.chunk + plan.chunk - LANES)
    else:
        line = pltpu.roll(ref[index], lax.rem(plan.width - target * plan.chunk, plan.width), 1)
        full = [line[:, t * LANES : (t + 1) * LANES] for t in range(plan.full)]
        east = line[:, plan.full * LANES : (plan.full + 1) * LANES]
        west = line[:, plan.width - LANES :]
    return full, jnp.where(lane_of(plan.rows) < plan.middle, east, west)


def field_tiles(plan, field, courant, target):
    tiles, rests = [], []
    for ref, lead in ((field, ()), (courant, (0,)), (courant, (1,))):
        for level in range(plan.count):
            full, rest = window_tiles(plan, ref, lead + (level,), target)
            tiles += full
            rests.append(rest)
    return tiles + pack_lanes(rests, plan.slots, plan.pitch)


def diffusion_tile(plan, diffusion, level, t):
    width = min(LANES, plan.chunk - t * LANES)
    tile = diffusion[level, :, t * LANES : t * LANES + width]
    if width < LANES:
        tile = jnp.concatenate([tile, jnp.zeros((plan.rows, LANES - width), F32)], axis=1)
    return tile


def pack_rows(plan, get, size, north, store):
    first = plan.rows - HALO if north else 0
    gap = 0 if north else HALO
    row = row_of(plan.rows)
    kept = (row >= first) & (row < first + HALO)
    fours = size // 4 if plan.packed(size) < size else 0
    for four in range(fours):
        last = get(4 * four + 3)
        for j in range(3):
            store(3 * four + j, jnp.where(kept, get(4 * four + j), turn_rows(last, gap - first - 2 * j)))
    for index in range(4 * fours, size):
        store(index - fours, get(index))


def unpack_rows(plan, get, size, north, store):
    first = plan.rows - HALO if north else 0
    gap = 0 if north else HALO
    row = row_of(plan.rows)
    fours = size // 4 if plan.packed(size) < size else 0
    for four in range(fours):
        last = None
        for j in range(3):
            tile = get(3 * four + j)
            store(4 * four + j, tile)
            moved = turn_rows(tile, first + 2 * j - gap)
            last = moved if last is None else jnp.where(row >= first + 2 * j, moved, last)
        store(4 * four + 3, last)
    for index in range(4 * fours, size):
        store(index, get(index - fours))


def by_parity(body):
    even = lax.rem(lax.axis_index("lat"), 2) == 0

    @pl.when(even)
    def _():
        body(True)

    @pl.when(jnp.logical_not(even))
    def _():
        body(False)


def pack_body(plan, *refs):
    sources, (own, swap_a, swap_b), sent = refs[:3], refs[3:6], refs[6:-4]
    field, courant, diffusion, arrived = refs[-4:]
    copies = [
        pltpu.make_async_copy(source, target, arrived.at[i])
        for i, (source, target) in enumerate(zip(sources, (field, courant, diffusion)))
    ]
    for copy in copies:
        copy.start()
    for copy in copies:
        copy.wait()
    me = lax.axis_index("lev")
    tiles = field_tiles(plan, field, courant, me)
    for level in range(plan.levels - 1):
        tiles += [diffusion_tile(plan, diffusion, level, t) for t in range(plan.diffusion_tiles)]
    for index, tile in enumerate(tiles):
        own[index] = tile
    edges = []
    for level in range(plan.levels - 1):
        first = diffusion_tile(plan, diffusion, level, 0)
        last = turn_lanes(diffusion_tile(plan, diffusion, level, plan.diffusion_tiles - 1), -plan.rest)
        edges.append(jnp.where(lane_of(plan.rows) < LANES // 2, first, last))
    edges = pack_lanes(edges, plan.edge_slots, 16)
    for turn in range(1, plan.devices):
        target = partner_of(me, turn, plan.devices)
        for index, tile in enumerate(field_tiles(plan, field, courant, target) + edges):
            sent[turn - 1][index] = tile

    def rows(even):
        for north, swap in ((even, swap_a), (not even, swap_b)):
            pack_rows(plan, lambda i: own[i], plan.own_size, north, swap.__setitem__)

    by_parity(rows)


def forward_rows_body(plan, *refs):
    turns = plan.devices - 1
    got, swap_a, swap_b = refs[:turns], refs[turns], refs[turns + 1]
    size = plan.packed(plan.sent_size)

    def rows(even):
        for north, swap in ((even, swap_a), (not even, swap_b)):
            for turn in range(turns):
                def store(index, tile, base=turn * size, swap=swap):
                    swap[base + index] = tile

                pack_rows(plan, lambda i, turn=turn: got[turn][i], plan.sent_size, north, store)

    by_parity(rows)


def place_fields(plan, base, get, targets):
    for kind, (target, at) in enumerate(targets):
        for level in range(plan.count):
            item = kind * plan.count + level
            for t in range(plan.full):
                target[base + level, at, t * LANES : (t + 1) * LANES] = get(item * plan.full + t)
            rest = get(plan.rests_at + item // plan.slots)
            target[base + level, at, plan.full * LANES :] = unpack_lanes(rest, item % plan.slots, plan.pitch)


def place_diffusion(plan, at, get, target):
    for level in range(plan.levels - 1):
        for t in range(plan.full):
            target[level, at, t * LANES : (t + 1) * LANES] = get(plan.diffusion_at + level * plan.diffusion_tiles + t)


def place_diffusion_rest(plan, me, at, mine, get, target):
    lane = lane_of(plan.rows)
    for level in range(plan.levels - 1):
        east = west = None
        for turn in range(1, plan.devices):
            edge = get(turn, plan.diffusion_at + level // plan.edge_slots)
            edge = unpack_lanes(edge, level % plan.edge_slots, 16)
            source = source_of(me, turn, plan.devices)
            if east is None:
                east = west = edge
            else:
                east = jnp.where(source == lax.rem(me + 1, plan.devices), edge, east)
                west = jnp.where(source == lax.rem(me + plan.devices - 1, plan.devices), edge, west)
        rest = jnp.where(lane < plan.middle, turn_lanes(east, plan.rest), west)
        target[level, at] = jnp.where(lane < plan.rest, mine(level), rest) if plan.rest else rest


def column_factors(plan, r, a, g):
    k_prev = gain = zero = jnp.zeros(g.shape[1:], F32)
    for level in range(plan.levels):
        k_next = g[level] if level < plan.levels - 1 else zero
        inverse = 1.0 / (1.0 + k_prev + k_next - k_prev * gain)
        gain = k_next * inverse
        r[level], a[level], g[level] = inverse, k_prev * inverse, gain
        k_prev = k_next


def split_zonal(plan, level, face_e, face_w):
    west = face_w[level]
    face_e[level] = jnp.maximum(pltpu.roll(west, plan.window - 1, 1), 0.0)
    face_w[level] = jnp.minimum(west, 0.0)


def sides(plan, even, swap_a, swap_b, begin):
    return (
        (True, slice(begin, begin + plan.rows), swap_a if even else swap_b),
        (False, slice(begin + plan.rows, begin + 2 * plan.rows), swap_b if even else swap_a),
    )


def early_shapes(plan):
    rows, window, full = plan.rows, plan.window, plan.full * LANES
    shapes = [(plan.levels, rows, window)] * 4 + [(plan.count, 2 * rows, window)] * 4
    shapes += [(plan.levels, rows, LANES)] * 3
    shapes += [(plan.levels, 3 * rows, full)] * 3 if full else []
    return shapes + ([(plan.levels, 2 * rows, LANES)] if plan.rest else [])


def early_body(plan, *refs):
    turns = plan.devices - 1
    own, swap_a, swap_b = refs[:3]
    lists = [own, *refs[3 : 3 + turns]]
    outs, unpacked = refs[3 + turns : -1], refs[-1]
    lam, face_e, face_w, lat = outs[:4]
    halo_lam, halo_e, halo_w, halo_lat = outs[4:8]
    rest_factors, full_factors = outs[8:11], outs[11:14]
    me = lax.axis_index("lev")
    rows = plan.rows
    at = slice(0, rows)
    for turn in range(plan.devices):
        base = (source_of(me, turn, plan.devices) if turn else me) * plan.count
        place_fields(plan, base, lists[turn].__getitem__, ((lam, at), (face_w, at), (lat, at)))
    if plan.full:
        place_diffusion(plan, at, own.__getitem__, full_factors[2])

    def mine(level):
        return own[plan.diffusion_at + level * plan.diffusion_tiles + plan.full]

    place_diffusion_rest(plan, me, at, mine, lambda turn, index: lists[turn][index], rest_factors[2])

    def halos(even):
        for north, at, swap in sides(plan, even, swap_a, swap_b, 0):
            unpack_rows(plan, swap.__getitem__, plan.own_size, not north, unpacked.__setitem__)
            place_fields(plan, 0, unpacked.__getitem__, ((halo_lam, at), (halo_w, at), (halo_lat, at)))
            if plan.full:
                below = slice(at.start + rows, at.stop + rows)
                place_diffusion(plan, below, unpacked.__getitem__, full_factors[2])
            if plan.rest:
                for level in range(plan.levels - 1):
                    outs[-1][level, at] = unpacked[plan.diffusion_at + level * plan.diffusion_tiles + plan.full]

    by_parity(halos)
    for level in range(plan.levels):
        split_zonal(plan, level, face_e, face_w)
    for level in range(plan.count):
        split_zonal(plan, level, halo_e, halo_w)
    column_factors(plan, *rest_factors)
    if plan.full:
        column_factors(plan, *full_factors)


def steps_body(plan, bands, *refs):
    turns = plan.devices - 1
    state = len(early_shapes(plan))
    own_lam, own_e, own_w, own_lat, early_lam, early_e, early_w, early_lat = refs[:8]
    own_factors, full_factors, left = refs[8:11], refs[11:14], refs[state - 1]
    swap_a, swap_b = refs[state : state + 2]
    outs = refs[state + 2 : state + 2 + plan.devices]
    flux, lam, halo_e, halo_w, lat_e, lat_w, *rest_factors, unpacked = refs[state + 2 + plan.devices :]
    me, band = lax.axis_index("lev"), lax.axis_index("lat")
    rows, levels = plan.rows, plan.levels
    packed = plan.packed(plan.sent_size)

    for level in range(levels):
        lam[level, :rows] = own_lam[level]
        lat_w[level, :rows] = own_lat[level]
    for level in range(plan.count):
        at = me * plan.count + level
        lam[at, rows:] = early_lam[level]
        lat_w[at, rows:] = early_lat[level]
        halo_e[at], halo_w[at] = early_e[level], early_w[level]

    def halos(even):
        for north, at, swap in sides(plan, even, swap_a, swap_b, rows):
            above = slice(at.start - rows, at.stop - rows)
            for turn in range(turns):
                def get(index, base=turn * packed, swap=swap):
                    return swap[base + index]

                def store(index, tile, base=turn * plan.sent_size):
                    unpacked[base + index] = tile

                unpack_rows(plan, get, plan.sent_size, not north, store)

            def tile_of(turn, index):
                return unpacked[(turn - 1) * plan.sent_size + index]

            for turn in range(1, plan.devices):
                base = source_of(me, turn, plan.devices) * plan.count
                get = functools.partial(tile_of, turn)
                place_fields(plan, base, get, ((lam, at), (halo_w, above), (lat_w, at)))
            place_diffusion_rest(plan, me, above, lambda level, above=above: left[level, above], tile_of, rest_factors[2])

    by_parity(halos)
    for turn in range(1, plan.devices):
        base = source_of(me, turn, plan.devices) * plan.count
        for level in range(plan.count):
            split_zonal(plan, base + level, halo_e, halo_w)
    row = lax.broadcasted_iota(jnp.int32, (3 * rows, plan.window), 0)
    closed = ((row == 0) & (band == 0)) | ((row == rows) & (band == bands - 1))
    for level in range(levels):
        south = jnp.where(closed, 0.0, lat_w[level])
        lat_e[level] = jnp.maximum(pltpu.roll(south, 3 * rows - 1, 0), 0.0)
        lat_w[level] = jnp.minimum(south, 0.0)
    column_factors(plan, *rest_factors)

    flux[...] = jnp.zeros_like(flux)
    zero = jnp.zeros((3 * rows, plan.window), F32)

    def factor(kind, level):
        rest = jnp.concatenate([own_factors[kind][level], rest_factors[kind][level]], axis=0)
        return jnp.concatenate([full_factors[kind][level], rest], axis=1) if plan.full else rest

    def step(_, carry):
        y = zero
        for level in range(levels):
            y = lam[level] * factor(0, level) + factor(1, level) * y
            lam[level] = y
        w = zero
        for level in range(levels - 1, -1, -1):
            w = lam[level] + factor(2, level) * w
            up, down = pltpu.roll(w, 3 * rows - 1, 0), pltpu.roll(w, 1, 0)
            v = w + lat_e[level] * (up - w) + lat_w[level] * (w - down)
            east, west = pltpu.roll(v, plan.window - 1, 1), pltpu.roll(v, 1, 1)
            face_e = jnp.concatenate([own_e[level], halo_e[level]], axis=0)
            face_w = jnp.concatenate([own_w[level], halo_w[level]], axis=0)
            lam[level] = v + face_e * (east - v) + face_w * (v - west)
        flux[...] += w[:rows, : plan.chunk]
        return carry

    lax.fori_loop(0, STEPS, step, 0)
    flux[...] = flux[...] / STEPS
    for turn in range(plan.devices):
        base = (partner_of(me, turn, plan.devices) if turn else me) * plan.count
        for level in range(plan.count):
            outs[turn][level] = lam[base + level, :rows, : plan.chunk]


def sum_body(plan, *refs):
    buckets, out = refs[:-1], refs[-1]
    count, rows, width = plan.count, plan.rows, plan.width
    cells = jnp.concatenate([bucket[count] for bucket in buckets], axis=0)
    tile = cells.shape[1]
    blocks = width // tile
    lane = lax.broadcasted_iota(jnp.int32, cells.shape, 1)
    place = (lane % rows * blocks + lane // rows).astype(F32)
    hits = jnp.where((cells == place) & (lane < rows * blocks), 1.0, 0.0)
    hits = hits.T[: rows * blocks]
    for level in range(count):
        values = jnp.concatenate([bucket[level] for bucket in buckets], axis=0)
        added = lax.dot_general(
            hits, values, (((1,), (0,)), ((), ())), precision=lax.Precision.HIGHEST, preferred_element_type=F32
        )
        for block in range(blocks):
            out[level, :, block * tile : (block + 1) * tile] = added[block * rows : (block + 1) * rows]


def finish_body(plan, *refs):
    parts, added, out = refs[: plan.devices], refs[plan.devices], refs[-1]
    me = lax.axis_index("lev")
    for level in range(plan.count):
        for q in range(plan.devices):
            piece = parts[0][level]
            for turn in range(1, plan.devices):
                piece = jnp.where(source_of(me, turn, plan.devices) == q, parts[turn][level], piece)
            at = slice(q * plan.chunk, (q + 1) * plan.chunk)
            out[level, :, at] = piece + added[level, :, at]


def bucket_body(regions, values, region_column, region_row, cell_column, *outs):
    count, tiles, tile = values.shape
    capacity = outs[0].shape[1]
    band = lax.axis_index("lat")
    earlier = lax.broadcasted_iota(jnp.int32, (tiles, tiles), 0) < lax.broadcasted_iota(jnp.int32, (tiles, tiles), 1)
    same = (region_column[...] == region_row[...]) & earlier
    rank = jnp.sum(jnp.where(same, 1.0, 0.0), axis=0, keepdims=True).astype(jnp.int32)
    slot = lax.broadcasted_iota(jnp.int32, (capacity, tiles), 0)
    cells = jnp.broadcast_to(cell_column[...].astype(F32), (tiles, tile))
    picks = [
        jnp.where((slot == rank) & (region_row[...] == partner_of(band, s, regions)), 1.0, 0.0) for s in range(regions)
    ]
    picks = jnp.concatenate(picks, axis=0)
    for level in range(count + 1):
        got = lax.dot_general(
            picks,
            cells if level == count else values[level],
            (((1,), (0,)), ((), ())),
            precision=lax.Precision.HIGHEST,
            preferred_element_type=F32,
        )
        for s in range(regions):
            outs[s][level] = got[s * capacity : (s + 1) * capacity]


def bucket_tiles(tile_values, tile_region, tile_cell):
    regions = lax.axis_size("lat")
    count, tiles, tile = tile_values.shape
    return call(
        functools.partial(bucket_body, regions),
        [(count + 1, tiles // 4, tile)] * regions,
        tile_values,
        tile_region,
        tile_region.reshape(1, tiles),
        tile_cell.reshape(tiles, 1),
    )

def local(adjoint_in, courant, diffusion, tile_values, tile_region, tile_cell):
    field = adjoint_in[0]
    count, rows, width = field.shape
    devices = lax.axis_size("lev")
    bands = lax.axis_size("lat")
    plan = Plan(count, rows, width, devices)
    tracers = lax.axis_size("tr")
    swaps_a, swaps_b = band_swaps(bands, tracers, 0), band_swaps(bands, tracers, 1)
    tile = (rows, LANES)

    early = plan.packed(plan.own_size)
    late = plan.packed(plan.sent_size) * (devices - 1)
    own, early_a, early_b, *sent = call(
        functools.partial(pack_body, plan),
        [(plan.own_size,) + tile] + [(early,) + tile] * 2 + [(plan.sent_size,) + tile] * (devices - 1),
        field,
        courant,
        diffusion,
        scratch=[field.shape, courant.shape, diffusion.shape],
        semaphores=3,
        inputs=pltpu.HBM,
    )
    got = [lax.ppermute(part, "lev", pairs) for part, pairs in zip(sent, rounds(devices))]
    early_b = lax.ppermute(early_b, ("lat", "tr"), swaps_b)
    early_a = lax.ppermute(early_a, ("lat", "tr"), swaps_a)
    late_a, late_b = call(functools.partial(forward_rows_body, plan), [(late,) + tile] * 2, *got)
    late_b = lax.ppermute(late_b, ("lat", "tr"), swaps_b)
    late_a = lax.ppermute(late_a, ("lat", "tr"), swaps_a)
    state = call(
        functools.partial(early_body, plan),
        early_shapes(plan),
        own,
        early_a,
        early_b,
        *got,
        scratch=[(plan.own_size,) + tile],
    )
    buckets = bucket_tiles(tile_values[0], tile_region, tile_cell)
    late_a, late_b, state, buckets = lax.optimization_barrier((late_a, late_b, state, buckets))
    buckets = [buckets[0]] + [lax.ppermute(part, "lat", pairs) for part, pairs in zip(buckets[1:], rounds(bands))]

    whole, halo = (plan.levels, 3 * rows, plan.window), (plan.levels, 2 * rows, plan.window)
    *outs, flux = call(
        functools.partial(steps_body, plan, bands),
        [(count, rows, plan.chunk)] * devices + [(rows, plan.chunk)],
        *state,
        late_a,
        late_b,
        scratch=[whole, halo, halo, whole, whole]
        + [(plan.levels, 2 * rows, LANES)] * 3
        + [((devices - 1) * plan.sent_size,) + tile],
    )
    parts = [outs[0]] + [lax.ppermute(part, "lev", pairs) for part, pairs in zip(outs[1:], rounds(devices))]
    (added,) = call(functools.partial(sum_body, plan), [(count, rows, width)], *buckets)
    (out,) = call(functools.partial(finish_body, plan), [(count, rows, width)], *parts, added)
    return out[None], flux[None]


def solution(mesh):
    return jax.shard_map(
        local,
        mesh=mesh,
        in_specs=(
            P(("groups", "tr"), "lev", "lat", None),
            P(None, "lev", "lat", None),
            P(None, "lat", "lev"),
            P(("groups", "tr"), "lev", "lat", None),
            P(("groups", "lat"), None),
            P(("groups", "lat")),
        ),
        out_specs=(P(("groups", "tr"), "lev", "lat", None), P(("groups", "tr"), "lat", "lev")),
        check_vma=False,
    )
```

```python
import functools

import jax
import jax.numpy as jnp
from jax import lax
from jax.experimental import pallas as pl
from jax.experimental.pallas import tpu as pltpu
from jax.sharding import PartitionSpec as P

STEPS = 6
HALO = STEPS
LANES = 128
F32 = jnp.float32


def call(body, out_shapes, *args, scratch=(), semaphores=0, inputs=pltpu.VMEM):
    spec = pl.BlockSpec(memory_space=pltpu.VMEM)
    if inputs == pltpu.HBM:
        args = [pltpu.with_memory_space_constraint(arg, pltpu.HBM) for arg in args]
    shapes = [pltpu.VMEM(shape, F32) for shape in scratch]
    if semaphores:
        shapes.append(pltpu.SemaphoreType.DMA((semaphores,)))
    return pl.pallas_call(
        body,
        out_shape=[jax.ShapeDtypeStruct(shape, F32) for shape in out_shapes],
        in_specs=[pl.BlockSpec(memory_space=inputs)] * len(args),
        out_specs=[spec] * len(out_shapes),
        scratch_shapes=shapes,
        compiler_params=pltpu.CompilerParams(vmem_limit_bytes=16 * 1024 * 1024),
    )(*args)


def partner_of(index, turn, count):
    if count & (count - 1) == 0:
        return index ^ turn
    return (index + turn) % count


def source_of(index, turn, count):
    if count & (count - 1) == 0:
        return index ^ turn
    return (index - turn) % count


def rounds(count):
    return [[(b, partner_of(b, turn, count)) for b in range(count)] for turn in range(1, count)]


def band_swaps(bands, tracers, first):
    swaps = []
    for b in range(bands):
        partner = b + 1 if (b - first) % 2 == 0 else b - 1
        for t in range(tracers):
            if 0 <= partner < bands:
                swaps.append((b * tracers + t, partner * tracers + t))
            else:
                swaps.append((b * tracers + t, b * tracers + (t ^ 1 if tracers % 2 == 0 else t)))
    return swaps


class Plan:
    def __init__(self, count, rows, width, devices):
        self.count, self.rows, self.width, self.devices = count, rows, width, devices
        self.levels = count * devices
        self.chunk = width // devices
        self.full = self.chunk // LANES
        self.rest = self.chunk % LANES
        self.window = (self.full + 1) * LANES
        assert self.rest + 2 * HALO <= LANES
        self.middle = (self.rest + LANES) // 2
        self.pitch = -(-(self.rest + 2 * HALO) // 16) * 16
        self.slots = LANES // self.pitch
        self.edge_slots = LANES // 16
        fields = 3 * count
        self.rests_at = fields * self.full
        self.diffusion_at = self.rests_at + -(-fields // self.slots)
        self.diffusion_tiles = -(-self.chunk // LANES)
        self.own_size = self.diffusion_at + (self.levels - 1) * self.diffusion_tiles
        self.sent_size = self.diffusion_at + -(-(self.levels - 1) // self.edge_slots)

    def packed(self, size):
        return size - size // 4 if 4 * HALO == 3 * self.rows else size


def lane_of(rows=8):
    return lax.broadcasted_iota(jnp.int32, (rows, LANES), 1)


def row_of(rows=8):
    return lax.broadcasted_iota(jnp.int32, (rows, LANES), 0)


def turn_lanes(tile, shift):
    return pltpu.roll(tile, shift % LANES, 1) if shift % LANES else tile


def turn_rows(tile, shift):
    rows = tile.shape[0]
    return pltpu.roll(tile, shift % rows, 0) if shift % rows else tile


def pack_lanes(tiles, slots, pitch):
    packed = []
    lane = lane_of(tiles[0].shape[0])
    for begin in range(0, len(tiles), slots):
        total = jnp.zeros_like(tiles[0])
        for slot, tile in enumerate(tiles[begin : begin + slots]):
            moved = turn_lanes(tile, HALO + slot * pitch)
            if slots > 1:
                moved = jnp.where((lane >= slot * pitch) & (lane < (slot + 1) * pitch), moved, total)
            total = moved
        packed.append(total)
    return packed


def unpack_lanes(tile, slot, pitch):
    return turn_lanes(tile, -HALO - slot * pitch)


def window_tiles(plan, ref, index, target):
    if plan.rest == 0:
        def at(column):
            return ref[index + (slice(None), pl.ds(pl.multiple_of(column, LANES), LANES))]

        full = [at(target * plan.chunk + t * LANES) for t in range(plan.full)]
        east = at(lax.rem(target + 1, plan.devices) * plan.chunk)
        west = at(lax.rem(target + plan.devices - 1, plan.devices) * plan.chunk + plan.chunk - LANES)
    else:
        line = pltpu.roll(ref[index], lax.rem(plan.width - target * plan.chunk, plan.width), 1)
        full = [line[:, t * LANES : (t + 1) * LANES] for t in range(plan.full)]
        east = line[:, plan.full * LANES : (plan.full + 1) * LANES]
        west = line[:, plan.width - LANES :]
    return full, jnp.where(lane_of(plan.rows) < plan.middle, east, west)


def field_tiles(plan, field, courant, target):
    tiles, rests = [], []
    for ref, lead in ((field, ()), (courant, (0,)), (courant, (1,))):
        for level in range(plan.count):
            full, rest = window_tiles(plan, ref, lead + (level,), target)
            tiles += full
            rests.append(rest)
    return tiles + pack_lanes(rests, plan.slots, plan.pitch)


def diffusion_tile(plan, diffusion, level, t):
    width = min(LANES, plan.chunk - t * LANES)
    tile = diffusion[level, :, t * LANES : t * LANES + width]
    if width < LANES:
        tile = jnp.concatenate([tile, jnp.zeros((plan.rows, LANES - width), F32)], axis=1)
    return tile


def pack_rows(plan, get, size, north, store):
    first = plan.rows - HALO if north else 0
    gap = 0 if north else HALO
    row = row_of(plan.rows)
    kept = (row >= first) & (row < first + HALO)
    fours = size // 4 if plan.packed(size) < size else 0
    for four in range(fours):
        last = get(4 * four + 3)
        for j in range(3):
            store(3 * four + j, jnp.where(kept, get(4 * four + j), turn_rows(last, gap - first - 2 * j)))
    for index in range(4 * fours, size):
        store(index - fours, get(index))


def unpack_rows(plan, get, size, north, store):
    first = plan.rows - HALO if north else 0
    gap = 0 if north else HALO
    row = row_of(plan.rows)
    fours = size // 4 if plan.packed(size) < size else 0
    for four in range(fours):
        last = None
        for j in range(3):
            tile = get(3 * four + j)
            store(4 * four + j, tile)
            moved = turn_rows(tile, first + 2 * j - gap)
            last = moved if last is None else jnp.where(row >= first + 2 * j, moved, last)
        store(4 * four + 3, last)
    for index in range(4 * fours, size):
        store(index, get(index - fours))


def by_parity(body):
    even = lax.rem(lax.axis_index("lat"), 2) == 0

    @pl.when(even)
    def _():
        body(True)

    @pl.when(jnp.logical_not(even))
    def _():
        body(False)


def pack_body(plan, *refs):
    sources, (own, swap_a, swap_b), sent = refs[:3], refs[3:6], refs[6:-4]
    field, courant, diffusion, arrived = refs[-4:]
    copies = [
        pltpu.make_async_copy(source, target, arrived.at[i])
        for i, (source, target) in enumerate(zip(sources, (field, courant, diffusion)))
    ]
    for copy in copies:
        copy.start()
    for copy in copies:
        copy.wait()
    me = lax.axis_index("lev")
    tiles = field_tiles(plan, field, courant, me)
    for level in range(plan.levels - 1):
        tiles += [diffusion_tile(plan, diffusion, level, t) for t in range(plan.diffusion_tiles)]
    for index, tile in enumerate(tiles):
        own[index] = tile
    edges = []
    for level in range(plan.levels - 1):
        first = diffusion_tile(plan, diffusion, level, 0)
        last = turn_lanes(diffusion_tile(plan, diffusion, level, plan.diffusion_tiles - 1), -plan.rest)
        edges.append(jnp.where(lane_of(plan.rows) < LANES // 2, first, last))
    edges = pack_lanes(edges, plan.edge_slots, 16)
    for turn in range(1, plan.devices):
        target = partner_of(me, turn, plan.devices)
        for index, tile in enumerate(field_tiles(plan, field, courant, target) + edges):
            sent[turn - 1][index] = tile

    def rows(even):
        for north, swap in ((even, swap_a), (not even, swap_b)):
            pack_rows(plan, lambda i: own[i], plan.own_size, north, swap.__setitem__)

    by_parity(rows)


def forward_rows_body(plan, *refs):
    turns = plan.devices - 1
    got, swap_a, swap_b = refs[:turns], refs[turns], refs[turns + 1]
    size = plan.packed(plan.sent_size)

    def rows(even):
        for north, swap in ((even, swap_a), (not even, swap_b)):
            for turn in range(turns):
                def store(index, tile, base=turn * size, swap=swap):
                    swap[base + index] = tile

                pack_rows(plan, lambda i, turn=turn: got[turn][i], plan.sent_size, north, store)

    by_parity(rows)


def place_fields(plan, base, get, targets):
    for kind, (target, at) in enumerate(targets):
        for level in range(plan.count):
            item = kind * plan.count + level
            for t in range(plan.full):
                target[base + level, at, t * LANES : (t + 1) * LANES] = get(item * plan.full + t)
            rest = get(plan.rests_at + item // plan.slots)
            target[base + level, at, plan.full * LANES :] = unpack_lanes(rest, item % plan.slots, plan.pitch)


def place_diffusion(plan, at, get, target):
    for level in range(plan.levels - 1):
        for t in range(plan.full):
            target[level, at, t * LANES : (t + 1) * LANES] = get(plan.diffusion_at + level * plan.diffusion_tiles + t)


def place_diffusion_rest(plan, me, at, mine, get, target):
    lane = lane_of(plan.rows)
    for level in range(plan.levels - 1):
        east = west = None
        for turn in range(1, plan.devices):
            edge = get(turn, plan.diffusion_at + level // plan.edge_slots)
            edge = unpack_lanes(edge, level % plan.edge_slots, 16)
            source = source_of(me, turn, plan.devices)
            if east is None:
                east = west = edge
            else:
                east = jnp.where(source == lax.rem(me + 1, plan.devices), edge, east)
                west = jnp.where(source == lax.rem(me + plan.devices - 1, plan.devices), edge, west)
        rest = jnp.where(lane < plan.middle, turn_lanes(east, plan.rest), west)
        target[level, at] = jnp.where(lane < plan.rest, mine(level), rest) if plan.rest else rest


def column_factors(plan, r, a, g):
    k_prev = gain = zero = jnp.zeros(g.shape[1:], F32)
    for level in range(plan.levels):
        k_next = g[level] if level < plan.levels - 1 else zero
        inverse = 1.0 / (1.0 + k_prev + k_next - k_prev * gain)
        gain = k_next * inverse
        r[level], a[level], g[level] = inverse, k_prev * inverse, gain
        k_prev = k_next


def split_zonal(plan, level, face_e, face_w):
    west = face_w[level]
    face_e[level] = jnp.maximum(pltpu.roll(west, plan.window - 1, 1), 0.0)
    face_w[level] = jnp.minimum(west, 0.0)


def sides(plan, even, swap_a, swap_b, begin):
    return (
        (True, slice(begin, begin + plan.rows), swap_a if even else swap_b),
        (False, slice(begin + plan.rows, begin + 2 * plan.rows), swap_b if even else swap_a),
    )


def early_shapes(plan):
    rows, window, full = plan.rows, plan.window, plan.full * LANES
    shapes = [(plan.levels, rows, window)] * 4 + [(plan.count, 2 * rows, window)] * 4
    shapes += [(plan.levels, rows, LANES)] * 3
    shapes += [(plan.levels, 3 * rows, full)] * 3 if full else []
    return shapes + ([(plan.levels, 2 * rows, LANES)] if plan.rest else [])


def early_body(plan, *refs):
    turns = plan.devices - 1
    own, swap_a, swap_b = refs[:3]
    lists = [own, *refs[3 : 3 + turns]]
    outs, unpacked = refs[3 + turns : -1], refs[-1]
    lam, face_e, face_w, lat = outs[:4]
    halo_lam, halo_e, halo_w, halo_lat = outs[4:8]
    rest_factors, full_factors = outs[8:11], outs[11:14]
    me = lax.axis_index("lev")
    rows = plan.rows
    at = slice(0, rows)
    for turn in range(plan.devices):
        base = (source_of(me, turn, plan.devices) if turn else me) * plan.count
        place_fields(plan, base, lists[turn].__getitem__, ((lam, at), (face_w, at), (lat, at)))
    if plan.full:
        place_diffusion(plan, at, own.__getitem__, full_factors[2])

    def mine(level):
        return own[plan.diffusion_at + level * plan.diffusion_tiles + plan.full]

    place_diffusion_rest(plan, me, at, mine, lambda turn, index: lists[turn][index], rest_factors[2])

    def halos(even):
        for north, at, swap in sides(plan, even, swap_a, swap_b, 0):
            unpack_rows(plan, swap.__getitem__, plan.own_size, not north, unpacked.__setitem__)
            place_fields(plan, 0, unpacked.__getitem__, ((halo_lam, at), (halo_w, at), (halo_lat, at)))
            if plan.full:
                below = slice(at.start + rows, at.stop + rows)
                place_diffusion(plan, below, unpacked.__getitem__, full_factors[2])
            if plan.rest:
                for level in range(plan.levels - 1):
                    outs[-1][level, at] = unpacked[plan.diffusion_at + level * plan.diffusion_tiles + plan.full]

    by_parity(halos)
    for level in range(plan.levels):
        split_zonal(plan, level, face_e, face_w)
    for level in range(plan.count):
        split_zonal(plan, level, halo_e, halo_w)
    column_factors(plan, *rest_factors)
    if plan.full:
        column_factors(plan, *full_factors)


def steps_body(plan, bands, *refs):
    turns = plan.devices - 1
    state = len(early_shapes(plan))
    own_lam, own_e, own_w, own_lat, early_lam, early_e, early_w, early_lat = refs[:8]
    own_factors, full_factors, left = refs[8:11], refs[11:14], refs[state - 1]
    swap_a, swap_b = refs[state : state + 2]
    outs = refs[state + 2 : state + 2 + plan.devices]
    flux, lam, halo_e, halo_w, lat_e, lat_w, *rest_factors, unpacked = refs[state + 2 + plan.devices :]
    me, band = lax.axis_index("lev"), lax.axis_index("lat")
    rows, levels = plan.rows, plan.levels
    packed = plan.packed(plan.sent_size)

    for level in range(levels):
        lam[level, :rows] = own_lam[level]
        lat_w[level, :rows] = own_lat[level]
    for level in range(plan.count):
        at = me * plan.count + level
        lam[at, rows:] = early_lam[level]
        lat_w[at, rows:] = early_lat[level]
        halo_e[at], halo_w[at] = early_e[level], early_w[level]

    def halos(even):
        for north, at, swap in sides(plan, even, swap_a, swap_b, rows):
            above = slice(at.start - rows, at.stop - rows)
            for turn in range(turns):
                def get(index, base=turn * packed, swap=swap):
                    return swap[base + index]

                def store(index, tile, base=turn * plan.sent_size):
                    unpacked[base + index] = tile

                unpack_rows(plan, get, plan.sent_size, not north, store)

            def tile_of(turn, index):
                return unpacked[(turn - 1) * plan.sent_size + index]

            for turn in range(1, plan.devices):
                base = source_of(me, turn, plan.devices) * plan.count
                get = functools.partial(tile_of, turn)
                place_fields(plan, base, get, ((lam, at), (halo_w, above), (lat_w, at)))
            place_diffusion_rest(plan, me, above, lambda level, above=above: left[level, above], tile_of, rest_factors[2])

    by_parity(halos)
    for turn in range(1, plan.devices):
        base = source_of(me, turn, plan.devices) * plan.count
        for level in range(plan.count):
            split_zonal(plan, base + level, halo_e, halo_w)
    row = lax.broadcasted_iota(jnp.int32, (3 * rows, plan.window), 0)
    closed = ((row == 0) & (band == 0)) | ((row == rows) & (band == bands - 1))
    for level in range(levels):
        south = jnp.where(closed, 0.0, lat_w[level])
        lat_e[level] = jnp.maximum(pltpu.roll(south, 3 * rows - 1, 0), 0.0)
        lat_w[level] = jnp.minimum(south, 0.0)
    column_factors(plan, *rest_factors)

    flux[...] = jnp.zeros_like(flux)
    zero = jnp.zeros((3 * rows, plan.window), F32)

    def factor(kind, level):
        rest = jnp.concatenate([own_factors[kind][level], rest_factors[kind][level]], axis=0)
        return jnp.concatenate([full_factors[kind][level], rest], axis=1) if plan.full else rest

    def step(_, carry):
        y = zero
        for level in range(levels):
            y = lam[level] * factor(0, level) + factor(1, level) * y
            lam[level] = y
        w = zero
        for level in range(levels - 1, -1, -1):
            w = lam[level] + factor(2, level) * w
            up, down = pltpu.roll(w, 3 * rows - 1, 0), pltpu.roll(w, 1, 0)
            v = w + lat_e[level] * (up - w) + lat_w[level] * (w - down)
            east, west = pltpu.roll(v, plan.window - 1, 1), pltpu.roll(v, 1, 1)
            face_e = jnp.concatenate([own_e[level], halo_e[level]], axis=0)
            face_w = jnp.concatenate([own_w[level], halo_w[level]], axis=0)
            lam[level] = v + face_e * (east - v) + face_w * (v - west)
        flux[...] += w[:rows, : plan.chunk]
        return carry

    lax.fori_loop(0, STEPS, step, 0)
    flux[...] = flux[...] / STEPS
    for turn in range(plan.devices):
        base = (partner_of(me, turn, plan.devices) if turn else me) * plan.count
        for level in range(plan.count):
            outs[turn][level] = lam[base + level, :rows, : plan.chunk]


def sum_body(plan, *refs):
    buckets, out = refs[:-1], refs[-1]
    count, rows, width = plan.count, plan.rows, plan.width
    cells = jnp.concatenate([bucket[count] for bucket in buckets], axis=0)
    tile = cells.shape[1]
    blocks = width // tile
    lane = lax.broadcasted_iota(jnp.int32, cells.shape, 1)
    place = (lane % rows * blocks + lane // rows).astype(F32)
    hits = jnp.where((cells == place) & (lane < rows * blocks), 1.0, 0.0)
    hits = hits.T[: rows * blocks]
    for level in range(count):
        values = jnp.concatenate([bucket[level] for bucket in buckets], axis=0)
        added = lax.dot_general(
            hits, values, (((1,), (0,)), ((), ())), precision=lax.Precision.HIGHEST, preferred_element_type=F32
        )
        for block in range(blocks):
            out[level, :, block * tile : (block + 1) * tile] = added[block * rows : (block + 1) * rows]


def finish_body(plan, *refs):
    parts, added, out = refs[: plan.devices], refs[plan.devices], refs[-1]
    me = lax.axis_index("lev")
    for level in range(plan.count):
        for q in range(plan.devices):
            piece = parts[0][level]
            for turn in range(1, plan.devices):
                piece = jnp.where(source_of(me, turn, plan.devices) == q, parts[turn][level], piece)
            at = slice(q * plan.chunk, (q + 1) * plan.chunk)
            out[level, :, at] = piece + added[level, :, at]


def bucket_body(regions, values, region_column, region_row, cell_column, *outs):
    count, tiles, tile = values.shape
    capacity = outs[0].shape[1]
    band = lax.axis_index("lat")
    earlier = lax.broadcasted_iota(jnp.int32, (tiles, tiles), 0) < lax.broadcasted_iota(jnp.int32, (tiles, tiles), 1)
    same = (region_column[...] == region_row[...]) & earlier
    rank = jnp.sum(jnp.where(same, 1.0, 0.0), axis=0, keepdims=True).astype(jnp.int32)
    slot = lax.broadcasted_iota(jnp.int32, (capacity, tiles), 0)
    cells = jnp.broadcast_to(cell_column[...].astype(F32), (tiles, tile))
    picks = [
        jnp.where((slot == rank) & (region_row[...] == partner_of(band, s, regions)), 1.0, 0.0) for s in range(regions)
    ]
    picks = jnp.concatenate(picks, axis=0)
    for level in range(count + 1):
        got = lax.dot_general(
            picks,
            cells if level == count else values[level],
            (((1,), (0,)), ((), ())),
            precision=lax.Precision.HIGHEST,
            preferred_element_type=F32,
        )
        for s in range(regions):
            outs[s][level] = got[s * capacity : (s + 1) * capacity]


def bucket_tiles(tile_values, tile_region, tile_cell):
    regions = lax.axis_size("lat")
    count, tiles, tile = tile_values.shape
    return call(
        functools.partial(bucket_body, regions),
        [(count + 1, tiles // 4, tile)] * regions,
        tile_values,
        tile_region,
        tile_region.reshape(1, tiles),
        tile_cell.reshape(tiles, 1),
    )

def local(adjoint_in, courant, diffusion, tile_values, tile_region, tile_cell):
    field = adjoint_in[0]
    count, rows, width = field.shape
    devices = lax.axis_size("lev")
    bands = lax.axis_size("lat")
    plan = Plan(count, rows, width, devices)
    tracers = lax.axis_size("tr")
    swaps_a, swaps_b = band_swaps(bands, tracers, 0), band_swaps(bands, tracers, 1)
    tile = (rows, LANES)

    early = plan.packed(plan.own_size)
    late = plan.packed(plan.sent_size) * (devices - 1)
    own, early_a, early_b, *sent = call(
        functools.partial(pack_body, plan),
        [(plan.own_size,) + tile] + [(early,) + tile] * 2 + [(plan.sent_size,) + tile] * (devices - 1),
        field,
        courant,
        diffusion,
        scratch=[field.shape, courant.shape, diffusion.shape],
        semaphores=3,
        inputs=pltpu.HBM,
    )
    got = [lax.ppermute(part, "lev", pairs) for part, pairs in zip(sent, rounds(devices))]
    early_b = lax.ppermute(early_b, ("lat", "tr"), swaps_b)
    early_a = lax.ppermute(early_a, ("lat", "tr"), swaps_a)
    late_a, late_b = call(functools.partial(forward_rows_body, plan), [(late,) + tile] * 2, *got)
    late_b = lax.ppermute(late_b, ("lat", "tr"), swaps_b)
    late_a = lax.ppermute(late_a, ("lat", "tr"), swaps_a)
    state = call(
        functools.partial(early_body, plan),
        early_shapes(plan),
        own,
        early_a,
        early_b,
        *got,
        scratch=[(plan.own_size,) + tile],
    )
    buckets = bucket_tiles(tile_values[0], tile_region, tile_cell)
    state, buckets = lax.optimization_barrier((state, buckets))
    buckets = [buckets[0]] + [lax.ppermute(part, "lat", pairs) for part, pairs in zip(buckets[1:], rounds(bands))]

    whole, halo = (plan.levels, 3 * rows, plan.window), (plan.levels, 2 * rows, plan.window)
    *outs, flux = call(
        functools.partial(steps_body, plan, bands),
        [(count, rows, plan.chunk)] * devices + [(rows, plan.chunk)],
        *state,
        late_a,
        late_b,
        scratch=[whole, halo, halo, whole, whole]
        + [(plan.levels, 2 * rows, LANES)] * 3
        + [((devices - 1) * plan.sent_size,) + tile],
    )
    parts = [outs[0]] + [lax.ppermute(part, "lev", pairs) for part, pairs in zip(outs[1:], rounds(devices))]
    (added,) = call(functools.partial(sum_body, plan), [(count, rows, width)], *buckets)
    (out,) = call(functools.partial(finish_body, plan), [(count, rows, width)], *parts, added)
    return out[None], flux[None]


def solution(mesh):
    return jax.shard_map(
        local,
        mesh=mesh,
        in_specs=(
            P(("groups", "tr"), "lev", "lat", None),
            P(None, "lev", "lat", None),
            P(None, "lat", "lev"),
            P(("groups", "tr"), "lev", "lat", None),
            P(("groups", "lat"), None),
            P(("groups", "lat")),
        ),
        out_specs=(P(("groups", "tr"), "lev", "lat", None), P(("groups", "tr"), "lat", "lev")),
        check_vma=False,
    )
```

```python
import functools

import jax
import jax.numpy as jnp
from jax import lax
from jax.experimental import pallas as pl
from jax.experimental.pallas import tpu as pltpu
from jax.sharding import PartitionSpec as P

STEPS = 6
HALO = STEPS
LANES = 128
F32 = jnp.float32


def call(body, out_shapes, *args, scratch=(), semaphores=0, inputs=pltpu.VMEM, keep=False):
    spec = pl.BlockSpec(memory_space=pltpu.VMEM)
    if inputs == pltpu.HBM:
        args = [pltpu.with_memory_space_constraint(arg, pltpu.HBM) for arg in args]
    shapes = [pltpu.VMEM(shape, F32) for shape in scratch]
    if semaphores:
        shapes.append(pltpu.SemaphoreType.DMA((semaphores,)))
    return pl.pallas_call(
        body,
        out_shape=[pltpu.VMEM(shape, F32) if keep else jax.ShapeDtypeStruct(shape, F32) for shape in out_shapes],
        in_specs=[pl.BlockSpec(memory_space=inputs)] * len(args),
        out_specs=[spec] * len(out_shapes),
        scratch_shapes=shapes,
        compiler_params=pltpu.CompilerParams(vmem_limit_bytes=16 * 1024 * 1024),
    )(*args)


def partner_of(index, turn, count):
    if count & (count - 1) == 0:
        return index ^ turn
    return (index + turn) % count


def source_of(index, turn, count):
    if count & (count - 1) == 0:
        return index ^ turn
    return (index - turn) % count


def rounds(count):
    return [[(b, partner_of(b, turn, count)) for b in range(count)] for turn in range(1, count)]


def band_swaps(bands, tracers, first):
    swaps = []
    for b in range(bands):
        partner = b + 1 if (b - first) % 2 == 0 else b - 1
        for t in range(tracers):
            if 0 <= partner < bands:
                swaps.append((b * tracers + t, partner * tracers + t))
            else:
                swaps.append((b * tracers + t, b * tracers + (t ^ 1 if tracers % 2 == 0 else t)))
    return swaps


class Plan:
    def __init__(self, count, rows, width, devices):
        self.count, self.rows, self.width, self.devices = count, rows, width, devices
        self.levels = count * devices
        self.chunk = width // devices
        self.full = self.chunk // LANES
        self.rest = self.chunk % LANES
        self.window = (self.full + 1) * LANES
        assert self.rest + 2 * HALO <= LANES
        self.middle = (self.rest + LANES) // 2
        self.pitch = -(-(self.rest + 2 * HALO) // 16) * 16
        self.slots = LANES // self.pitch
        self.edge_slots = LANES // 16
        fields = 3 * count
        self.rests_at = fields * self.full
        self.diffusion_at = self.rests_at + -(-fields // self.slots)
        self.diffusion_tiles = -(-self.chunk // LANES)
        self.own_size = self.diffusion_at + (self.levels - 1) * self.diffusion_tiles
        self.sent_size = self.diffusion_at + -(-(self.levels - 1) // self.edge_slots)

    def packed(self, size):
        return size - size // 4 if 4 * HALO == 3 * self.rows else size


def lane_of(rows=8):
    return lax.broadcasted_iota(jnp.int32, (rows, LANES), 1)


def row_of(rows=8):
    return lax.broadcasted_iota(jnp.int32, (rows, LANES), 0)


def turn_lanes(tile, shift):
    return pltpu.roll(tile, shift % LANES, 1) if shift % LANES else tile


def turn_rows(tile, shift):
    rows = tile.shape[0]
    return pltpu.roll(tile, shift % rows, 0) if shift % rows else tile


def pack_lanes(tiles, slots, pitch):
    packed = []
    lane = lane_of(tiles[0].shape[0])
    for begin in range(0, len(tiles), slots):
        total = jnp.zeros_like(tiles[0])
        for slot, tile in enumerate(tiles[begin : begin + slots]):
            moved = turn_lanes(tile, HALO + slot * pitch)
            if slots > 1:
                moved = jnp.where((lane >= slot * pitch) & (lane < (slot + 1) * pitch), moved, total)
            total = moved
        packed.append(total)
    return packed


def unpack_lanes(tile, slot, pitch):
    return turn_lanes(tile, -HALO - slot * pitch)


def window_tiles(plan, ref, index, target):
    if plan.rest == 0:
        def at(column):
            return ref[index + (slice(None), pl.ds(pl.multiple_of(column, LANES), LANES))]

        full = [at(target * plan.chunk + t * LANES) for t in range(plan.full)]
        east = at(lax.rem(target + 1, plan.devices) * plan.chunk)
        west = at(lax.rem(target + plan.devices - 1, plan.devices) * plan.chunk + plan.chunk - LANES)
    else:
        line = pltpu.roll(ref[index], lax.rem(plan.width - target * plan.chunk, plan.width), 1)
        full = [line[:, t * LANES : (t + 1) * LANES] for t in range(plan.full)]
        east = line[:, plan.full * LANES : (plan.full + 1) * LANES]
        west = line[:, plan.width - LANES :]
    return full, jnp.where(lane_of(plan.rows) < plan.middle, east, west)


def field_tiles(plan, field, courant, target):
    tiles, rests = [], []
    for ref, lead in ((field, ()), (courant, (0,)), (courant, (1,))):
        for level in range(plan.count):
            full, rest = window_tiles(plan, ref, lead + (level,), target)
            tiles += full
            rests.append(rest)
    return tiles + pack_lanes(rests, plan.slots, plan.pitch)


def diffusion_tile(plan, diffusion, level, t):
    width = min(LANES, plan.chunk - t * LANES)
    tile = diffusion[level, :, t * LANES : t * LANES + width]
    if width < LANES:
        tile = jnp.concatenate([tile, jnp.zeros((plan.rows, LANES - width), F32)], axis=1)
    return tile


def pack_rows(plan, get, size, north, store):
    first = plan.rows - HALO if north else 0
    gap = 0 if north else HALO
    row = row_of(plan.rows)
    kept = (row >= first) & (row < first + HALO)
    fours = size // 4 if plan.packed(size) < size else 0
    for four in range(fours):
        last = get(4 * four + 3)
        for j in range(3):
            store(3 * four + j, jnp.where(kept, get(4 * four + j), turn_rows(last, gap - first - 2 * j)))
    for index in range(4 * fours, size):
        store(index - fours, get(index))


def unpack_rows(plan, get, size, north, store):
    first = plan.rows - HALO if north else 0
    gap = 0 if north else HALO
    row = row_of(plan.rows)
    fours = size // 4 if plan.packed(size) < size else 0
    for four in range(fours):
        last = None
        for j in range(3):
            tile = get(3 * four + j)
            store(4 * four + j, tile)
            moved = turn_rows(tile, first + 2 * j - gap)
            last = moved if last is None else jnp.where(row >= first + 2 * j, moved, last)
        store(4 * four + 3, last)
    for index in range(4 * fours, size):
        store(index, get(index - fours))


def by_parity(body):
    even = lax.rem(lax.axis_index("lat"), 2) == 0

    @pl.when(even)
    def _():
        body(True)

    @pl.when(jnp.logical_not(even))
    def _():
        body(False)


def pack_body(plan, *refs):
    sources, (own, swap_a, swap_b), sent = refs[:3], refs[3:6], refs[6:-4]
    field, courant, diffusion, arrived = refs[-4:]
    copies = [
        pltpu.make_async_copy(source, target, arrived.at[i])
        for i, (source, target) in enumerate(zip(sources, (field, courant, diffusion)))
    ]
    for copy in copies:
        copy.start()
    for copy in copies:
        copy.wait()
    me = lax.axis_index("lev")
    tiles = field_tiles(plan, field, courant, me)
    for level in range(plan.levels - 1):
        tiles += [diffusion_tile(plan, diffusion, level, t) for t in range(plan.diffusion_tiles)]
    for index, tile in enumerate(tiles):
        own[index] = tile
    edges = []
    for level in range(plan.levels - 1):
        first = diffusion_tile(plan, diffusion, level, 0)
        last = turn_lanes(diffusion_tile(plan, diffusion, level, plan.diffusion_tiles - 1), -plan.rest)
        edges.append(jnp.where(lane_of(plan.rows) < LANES // 2, first, last))
    edges = pack_lanes(edges, plan.edge_slots, 16)
    for turn in range(1, plan.devices):
        target = partner_of(me, turn, plan.devices)
        for index, tile in enumerate(field_tiles(plan, field, courant, target) + edges):
            sent[turn - 1][index] = tile

    def rows(even):
        for north, swap in ((even, swap_a), (not even, swap_b)):
            pack_rows(plan, lambda i: own[i], plan.own_size, north, swap.__setitem__)

    by_parity(rows)


def forward_rows_body(plan, *refs):
    turns = plan.devices - 1
    got, swap_a, swap_b = refs[:turns], refs[turns], refs[turns + 1]
    size = plan.packed(plan.sent_size)

    def rows(even):
        for north, swap in ((even, swap_a), (not even, swap_b)):
            for turn in range(turns):
                def store(index, tile, base=turn * size, swap=swap):
                    swap[base + index] = tile

                pack_rows(plan, lambda i, turn=turn: got[turn][i], plan.sent_size, north, store)

    by_parity(rows)


def place_fields(plan, base, get, targets):
    for kind, (target, at) in enumerate(targets):
        for level in range(plan.count):
            item = kind * plan.count + level
            for t in range(plan.full):
                target[base + level, at, t * LANES : (t + 1) * LANES] = get(item * plan.full + t)
            rest = get(plan.rests_at + item // plan.slots)
            target[base + level, at, plan.full * LANES :] = unpack_lanes(rest, item % plan.slots, plan.pitch)


def place_diffusion(plan, at, get, target):
    for level in range(plan.levels - 1):
        for t in range(plan.full):
            target[level, at, t * LANES : (t + 1) * LANES] = get(plan.diffusion_at + level * plan.diffusion_tiles + t)


def place_diffusion_rest(plan, me, at, mine, get, target):
    lane = lane_of(plan.rows)
    for level in range(plan.levels - 1):
        east = west = None
        for turn in range(1, plan.devices):
            edge = get(turn, plan.diffusion_at + level // plan.edge_slots)
            edge = unpack_lanes(edge, level % plan.edge_slots, 16)
            source = source_of(me, turn, plan.devices)
            if east is None:
                east = west = edge
            else:
                east = jnp.where(source == lax.rem(me + 1, plan.devices), edge, east)
                west = jnp.where(source == lax.rem(me + plan.devices - 1, plan.devices), edge, west)
        rest = jnp.where(lane < plan.middle, turn_lanes(east, plan.rest), west)
        target[level, at] = jnp.where(lane < plan.rest, mine(level), rest) if plan.rest else rest


def column_factors(plan, r, a, g):
    k_prev = gain = zero = jnp.zeros(g.shape[1:], F32)
    for level in range(plan.levels):
        k_next = g[level] if level < plan.levels - 1 else zero
        inverse = 1.0 / (1.0 + k_prev + k_next - k_prev * gain)
        gain = k_next * inverse
        r[level], a[level], g[level] = inverse, k_prev * inverse, gain
        k_prev = k_next


def split_zonal(plan, level, face_e, face_w):
    west = face_w[level]
    face_e[level] = jnp.maximum(pltpu.roll(west, plan.window - 1, 1), 0.0)
    face_w[level] = jnp.minimum(west, 0.0)


def sides(plan, even, swap_a, swap_b, begin):
    return (
        (True, slice(begin, begin + plan.rows), swap_a if even else swap_b),
        (False, slice(begin + plan.rows, begin + 2 * plan.rows), swap_b if even else swap_a),
    )


def early_shapes(plan):
    rows, window, full = plan.rows, plan.window, plan.full * LANES
    shapes = [(plan.levels, rows, window)] * 4 + [(plan.count, 2 * rows, window)] * 4
    shapes += [(plan.levels, rows, LANES)] * 3
    shapes += [(plan.levels, 3 * rows, full)] * 3 + [(plan.levels, rows, full)] * 3 if full else []
    return shapes + ([(plan.levels, 2 * rows, LANES)] if plan.rest else [])


def early_body(plan, *refs):
    turns = plan.devices - 1
    own, swap_a, swap_b = refs[:3]
    lists = [own, *refs[3 : 3 + turns]]
    outs, unpacked = refs[3 + turns : -1], refs[-1]
    lam, face_e, face_w, lat = outs[:4]
    halo_lam, halo_e, halo_w, halo_lat = outs[4:8]
    rest_factors, full_factors = outs[8:11], outs[11:14]
    me = lax.axis_index("lev")
    rows = plan.rows
    at = slice(0, rows)
    for turn in range(plan.devices):
        base = (source_of(me, turn, plan.devices) if turn else me) * plan.count
        place_fields(plan, base, lists[turn].__getitem__, ((lam, at), (face_w, at), (lat, at)))
    if plan.full:
        place_diffusion(plan, at, own.__getitem__, full_factors[2])

    def mine(level):
        return own[plan.diffusion_at + level * plan.diffusion_tiles + plan.full]

    place_diffusion_rest(plan, me, at, mine, lambda turn, index: lists[turn][index], rest_factors[2])

    def halos(even):
        for north, at, swap in sides(plan, even, swap_a, swap_b, 0):
            unpack_rows(plan, swap.__getitem__, plan.own_size, not north, unpacked.__setitem__)
            place_fields(plan, 0, unpacked.__getitem__, ((halo_lam, at), (halo_w, at), (halo_lat, at)))
            if plan.full:
                below = slice(at.start + rows, at.stop + rows)
                place_diffusion(plan, below, unpacked.__getitem__, full_factors[2])
            if plan.rest:
                for level in range(plan.levels - 1):
                    outs[-1][level, at] = unpacked[plan.diffusion_at + level * plan.diffusion_tiles + plan.full]

    by_parity(halos)
    for level in range(plan.levels):
        split_zonal(plan, level, face_e, face_w)
    for level in range(plan.count):
        split_zonal(plan, level, halo_e, halo_w)
    column_factors(plan, *rest_factors)
    if plan.full:
        column_factors(plan, *full_factors)
        for narrow, factors in zip(outs[14:17], full_factors):
            for level in range(plan.levels):
                narrow[level] = near_rows(plan, factors[level, rows : 2 * rows], factors[level, 2 * rows :])


def near_rows(plan, north, south):
    return jnp.where(lax.broadcasted_iota(jnp.int32, north.shape, 0) < plan.rows // 2, north, south)


def steps_body(plan, bands, *refs):
    turns = plan.devices - 1
    state = len(early_shapes(plan))
    own_lam, own_e, own_w, own_lat, early_lam, early_e, early_w, early_lat = refs[:8]
    own_factors, full_factors, narrow_factors, left = refs[8:11], refs[11:14], refs[14:17], refs[state - 1]
    swap_a, swap_b = refs[state : state + 2]
    outs = refs[state + 2 : state + 2 + plan.devices]
    flux, lam, halo_e, halo_w, lat_e, lat_w, *rest_factors, unpacked = refs[state + 2 + plan.devices :]
    me, band = lax.axis_index("lev"), lax.axis_index("lat")
    rows, levels = plan.rows, plan.levels
    packed = plan.packed(plan.sent_size)

    for level in range(levels):
        lam[level, :rows] = own_lam[level]
        lat_w[level, :rows] = own_lat[level]
    for level in range(plan.count):
        at = me * plan.count + level
        lam[at, rows:] = early_lam[level]
        lat_w[at, rows:] = early_lat[level]
        halo_e[at], halo_w[at] = early_e[level], early_w[level]

    def halos(even):
        for north, at, swap in sides(plan, even, swap_a, swap_b, rows):
            above = slice(at.start - rows, at.stop - rows)
            for turn in range(turns):
                def get(index, base=turn * packed, swap=swap):
                    return swap[base + index]

                def store(index, tile, base=turn * plan.sent_size):
                    unpacked[base + index] = tile

                unpack_rows(plan, get, plan.sent_size, not north, store)

            def tile_of(turn, index):
                return unpacked[(turn - 1) * plan.sent_size + index]

            for turn in range(1, plan.devices):
                base = source_of(me, turn, plan.devices) * plan.count
                get = functools.partial(tile_of, turn)
                place_fields(plan, base, get, ((lam, at), (halo_w, above), (lat_w, at)))
            place_diffusion_rest(plan, me, above, lambda level, above=above: left[level, above], tile_of, rest_factors[2])

    by_parity(halos)
    for turn in range(1, plan.devices):
        base = source_of(me, turn, plan.devices) * plan.count
        for level in range(plan.count):
            split_zonal(plan, base + level, halo_e, halo_w)
    row = lax.broadcasted_iota(jnp.int32, (3 * rows, plan.window), 0)
    closed = ((row == 0) & (band == 0)) | ((row == rows) & (band == bands - 1))
    for level in range(levels):
        south = jnp.where(closed, 0.0, lat_w[level])
        lat_e[level] = jnp.maximum(pltpu.roll(south, 3 * rows - 1, 0), 0.0)
        lat_w[level] = jnp.minimum(south, 0.0)
    column_factors(plan, *rest_factors)

    flux[...] = jnp.zeros_like(flux)

    def factor(kind, level, height):
        rest = jnp.concatenate([own_factors[kind][level], rest_factors[kind][level, : height - rows]], axis=0)
        if not plan.full:
            return rest
        if height == 3 * rows:
            full = full_factors[kind][level]
        else:
            full = jnp.concatenate([full_factors[kind][level, :rows], narrow_factors[kind][level]], axis=0)
        return jnp.concatenate([full, rest], axis=1)

    def step(height, _, carry):
        y = w = jnp.zeros((height, plan.window), F32)
        for level in range(levels):
            y = lam[level, :height] * factor(0, level, height) + factor(1, level, height) * y
            lam[level, :height] = y
        for level in range(levels - 1, -1, -1):
            w = lam[level, :height] + factor(2, level, height) * w
            up, down = pltpu.roll(w, height - 1, 0), pltpu.roll(w, 1, 0)
            v = w + lat_e[level, :height] * (up - w) + lat_w[level, :height] * (w - down)
            east, west = pltpu.roll(v, plan.window - 1, 1), pltpu.roll(v, 1, 1)
            face_e = jnp.concatenate([own_e[level], halo_e[level, : height - rows]], axis=0)
            face_w = jnp.concatenate([own_w[level], halo_w[level, : height - rows]], axis=0)
            lam[level, :height] = v + face_e * (east - v) + face_w * (v - west)
        flux[...] += w[:rows, : plan.chunk]
        return carry

    wide = max(0, HALO - rows // 2)
    lax.fori_loop(0, wide, functools.partial(step, 3 * rows), 0)
    for level in range(levels):
        for ref, begin in ((lam, rows), (lat_e, rows), (lat_w, rows), (halo_e, 0), (halo_w, 0), *((f, 0) for f in rest_factors)):
            north, south = ref[level, begin : begin + rows], ref[level, begin + rows : begin + 2 * rows]
            ref[level, begin : begin + rows] = near_rows(plan, north, south)
    lax.fori_loop(wide, STEPS, functools.partial(step, 2 * rows), 0)
    flux[...] = flux[...] / STEPS
    for turn in range(plan.devices):
        base = (partner_of(me, turn, plan.devices) if turn else me) * plan.count
        for level in range(plan.count):
            outs[turn][level] = lam[base + level, :rows, : plan.chunk]


def sum_body(plan, *refs):
    buckets, out = refs[:-1], refs[-1]
    count, rows, width = plan.count, plan.rows, plan.width
    cells = jnp.concatenate([bucket[count] for bucket in buckets], axis=0)
    tile = cells.shape[1]
    blocks = width // tile
    lane = lax.broadcasted_iota(jnp.int32, cells.shape, 1)
    place = (lane % rows * blocks + lane // rows).astype(F32)
    hits = jnp.where((cells == place) & (lane < rows * blocks), 1.0, 0.0)
    hits = hits.T[: rows * blocks]
    for level in range(count):
        values = jnp.concatenate([bucket[level] for bucket in buckets], axis=0)
        added = lax.dot_general(
            hits, values, (((1,), (0,)), ((), ())), precision=lax.Precision.HIGHEST, preferred_element_type=F32
        )
        for block in range(blocks):
            out[level, :, block * tile : (block + 1) * tile] = added[block * rows : (block + 1) * rows]


def finish_body(plan, *refs):
    parts, added, out = refs[: plan.devices], refs[plan.devices], refs[-1]
    me = lax.axis_index("lev")
    for level in range(plan.count):
        for q in range(plan.devices):
            piece = parts[0][level]
            for turn in range(1, plan.devices):
                piece = jnp.where(source_of(me, turn, plan.devices) == q, parts[turn][level], piece)
            at = slice(q * plan.chunk, (q + 1) * plan.chunk)
            out[level, :, at] = piece + added[level, :, at]


def bucket_body(regions, values, region_column, region_row, cell_column, *outs):
    count, tiles, tile = values.shape
    capacity = outs[0].shape[1]
    band = lax.axis_index("lat")
    earlier = lax.broadcasted_iota(jnp.int32, (tiles, tiles), 0) < lax.broadcasted_iota(jnp.int32, (tiles, tiles), 1)
    same = (region_column[...] == region_row[...]) & earlier
    rank = jnp.sum(jnp.where(same, 1.0, 0.0), axis=0, keepdims=True).astype(jnp.int32)
    slot = lax.broadcasted_iota(jnp.int32, (capacity, tiles), 0)
    cells = jnp.broadcast_to(cell_column[...].astype(F32), (tiles, tile))
    picks = [
        jnp.where((slot == rank) & (region_row[...] == partner_of(band, s, regions)), 1.0, 0.0) for s in range(regions)
    ]
    picks = jnp.concatenate(picks, axis=0)
    for level in range(count + 1):
        got = lax.dot_general(
            picks,
            cells if level == count else values[level],
            (((1,), (0,)), ((), ())),
            precision=lax.Precision.HIGHEST,
            preferred_element_type=F32,
        )
        for s in range(regions):
            outs[s][level] = got[s * capacity : (s + 1) * capacity]


def bucket_tiles(tile_values, tile_region, tile_cell):
    regions = lax.axis_size("lat")
    count, tiles, tile = tile_values.shape
    return call(
        functools.partial(bucket_body, regions),
        [(count + 1, tiles // 4, tile)] * regions,
        tile_values,
        tile_region,
        tile_region.reshape(1, tiles),
        tile_cell.reshape(tiles, 1),
    )

def local(adjoint_in, courant, diffusion, tile_values, tile_region, tile_cell):
    field = adjoint_in[0]
    count, rows, width = field.shape
    devices = lax.axis_size("lev")
    bands = lax.axis_size("lat")
    plan = Plan(count, rows, width, devices)
    tracers = lax.axis_size("tr")
    swaps_a, swaps_b = band_swaps(bands, tracers, 0), band_swaps(bands, tracers, 1)
    tile = (rows, LANES)

    early = plan.packed(plan.own_size)
    late = plan.packed(plan.sent_size) * (devices - 1)
    own, early_a, early_b, *sent = call(
        functools.partial(pack_body, plan),
        [(plan.own_size,) + tile] + [(early,) + tile] * 2 + [(plan.sent_size,) + tile] * (devices - 1),
        field,
        courant,
        diffusion,
        scratch=[field.shape, courant.shape, diffusion.shape],
        semaphores=3,
        inputs=pltpu.HBM,
    )
    got = [lax.ppermute(part, "lev", pairs) for part, pairs in zip(sent, rounds(devices))]
    early_b = lax.ppermute(early_b, ("lat", "tr"), swaps_b)
    early_a = lax.ppermute(early_a, ("lat", "tr"), swaps_a)
    late_a, late_b = call(functools.partial(forward_rows_body, plan), [(late,) + tile] * 2, *got, keep=True)
    late_b = lax.ppermute(late_b, ("lat", "tr"), swaps_b)
    late_a = lax.ppermute(late_a, ("lat", "tr"), swaps_a)
    state = call(
        functools.partial(early_body, plan),
        early_shapes(plan),
        own,
        early_a,
        early_b,
        *got,
        scratch=[(plan.own_size,) + tile],
    )
    buckets = bucket_tiles(tile_values[0], tile_region, tile_cell)
    late_a, late_b, state, buckets = lax.optimization_barrier((late_a, late_b, state, buckets))
    buckets = [buckets[0]] + [lax.ppermute(part, "lat", pairs) for part, pairs in zip(buckets[1:], rounds(bands))]

    whole, halo = (plan.levels, 3 * rows, plan.window), (plan.levels, 2 * rows, plan.window)
    *outs, flux = call(
        functools.partial(steps_body, plan, bands),
        [(count, rows, plan.chunk)] * devices + [(rows, plan.chunk)],
        *state,
        late_a,
        late_b,
        scratch=[whole, halo, halo, whole, whole]
        + [(plan.levels, 2 * rows, LANES)] * 3
        + [((devices - 1) * plan.sent_size,) + tile],
    )
    parts = [outs[0]] + [lax.ppermute(part, "lev", pairs) for part, pairs in zip(outs[1:], rounds(devices))]
    (added,) = call(functools.partial(sum_body, plan), [(count, rows, width)], *buckets)
    (out,) = call(functools.partial(finish_body, plan), [(count, rows, width)], *parts, added)
    return out[None], flux[None]


def solution(mesh):
    return jax.shard_map(
        local,
        mesh=mesh,
        in_specs=(
            P(("groups", "tr"), "lev", "lat", None),
            P(None, "lev", "lat", None),
            P(None, "lat", "lev"),
            P(("groups", "tr"), "lev", "lat", None),
            P(("groups", "lat"), None),
            P(("groups", "lat")),
        ),
        out_specs=(P(("groups", "tr"), "lev", "lat", None), P(("groups", "tr"), "lat", "lev")),
        check_vma=False,
    )
```

```python
import functools

import jax
import jax.numpy as jnp
from jax import lax
from jax.experimental import pallas as pl
from jax.experimental.pallas import tpu as pltpu
from jax.sharding import PartitionSpec as P

STEPS = 6
HALO = STEPS
LANES = 128
F32 = jnp.float32


def call(body, out_shapes, *args, scratch=(), semaphores=0, inputs=pltpu.VMEM, keep=False):
    spec = pl.BlockSpec(memory_space=pltpu.VMEM)
    if inputs == pltpu.HBM:
        args = [pltpu.with_memory_space_constraint(arg, pltpu.HBM) for arg in args]
    shapes = [pltpu.VMEM(shape, F32) for shape in scratch]
    if semaphores:
        shapes.append(pltpu.SemaphoreType.DMA((semaphores,)))
    return pl.pallas_call(
        body,
        out_shape=[pltpu.VMEM(shape, F32) if keep else jax.ShapeDtypeStruct(shape, F32) for shape in out_shapes],
        in_specs=[pl.BlockSpec(memory_space=inputs)] * len(args),
        out_specs=[spec] * len(out_shapes),
        scratch_shapes=shapes,
        compiler_params=pltpu.CompilerParams(vmem_limit_bytes=16 * 1024 * 1024),
    )(*args)


def partner_of(index, turn, count):
    if count & (count - 1) == 0:
        return index ^ turn
    return (index + turn) % count


def source_of(index, turn, count):
    if count & (count - 1) == 0:
        return index ^ turn
    return (index - turn) % count


def rounds(count):
    return [[(b, partner_of(b, turn, count)) for b in range(count)] for turn in range(1, count)]


def band_swaps(bands, tracers, first):
    swaps = []
    for b in range(bands):
        partner = b + 1 if (b - first) % 2 == 0 else b - 1
        for t in range(tracers):
            if 0 <= partner < bands:
                swaps.append((b * tracers + t, partner * tracers + t))
            else:
                swaps.append((b * tracers + t, b * tracers + (t ^ 1 if tracers % 2 == 0 else t)))
    return swaps


class Plan:
    def __init__(self, count, rows, width, devices):
        self.count, self.rows, self.width, self.devices = count, rows, width, devices
        self.levels = count * devices
        self.chunk = width // devices
        self.full = self.chunk // LANES
        self.rest = self.chunk % LANES
        self.window = (self.full + 1) * LANES
        assert self.rest + 2 * HALO <= LANES
        self.middle = (self.rest + LANES) // 2
        self.pitch = -(-(self.rest + 2 * HALO) // 16) * 16
        self.slots = LANES // self.pitch
        self.edge_slots = LANES // 16
        fields = 3 * count
        self.rests_at = fields * self.full
        self.diffusion_at = self.rests_at + -(-fields // self.slots)
        self.diffusion_tiles = -(-self.chunk // LANES)
        self.own_size = self.diffusion_at + (self.levels - 1) * self.diffusion_tiles
        self.sent_size = self.diffusion_at + -(-(self.levels - 1) // self.edge_slots)

    def packed(self, size):
        return size - size // 4 if 4 * HALO == 3 * self.rows else size


def lane_of(rows=8):
    return lax.broadcasted_iota(jnp.int32, (rows, LANES), 1)


def row_of(rows=8):
    return lax.broadcasted_iota(jnp.int32, (rows, LANES), 0)


def turn_lanes(tile, shift):
    return pltpu.roll(tile, shift % LANES, 1) if shift % LANES else tile


def turn_rows(tile, shift):
    rows = tile.shape[0]
    return pltpu.roll(tile, shift % rows, 0) if shift % rows else tile


def pack_lanes(tiles, slots, pitch):
    packed = []
    lane = lane_of(tiles[0].shape[0])
    for begin in range(0, len(tiles), slots):
        total = jnp.zeros_like(tiles[0])
        for slot, tile in enumerate(tiles[begin : begin + slots]):
            moved = turn_lanes(tile, HALO + slot * pitch)
            if slots > 1:
                moved = jnp.where((lane >= slot * pitch) & (lane < (slot + 1) * pitch), moved, total)
            total = moved
        packed.append(total)
    return packed


def unpack_lanes(tile, slot, pitch):
    return turn_lanes(tile, -HALO - slot * pitch)


def window_tiles(plan, ref, index, target):
    if plan.rest == 0:
        def at(column):
            return ref[index + (slice(None), pl.ds(pl.multiple_of(column, LANES), LANES))]

        full = [at(target * plan.chunk + t * LANES) for t in range(plan.full)]
        east = at(lax.rem(target + 1, plan.devices) * plan.chunk)
        west = at(lax.rem(target + plan.devices - 1, plan.devices) * plan.chunk + plan.chunk - LANES)
    else:
        line = pltpu.roll(ref[index], lax.rem(plan.width - target * plan.chunk, plan.width), 1)
        full = [line[:, t * LANES : (t + 1) * LANES] for t in range(plan.full)]
        east = line[:, plan.full * LANES : (plan.full + 1) * LANES]
        west = line[:, plan.width - LANES :]
    return full, jnp.where(lane_of(plan.rows) < plan.middle, east, west)


def field_tiles(plan, field, courant, target):
    tiles, rests = [], []
    for ref, lead in ((field, ()), (courant, (0,)), (courant, (1,))):
        for level in range(plan.count):
            full, rest = window_tiles(plan, ref, lead + (level,), target)
            tiles += full
            rests.append(rest)
    return tiles + pack_lanes(rests, plan.slots, plan.pitch)


def diffusion_tile(plan, diffusion, level, t):
    width = min(LANES, plan.chunk - t * LANES)
    tile = diffusion[level, :, t * LANES : t * LANES + width]
    if width < LANES:
        tile = jnp.concatenate([tile, jnp.zeros((plan.rows, LANES - width), F32)], axis=1)
    return tile


def pack_rows(plan, get, size, north, store):
    first = plan.rows - HALO if north else 0
    gap = 0 if north else HALO
    row = row_of(plan.rows)
    kept = (row >= first) & (row < first + HALO)
    fours = size // 4 if plan.packed(size) < size else 0
    for four in range(fours):
        last = get(4 * four + 3)
        for j in range(3):
            store(3 * four + j, jnp.where(kept, get(4 * four + j), turn_rows(last, gap - first - 2 * j)))
    for index in range(4 * fours, size):
        store(index - fours, get(index))


def unpack_rows(plan, get, size, north, store):
    first = plan.rows - HALO if north else 0
    gap = 0 if north else HALO
    row = row_of(plan.rows)
    fours = size // 4 if plan.packed(size) < size else 0
    for four in range(fours):
        last = None
        for j in range(3):
            tile = get(3 * four + j)
            store(4 * four + j, tile)
            moved = turn_rows(tile, first + 2 * j - gap)
            last = moved if last is None else jnp.where(row >= first + 2 * j, moved, last)
        store(4 * four + 3, last)
    for index in range(4 * fours, size):
        store(index, get(index - fours))


def by_parity(body):
    even = lax.rem(lax.axis_index("lat"), 2) == 0

    @pl.when(even)
    def _():
        body(True)

    @pl.when(jnp.logical_not(even))
    def _():
        body(False)


def pack_body(plan, *refs):
    sources, own, sent = refs[:3], refs[3], refs[4:-4]
    field, courant, diffusion, arrived = refs[-4:]
    copies = [
        pltpu.make_async_copy(source, target, arrived.at[i])
        for i, (source, target) in enumerate(zip(sources, (field, courant, diffusion)))
    ]
    for copy in copies:
        copy.start()
    for copy in copies:
        copy.wait()
    me = lax.axis_index("lev")
    tiles = field_tiles(plan, field, courant, me)
    for level in range(plan.levels - 1):
        tiles += [diffusion_tile(plan, diffusion, level, t) for t in range(plan.diffusion_tiles)]
    for index, tile in enumerate(tiles):
        own[index] = tile
    edges = []
    for level in range(plan.levels - 1):
        first = diffusion_tile(plan, diffusion, level, 0)
        last = turn_lanes(diffusion_tile(plan, diffusion, level, plan.diffusion_tiles - 1), -plan.rest)
        edges.append(jnp.where(lane_of(plan.rows) < LANES // 2, first, last))
    edges = pack_lanes(edges, plan.edge_slots, 16)
    for turn in range(1, plan.devices):
        target = partner_of(me, turn, plan.devices)
        for index, tile in enumerate(field_tiles(plan, field, courant, target) + edges):
            sent[turn - 1][index] = tile


def pack_rows_body(plan, own, swap_a, swap_b):
    def rows(even):
        for north, swap in ((even, swap_a), (not even, swap_b)):
            pack_rows(plan, own.__getitem__, plan.own_size, north, swap.__setitem__)

    by_parity(rows)


def forward_rows_body(plan, *refs):
    turns = plan.devices - 1
    got, swap_a, swap_b = refs[:turns], refs[turns], refs[turns + 1]
    size = plan.packed(plan.sent_size)

    def rows(even):
        for north, swap in ((even, swap_a), (not even, swap_b)):
            for turn in range(turns):
                def store(index, tile, base=turn * size, swap=swap):
                    swap[base + index] = tile

                pack_rows(plan, lambda i, turn=turn: got[turn][i], plan.sent_size, north, store)

    by_parity(rows)


def place_fields(plan, base, get, targets):
    for kind, (target, at) in enumerate(targets):
        for level in range(plan.count):
            item = kind * plan.count + level
            for t in range(plan.full):
                target[base + level, at, t * LANES : (t + 1) * LANES] = get(item * plan.full + t)
            rest = get(plan.rests_at + item // plan.slots)
            target[base + level, at, plan.full * LANES :] = unpack_lanes(rest, item % plan.slots, plan.pitch)


def place_diffusion(plan, at, get, target):
    for level in range(plan.levels - 1):
        for t in range(plan.full):
            target[level, at, t * LANES : (t + 1) * LANES] = get(plan.diffusion_at + level * plan.diffusion_tiles + t)


def place_diffusion_rest(plan, me, at, mine, get, target):
    lane = lane_of(plan.rows)
    for level in range(plan.levels - 1):
        east = west = None
        for turn in range(1, plan.devices):
            edge = get(turn, plan.diffusion_at + level // plan.edge_slots)
            edge = unpack_lanes(edge, level % plan.edge_slots, 16)
            source = source_of(me, turn, plan.devices)
            if east is None:
                east = west = edge
            else:
                east = jnp.where(source == lax.rem(me + 1, plan.devices), edge, east)
                west = jnp.where(source == lax.rem(me + plan.devices - 1, plan.devices), edge, west)
        rest = jnp.where(lane < plan.middle, turn_lanes(east, plan.rest), west)
        target[level, at] = jnp.where(lane < plan.rest, mine(level), rest) if plan.rest else rest


def column_factors(plan, r, a, g):
    k_prev = gain = zero = jnp.zeros(g.shape[1:], F32)
    for level in range(plan.levels):
        k_next = g[level] if level < plan.levels - 1 else zero
        inverse = 1.0 / (1.0 + k_prev + k_next - k_prev * gain)
        gain = k_next * inverse
        r[level], a[level], g[level] = inverse, k_prev * inverse, gain
        k_prev = k_next


def split_zonal(plan, level, face_e, face_w):
    west = face_w[level]
    face_e[level] = jnp.maximum(pltpu.roll(west, plan.window - 1, 1), 0.0)
    face_w[level] = jnp.minimum(west, 0.0)


def sides(plan, even, swap_a, swap_b, begin):
    return (
        (True, slice(begin, begin + plan.rows), swap_a if even else swap_b),
        (False, slice(begin + plan.rows, begin + 2 * plan.rows), swap_b if even else swap_a),
    )


def early_shapes(plan):
    rows, window, full = plan.rows, plan.window, plan.full * LANES
    shapes = [(plan.levels, rows, window)] * 4 + [(plan.count, 2 * rows, window)] * 4
    shapes += [(plan.levels, rows, LANES)] * 3
    shapes += [(plan.levels, 3 * rows, full)] * 3 + [(plan.levels, rows, full)] * 3 if full else []
    return shapes + ([(plan.levels, 2 * rows, LANES)] if plan.rest else [])


def early_body(plan, *refs):
    turns = plan.devices - 1
    own, swap_a, swap_b = refs[:3]
    lists = [own, *refs[3 : 3 + turns]]
    outs, unpacked = refs[3 + turns : -1], refs[-1]
    lam, face_e, face_w, lat = outs[:4]
    halo_lam, halo_e, halo_w, halo_lat = outs[4:8]
    rest_factors, full_factors = outs[8:11], outs[11:14]
    me = lax.axis_index("lev")
    rows = plan.rows
    at = slice(0, rows)
    for turn in range(plan.devices):
        base = (source_of(me, turn, plan.devices) if turn else me) * plan.count
        place_fields(plan, base, lists[turn].__getitem__, ((lam, at), (face_w, at), (lat, at)))
    if plan.full:
        place_diffusion(plan, at, own.__getitem__, full_factors[2])

    def mine(level):
        return own[plan.diffusion_at + level * plan.diffusion_tiles + plan.full]

    place_diffusion_rest(plan, me, at, mine, lambda turn, index: lists[turn][index], rest_factors[2])

    def halos(even):
        for north, at, swap in sides(plan, even, swap_a, swap_b, 0):
            unpack_rows(plan, swap.__getitem__, plan.own_size, not north, unpacked.__setitem__)
            place_fields(plan, 0, unpacked.__getitem__, ((halo_lam, at), (halo_w, at), (halo_lat, at)))
            if plan.full:
                below = slice(at.start + rows, at.stop + rows)
                place_diffusion(plan, below, unpacked.__getitem__, full_factors[2])
            if plan.rest:
                for level in range(plan.levels - 1):
                    outs[-1][level, at] = unpacked[plan.diffusion_at + level * plan.diffusion_tiles + plan.full]

    by_parity(halos)
    for level in range(plan.levels):
        split_zonal(plan, level, face_e, face_w)
    for level in range(plan.count):
        split_zonal(plan, level, halo_e, halo_w)
    column_factors(plan, *rest_factors)
    if plan.full:
        column_factors(plan, *full_factors)
        for narrow, factors in zip(outs[14:17], full_factors):
            for level in range(plan.levels):
                narrow[level] = near_rows(plan, factors[level, rows : 2 * rows], factors[level, 2 * rows :])


def near_rows(plan, north, south):
    return jnp.where(lax.broadcasted_iota(jnp.int32, north.shape, 0) < plan.rows // 2, north, south)


def steps_body(plan, bands, *refs):
    turns = plan.devices - 1
    state = len(early_shapes(plan))
    own_lam, own_e, own_w, own_lat, early_lam, early_e, early_w, early_lat = refs[:8]
    own_factors, full_factors, narrow_factors, left = refs[8:11], refs[11:14], refs[14:17], refs[state - 1]
    swap_a, swap_b = refs[state : state + 2]
    outs = refs[state + 2 : state + 2 + plan.devices]
    flux, lam, halo_e, halo_w, lat_e, lat_w, *rest_factors, unpacked = refs[state + 2 + plan.devices :]
    me, band = lax.axis_index("lev"), lax.axis_index("lat")
    rows, levels = plan.rows, plan.levels
    packed = plan.packed(plan.sent_size)

    for level in range(levels):
        lam[level, :rows] = own_lam[level]
        lat_w[level, :rows] = own_lat[level]
    for level in range(plan.count):
        at = me * plan.count + level
        lam[at, rows:] = early_lam[level]
        lat_w[at, rows:] = early_lat[level]
        halo_e[at], halo_w[at] = early_e[level], early_w[level]

    def halos(even):
        for north, at, swap in sides(plan, even, swap_a, swap_b, rows):
            above = slice(at.start - rows, at.stop - rows)
            for turn in range(turns):
                def get(index, base=turn * packed, swap=swap):
                    return swap[base + index]

                def store(index, tile, base=turn * plan.sent_size):
                    unpacked[base + index] = tile

                unpack_rows(plan, get, plan.sent_size, not north, store)

            def tile_of(turn, index):
                return unpacked[(turn - 1) * plan.sent_size + index]

            for turn in range(1, plan.devices):
                base = source_of(me, turn, plan.devices) * plan.count
                get = functools.partial(tile_of, turn)
                place_fields(plan, base, get, ((lam, at), (halo_w, above), (lat_w, at)))
            place_diffusion_rest(plan, me, above, lambda level, above=above: left[level, above], tile_of, rest_factors[2])

    by_parity(halos)
    for turn in range(1, plan.devices):
        base = source_of(me, turn, plan.devices) * plan.count
        for level in range(plan.count):
            split_zonal(plan, base + level, halo_e, halo_w)
    row = lax.broadcasted_iota(jnp.int32, (3 * rows, plan.window), 0)
    closed = ((row == 0) & (band == 0)) | ((row == rows) & (band == bands - 1))
    for level in range(levels):
        south = jnp.where(closed, 0.0, lat_w[level])
        lat_e[level] = jnp.maximum(pltpu.roll(south, 3 * rows - 1, 0), 0.0)
        lat_w[level] = jnp.minimum(south, 0.0)
    column_factors(plan, *rest_factors)

    flux[...] = jnp.zeros_like(flux)

    def factor(kind, level, height):
        rest = jnp.concatenate([own_factors[kind][level], rest_factors[kind][level, : height - rows]], axis=0)
        if not plan.full:
            return rest
        if height == 3 * rows:
            full = full_factors[kind][level]
        else:
            full = jnp.concatenate([full_factors[kind][level, :rows], narrow_factors[kind][level]], axis=0)
        return jnp.concatenate([full, rest], axis=1)

    def step(height, kept, _, carry):
        y = w = jnp.zeros((height, plan.window), F32)
        for level in range(levels):
            y = lam[level, :height] * factor(0, level, height) + factor(1, level, height) * y
            lam[level, :height] = y
        for level in range(levels - 1, -1, -1):
            w = lam[level, :height] + factor(2, level, height) * w
            up, down, v = pltpu.roll(w, height - 1, 0)[:kept], pltpu.roll(w, 1, 0)[:kept], w[:kept]
            v = v + lat_e[level, :kept] * (up - v) + lat_w[level, :kept] * (v - down)
            east, west = pltpu.roll(v, plan.window - 1, 1), pltpu.roll(v, 1, 1)
            face_e, face_w = own_e[level], own_w[level]
            if kept > rows:
                face_e = jnp.concatenate([face_e, halo_e[level, : kept - rows]], axis=0)
                face_w = jnp.concatenate([face_w, halo_w[level, : kept - rows]], axis=0)
            lam[level, :kept] = v + face_e * (east - v) + face_w * (v - west)
        flux[...] += w[:rows, : plan.chunk]
        return carry

    wide = max(0, HALO - rows // 2)
    lax.fori_loop(0, wide, functools.partial(step, 3 * rows, 3 * rows), 0)
    for level in range(levels):
        for ref, begin in ((lam, rows), (lat_e, rows), (lat_w, rows), (halo_e, 0), (halo_w, 0), *((f, 0) for f in rest_factors)):
            north, south = ref[level, begin : begin + rows], ref[level, begin + rows : begin + 2 * rows]
            ref[level, begin : begin + rows] = near_rows(plan, north, south)
    lax.fori_loop(wide, STEPS - 1, functools.partial(step, 2 * rows, 2 * rows), 0)
    step(2 * rows, rows, 0, 0)
    flux[...] = flux[...] / STEPS
    for turn in range(plan.devices):
        base = (partner_of(me, turn, plan.devices) if turn else me) * plan.count
        for level in range(plan.count):
            outs[turn][level] = lam[base + level, :rows, : plan.chunk]


def sum_body(plan, *refs):
    buckets, out = refs[:-1], refs[-1]
    count, rows, width = plan.count, plan.rows, plan.width
    cells = jnp.concatenate([bucket[count] for bucket in buckets], axis=0)
    tile = cells.shape[1]
    blocks = width // tile
    lane = lax.broadcasted_iota(jnp.int32, cells.shape, 1)
    place = (lane % rows * blocks + lane // rows).astype(F32)
    hits = jnp.where((cells == place) & (lane < rows * blocks), 1.0, 0.0)
    hits = hits.T[: rows * blocks]
    for level in range(count):
        values = jnp.concatenate([bucket[level] for bucket in buckets], axis=0)
        added = lax.dot_general(
            hits, values, (((1,), (0,)), ((), ())), precision=lax.Precision.HIGHEST, preferred_element_type=F32
        )
        for block in range(blocks):
            out[level, :, block * tile : (block + 1) * tile] = added[block * rows : (block + 1) * rows]


def finish_body(plan, *refs):
    parts, added, out = refs[: plan.devices], refs[plan.devices], refs[-1]
    me = lax.axis_index("lev")
    for level in range(plan.count):
        for q in range(plan.devices):
            piece = parts[0][level]
            for turn in range(1, plan.devices):
                piece = jnp.where(source_of(me, turn, plan.devices) == q, parts[turn][level], piece)
            at = slice(q * plan.chunk, (q + 1) * plan.chunk)
            out[level, :, at] = piece + added[level, :, at]


def bucket_body(regions, values, region_column, region_row, cell_column, *outs):
    count, tiles, tile = values.shape
    capacity = outs[0].shape[1]
    band = lax.axis_index("lat")
    earlier = lax.broadcasted_iota(jnp.int32, (tiles, tiles), 0) < lax.broadcasted_iota(jnp.int32, (tiles, tiles), 1)
    same = (region_column[...] == region_row[...]) & earlier
    rank = jnp.sum(jnp.where(same, 1.0, 0.0), axis=0, keepdims=True).astype(jnp.int32)
    slot = lax.broadcasted_iota(jnp.int32, (capacity, tiles), 0)
    cells = jnp.broadcast_to(cell_column[...].astype(F32), (tiles, tile))
    picks = [
        jnp.where((slot == rank) & (region_row[...] == partner_of(band, s, regions)), 1.0, 0.0) for s in range(regions)
    ]
    picks = jnp.concatenate(picks, axis=0)
    for level in range(count + 1):
        got = lax.dot_general(
            picks,
            cells if level == count else values[level],
            (((1,), (0,)), ((), ())),
            precision=lax.Precision.HIGHEST,
            preferred_element_type=F32,
        )
        for s in range(regions):
            outs[s][level] = got[s * capacity : (s + 1) * capacity]


def bucket_tiles(tile_values, tile_region, tile_cell):
    regions = lax.axis_size("lat")
    count, tiles, tile = tile_values.shape
    return call(
        functools.partial(bucket_body, regions),
        [(count + 1, tiles // 4, tile)] * regions,
        tile_values,
        tile_region,
        tile_region.reshape(1, tiles),
        tile_cell.reshape(tiles, 1),
    )

def local(adjoint_in, courant, diffusion, tile_values, tile_region, tile_cell):
    field = adjoint_in[0]
    count, rows, width = field.shape
    devices = lax.axis_size("lev")
    bands = lax.axis_size("lat")
    plan = Plan(count, rows, width, devices)
    tracers = lax.axis_size("tr")
    swaps_a, swaps_b = band_swaps(bands, tracers, 0), band_swaps(bands, tracers, 1)
    tile = (rows, LANES)

    early = plan.packed(plan.own_size)
    late = plan.packed(plan.sent_size) * (devices - 1)
    own, *sent = call(
        functools.partial(pack_body, plan),
        [(plan.own_size,) + tile] + [(plan.sent_size,) + tile] * (devices - 1),
        field,
        courant,
        diffusion,
        scratch=[field.shape, courant.shape, diffusion.shape],
        semaphores=3,
        inputs=pltpu.HBM,
    )
    got = [lax.ppermute(part, "lev", pairs) for part, pairs in zip(sent, rounds(devices))]
    early_a, early_b = call(functools.partial(pack_rows_body, plan), [(early,) + tile] * 2, own)
    early_b = lax.ppermute(early_b, ("lat", "tr"), swaps_b)
    early_a = lax.ppermute(early_a, ("lat", "tr"), swaps_a)
    late_a, late_b = call(functools.partial(forward_rows_body, plan), [(late,) + tile] * 2, *got, keep=True)
    late_b = lax.ppermute(late_b, ("lat", "tr"), swaps_b)
    late_a = lax.ppermute(late_a, ("lat", "tr"), swaps_a)
    state = call(
        functools.partial(early_body, plan),
        early_shapes(plan),
        own,
        early_a,
        early_b,
        *got,
        scratch=[(plan.own_size,) + tile],
    )
    buckets = bucket_tiles(tile_values[0], tile_region, tile_cell)
    late_a, late_b, state, buckets = lax.optimization_barrier((late_a, late_b, state, buckets))
    crossing = {}
    for turn in sorted(range(1, bands), key=lambda turn: (turn == bands - 1, -turn)):
        crossing[turn] = lax.ppermute(buckets[turn], "lat", rounds(bands)[turn - 1])
    buckets = [buckets[0]] + [crossing[turn] for turn in range(1, bands)]

    whole, halo = (plan.levels, 3 * rows, plan.window), (plan.levels, 2 * rows, plan.window)
    *outs, flux = call(
        functools.partial(steps_body, plan, bands),
        [(count, rows, plan.chunk)] * devices + [(rows, plan.chunk)],
        *state,
        late_a,
        late_b,
        scratch=[whole, halo, halo, whole, whole]
        + [(plan.levels, 2 * rows, LANES)] * 3
        + [((devices - 1) * plan.sent_size,) + tile],
    )
    parts = [outs[0]] + [lax.ppermute(part, "lev", pairs) for part, pairs in zip(outs[1:], rounds(devices))]
    (added,) = call(functools.partial(sum_body, plan), [(count, rows, width)], *buckets)
    (out,) = call(functools.partial(finish_body, plan), [(count, rows, width)], *parts, added)
    return out[None], flux[None]


def solution(mesh):
    return jax.shard_map(
        local,
        mesh=mesh,
        in_specs=(
            P(("groups", "tr"), "lev", "lat", None),
            P(None, "lev", "lat", None),
            P(None, "lat", "lev"),
            P(("groups", "tr"), "lev", "lat", None),
            P(("groups", "lat"), None),
            P(("groups", "lat")),
        ),
        out_specs=(P(("groups", "tr"), "lev", "lat", None), P(("groups", "tr"), "lat", "lev")),
        check_vma=False,
    )
```

```python
import functools

import jax
import jax.numpy as jnp
from jax import lax
from jax.experimental import pallas as pl
from jax.experimental.pallas import tpu as pltpu
from jax.sharding import PartitionSpec as P

STEPS = 6
HALO = STEPS
LANES = 128
F32 = jnp.float32


def call(body, out_shapes, *args, scratch=(), semaphores=0, inputs=pltpu.VMEM):
    spec = pl.BlockSpec(memory_space=pltpu.VMEM)
    if inputs == pltpu.HBM:
        args = [pltpu.with_memory_space_constraint(arg, pltpu.HBM) for arg in args]
    shapes = [pltpu.VMEM(shape, F32) for shape in scratch]
    if semaphores:
        shapes.append(pltpu.SemaphoreType.DMA((semaphores,)))
    return pl.pallas_call(
        body,
        out_shape=[jax.ShapeDtypeStruct(shape, F32) for shape in out_shapes],
        in_specs=[pl.BlockSpec(memory_space=inputs)] * len(args),
        out_specs=[spec] * len(out_shapes),
        scratch_shapes=shapes,
        compiler_params=pltpu.CompilerParams(vmem_limit_bytes=16 * 1024 * 1024),
    )(*args)


def partner_of(index, turn, count):
    if count & (count - 1) == 0:
        return index ^ turn
    return (index + turn) % count


def source_of(index, turn, count):
    if count & (count - 1) == 0:
        return index ^ turn
    return (index - turn) % count


def rounds(count):
    return [[(b, partner_of(b, turn, count)) for b in range(count)] for turn in range(1, count)]


def band_swaps(bands, tracers, first):
    swaps = []
    for b in range(bands):
        partner = b + 1 if (b - first) % 2 == 0 else b - 1
        for t in range(tracers):
            if 0 <= partner < bands:
                swaps.append((b * tracers + t, partner * tracers + t))
            else:
                swaps.append((b * tracers + t, b * tracers + (t ^ 1 if tracers % 2 == 0 else t)))
    return swaps


class Plan:
    def __init__(self, count, rows, width, devices):
        self.count, self.rows, self.width, self.devices = count, rows, width, devices
        self.levels = count * devices
        self.chunk = width // devices
        self.full = self.chunk // LANES
        self.rest = self.chunk % LANES
        self.window = (self.full + 1) * LANES
        assert self.rest + 2 * HALO <= LANES
        self.middle = (self.rest + LANES) // 2
        self.pitch = -(-(self.rest + 2 * HALO) // 16) * 16
        self.slots = LANES // self.pitch
        self.edge_slots = LANES // 16
        fields = 3 * count
        self.rests_at = fields * self.full
        self.diffusion_at = self.rests_at + -(-fields // self.slots)
        self.diffusion_tiles = -(-self.chunk // LANES)
        self.own_size = self.diffusion_at + (self.levels - 1) * self.diffusion_tiles
        self.sent_size = self.diffusion_at + -(-(self.levels - 1) // self.edge_slots)

    def packed(self, size):
        return size - size // 4 if 4 * HALO == 3 * self.rows else size


def lane_of(rows=8):
    return lax.broadcasted_iota(jnp.int32, (rows, LANES), 1)


def row_of(rows=8):
    return lax.broadcasted_iota(jnp.int32, (rows, LANES), 0)


def turn_lanes(tile, shift):
    return pltpu.roll(tile, shift % LANES, 1) if shift % LANES else tile


def turn_rows(tile, shift):
    rows = tile.shape[0]
    return pltpu.roll(tile, shift % rows, 0) if shift % rows else tile


def pack_lanes(tiles, slots, pitch):
    packed = []
    lane = lane_of(tiles[0].shape[0])
    for begin in range(0, len(tiles), slots):
        total = jnp.zeros_like(tiles[0])
        for slot, tile in enumerate(tiles[begin : begin + slots]):
            moved = turn_lanes(tile, HALO + slot * pitch)
            if slots > 1:
                moved = jnp.where((lane >= slot * pitch) & (lane < (slot + 1) * pitch), moved, total)
            total = moved
        packed.append(total)
    return packed


def unpack_lanes(tile, slot, pitch):
    return turn_lanes(tile, -HALO - slot * pitch)


def window_tiles(plan, ref, index, target):
    if plan.rest == 0:
        def at(column):
            return ref[index + (slice(None), pl.ds(pl.multiple_of(column, LANES), LANES))]

        full = [at(target * plan.chunk + t * LANES) for t in range(plan.full)]
        east = at(lax.rem(target + 1, plan.devices) * plan.chunk)
        west = at(lax.rem(target + plan.devices - 1, plan.devices) * plan.chunk + plan.chunk - LANES)
    else:
        line = pltpu.roll(ref[index], lax.rem(plan.width - target * plan.chunk, plan.width), 1)
        full = [line[:, t * LANES : (t + 1) * LANES] for t in range(plan.full)]
        east = line[:, plan.full * LANES : (plan.full + 1) * LANES]
        west = line[:, plan.width - LANES :]
    return full, jnp.where(lane_of(plan.rows) < plan.middle, east, west)


def field_tiles(plan, field, courant, target):
    tiles, rests = [], []
    for ref, lead in ((field, ()), (courant, (0,)), (courant, (1,))):
        for level in range(plan.count):
            full, rest = window_tiles(plan, ref, lead + (level,), target)
            tiles += full
            rests.append(rest)
    return tiles + pack_lanes(rests, plan.slots, plan.pitch)


def diffusion_tile(plan, diffusion, level, t):
    width = min(LANES, plan.chunk - t * LANES)
    tile = diffusion[level, :, t * LANES : t * LANES + width]
    if width < LANES:
        tile = jnp.concatenate([tile, jnp.zeros((plan.rows, LANES - width), F32)], axis=1)
    return tile


def pack_rows(plan, get, size, north, store):
    first = plan.rows - HALO if north else 0
    gap = 0 if north else HALO
    row = row_of(plan.rows)
    kept = (row >= first) & (row < first + HALO)
    fours = size // 4 if plan.packed(size) < size else 0
    for four in range(fours):
        last = get(4 * four + 3)
        for j in range(3):
            store(3 * four + j, jnp.where(kept, get(4 * four + j), turn_rows(last, gap - first - 2 * j)))
    for index in range(4 * fours, size):
        store(index - fours, get(index))


def unpack_rows(plan, get, size, north, store):
    first = plan.rows - HALO if north else 0
    gap = 0 if north else HALO
    row = row_of(plan.rows)
    fours = size // 4 if plan.packed(size) < size else 0
    for four in range(fours):
        last = None
        for j in range(3):
            tile = get(3 * four + j)
            store(4 * four + j, tile)
            moved = turn_rows(tile, first + 2 * j - gap)
            last = moved if last is None else jnp.where(row >= first + 2 * j, moved, last)
        store(4 * four + 3, last)
    for index in range(4 * fours, size):
        store(index, get(index - fours))


def by_parity(body):
    even = lax.rem(lax.axis_index("lat"), 2) == 0

    @pl.when(even)
    def _():
        body(True)

    @pl.when(jnp.logical_not(even))
    def _():
        body(False)


def pack_body(plan, *refs):
    sources, own, sent = refs[:3], refs[3], refs[4:-4]
    field, courant, diffusion, arrived = refs[-4:]
    copies = [
        pltpu.make_async_copy(source, target, arrived.at[i])
        for i, (source, target) in enumerate(zip(sources, (field, courant, diffusion)))
    ]
    for copy in copies:
        copy.start()
    for copy in copies:
        copy.wait()
    me = lax.axis_index("lev")
    tiles = field_tiles(plan, field, courant, me)
    for level in range(plan.levels - 1):
        tiles += [diffusion_tile(plan, diffusion, level, t) for t in range(plan.diffusion_tiles)]
    for index, tile in enumerate(tiles):
        own[index] = tile
    edges = []
    for level in range(plan.levels - 1):
        first = diffusion_tile(plan, diffusion, level, 0)
        last = turn_lanes(diffusion_tile(plan, diffusion, level, plan.diffusion_tiles - 1), -plan.rest)
        edges.append(jnp.where(lane_of(plan.rows) < LANES // 2, first, last))
    edges = pack_lanes(edges, plan.edge_slots, 16)
    for turn in range(1, plan.devices):
        target = partner_of(me, turn, plan.devices)
        for index, tile in enumerate(field_tiles(plan, field, courant, target) + edges):
            sent[turn - 1][index] = tile


def pack_rows_body(plan, own, swap_a, swap_b):
    def rows(even):
        for north, swap in ((even, swap_a), (not even, swap_b)):
            pack_rows(plan, own.__getitem__, plan.own_size, north, swap.__setitem__)

    by_parity(rows)


def forward_rows_body(plan, first_swap, *refs):
    got, swap = refs[:-1], refs[-1]
    size = plan.packed(plan.sent_size)

    def rows(even):
        for turn, part in enumerate(got):
            def store(index, tile, base=turn * size):
                swap[base + index] = tile

            pack_rows(plan, part.__getitem__, plan.sent_size, even == first_swap, store)

    by_parity(rows)


def place_fields(plan, base, get, targets):
    for kind, (target, at) in enumerate(targets):
        for level in range(plan.count):
            item = kind * plan.count + level
            for t in range(plan.full):
                target[base + level, at, t * LANES : (t + 1) * LANES] = get(item * plan.full + t)
            rest = get(plan.rests_at + item // plan.slots)
            target[base + level, at, plan.full * LANES :] = unpack_lanes(rest, item % plan.slots, plan.pitch)


def place_diffusion(plan, at, get, target):
    for level in range(plan.levels - 1):
        for t in range(plan.full):
            target[level, at, t * LANES : (t + 1) * LANES] = get(plan.diffusion_at + level * plan.diffusion_tiles + t)


def place_diffusion_rest(plan, me, at, mine, get, target):
    lane = lane_of(plan.rows)
    for level in range(plan.levels - 1):
        east = west = None
        for turn in range(1, plan.devices):
            edge = get(turn, plan.diffusion_at + level // plan.edge_slots)
            edge = unpack_lanes(edge, level % plan.edge_slots, 16)
            source = source_of(me, turn, plan.devices)
            if east is None:
                east = west = edge
            else:
                east = jnp.where(source == lax.rem(me + 1, plan.devices), edge, east)
                west = jnp.where(source == lax.rem(me + plan.devices - 1, plan.devices), edge, west)
        rest = jnp.where(lane < plan.middle, turn_lanes(east, plan.rest), west)
        target[level, at] = jnp.where(lane < plan.rest, mine(level), rest) if plan.rest else rest


def column_factors(plan, r, a, g):
    k_prev = gain = zero = jnp.zeros(g.shape[1:], F32)
    for level in range(plan.levels):
        k_next = g[level] if level < plan.levels - 1 else zero
        inverse = 1.0 / (1.0 + k_prev + k_next - k_prev * gain)
        gain = k_next * inverse
        r[level], a[level], g[level] = inverse, k_prev * inverse, gain
        k_prev = k_next


def split_zonal(plan, level, face_e, face_w):
    west = face_w[level]
    face_e[level] = jnp.maximum(pltpu.roll(west, plan.window - 1, 1), 0.0)
    face_w[level] = jnp.minimum(west, 0.0)


def sides(plan, even, swap_a, swap_b, begin):
    return (
        (True, slice(begin, begin + plan.rows), swap_a if even else swap_b),
        (False, slice(begin + plan.rows, begin + 2 * plan.rows), swap_b if even else swap_a),
    )


def early_shapes(plan):
    rows, window, full = plan.rows, plan.window, plan.full * LANES
    shapes = [(plan.levels, rows, window)] * 4 + [(plan.count, 2 * rows, window)] * 4
    shapes += [(plan.levels, rows, LANES)] * 3
    shapes += [(plan.levels, 3 * rows, full)] * 3 + [(plan.levels, rows, full)] * 3 if full else []
    return shapes + ([(plan.levels, 2 * rows, LANES)] if plan.rest else [])


def early_body(plan, *refs):
    turns = plan.devices - 1
    own, swap_a, swap_b = refs[:3]
    lists = [own, *refs[3 : 3 + turns]]
    outs, unpacked = refs[3 + turns : -1], refs[-1]
    lam, face_e, face_w, lat = outs[:4]
    halo_lam, halo_e, halo_w, halo_lat = outs[4:8]
    rest_factors, full_factors = outs[8:11], outs[11:14]
    me = lax.axis_index("lev")
    rows = plan.rows
    at = slice(0, rows)
    for turn in range(plan.devices):
        base = (source_of(me, turn, plan.devices) if turn else me) * plan.count
        place_fields(plan, base, lists[turn].__getitem__, ((lam, at), (face_w, at), (lat, at)))
    if plan.full:
        place_diffusion(plan, at, own.__getitem__, full_factors[2])

    def mine(level):
        return own[plan.diffusion_at + level * plan.diffusion_tiles + plan.full]

    place_diffusion_rest(plan, me, at, mine, lambda turn, index: lists[turn][index], rest_factors[2])

    def halos(even):
        for north, at, swap in sides(plan, even, swap_a, swap_b, 0):
            unpack_rows(plan, swap.__getitem__, plan.own_size, not north, unpacked.__setitem__)
            place_fields(plan, 0, unpacked.__getitem__, ((halo_lam, at), (halo_w, at), (halo_lat, at)))
            if plan.full:
                below = slice(at.start + rows, at.stop + rows)
                place_diffusion(plan, below, unpacked.__getitem__, full_factors[2])
            if plan.rest:
                for level in range(plan.levels - 1):
                    outs[-1][level, at] = unpacked[plan.diffusion_at + level * plan.diffusion_tiles + plan.full]

    by_parity(halos)
    for level in range(plan.levels):
        split_zonal(plan, level, face_e, face_w)
    for level in range(plan.count):
        split_zonal(plan, level, halo_e, halo_w)
    column_factors(plan, *rest_factors)
    if plan.full:
        column_factors(plan, *full_factors)
        for narrow, factors in zip(outs[14:17], full_factors):
            for level in range(plan.levels):
                narrow[level] = near_rows(plan, factors[level, rows : 2 * rows], factors[level, 2 * rows :])


def near_rows(plan, north, south):
    return jnp.where(lax.broadcasted_iota(jnp.int32, north.shape, 0) < plan.rows // 2, north, south)


def steps_body(plan, bands, *refs):
    turns = plan.devices - 1
    state = len(early_shapes(plan))
    own_lam, own_e, own_w, own_lat, early_lam, early_e, early_w, early_lat = refs[:8]
    own_factors, full_factors, narrow_factors, left = refs[8:11], refs[11:14], refs[14:17], refs[state - 1]
    swap_a, swap_b = refs[state : state + 2]
    outs = refs[state + 2 : state + 2 + plan.devices]
    flux, lam, halo_e, halo_w, lat_e, lat_w, *rest_factors, unpacked = refs[state + 2 + plan.devices :]
    me, band = lax.axis_index("lev"), lax.axis_index("lat")
    rows, levels = plan.rows, plan.levels
    packed = plan.packed(plan.sent_size)

    for level in range(levels):
        lam[level, :rows] = own_lam[level]
        lat_w[level, :rows] = own_lat[level]
    for level in range(plan.count):
        at = me * plan.count + level
        lam[at, rows:] = early_lam[level]
        lat_w[at, rows:] = early_lat[level]
        halo_e[at], halo_w[at] = early_e[level], early_w[level]

    def halos(even):
        for north, at, swap in sides(plan, even, swap_a, swap_b, rows):
            above = slice(at.start - rows, at.stop - rows)
            for turn in range(turns):
                def get(index, base=turn * packed, swap=swap):
                    return swap[base + index]

                def store(index, tile, base=turn * plan.sent_size):
                    unpacked[base + index] = tile

                unpack_rows(plan, get, plan.sent_size, not north, store)

            def tile_of(turn, index):
                return unpacked[(turn - 1) * plan.sent_size + index]

            for turn in range(1, plan.devices):
                base = source_of(me, turn, plan.devices) * plan.count
                get = functools.partial(tile_of, turn)
                place_fields(plan, base, get, ((lam, at), (halo_w, above), (lat_w, at)))
            place_diffusion_rest(plan, me, above, lambda level, above=above: left[level, above], tile_of, rest_factors[2])

    by_parity(halos)
    for turn in range(1, plan.devices):
        base = source_of(me, turn, plan.devices) * plan.count
        for level in range(plan.count):
            split_zonal(plan, base + level, halo_e, halo_w)
    row = lax.broadcasted_iota(jnp.int32, (3 * rows, plan.window), 0)
    closed = ((row == 0) & (band == 0)) | ((row == rows) & (band == bands - 1))
    for level in range(levels):
        south = jnp.where(closed, 0.0, lat_w[level])
        lat_e[level] = jnp.maximum(pltpu.roll(south, 3 * rows - 1, 0), 0.0)
        lat_w[level] = jnp.minimum(south, 0.0)
    column_factors(plan, *rest_factors)

    flux[...] = jnp.zeros_like(flux)

    def factor(kind, level, height):
        rest = jnp.concatenate([own_factors[kind][level], rest_factors[kind][level, : height - rows]], axis=0)
        if not plan.full:
            return rest
        if height == 3 * rows:
            full = full_factors[kind][level]
        else:
            full = jnp.concatenate([full_factors[kind][level, :rows], narrow_factors[kind][level]], axis=0)
        return jnp.concatenate([full, rest], axis=1)

    def step(height, kept, _, carry):
        y = w = jnp.zeros((height, plan.window), F32)
        for level in range(levels):
            y = lam[level, :height] * factor(0, level, height) + factor(1, level, height) * y
            lam[level, :height] = y
        for level in range(levels - 1, -1, -1):
            w = lam[level, :height] + factor(2, level, height) * w
            up, down, v = pltpu.roll(w, height - 1, 0)[:kept], pltpu.roll(w, 1, 0)[:kept], w[:kept]
            v = v + lat_e[level, :kept] * (up - v) + lat_w[level, :kept] * (v - down)
            east, west = pltpu.roll(v, plan.window - 1, 1), pltpu.roll(v, 1, 1)
            face_e, face_w = own_e[level], own_w[level]
            if kept > rows:
                face_e = jnp.concatenate([face_e, halo_e[level, : kept - rows]], axis=0)
                face_w = jnp.concatenate([face_w, halo_w[level, : kept - rows]], axis=0)
            lam[level, :kept] = v + face_e * (east - v) + face_w * (v - west)
        flux[...] += w[:rows, : plan.chunk]
        return carry

    wide = max(0, HALO - rows // 2)
    lax.fori_loop(0, wide, functools.partial(step, 3 * rows, 3 * rows), 0)
    for level in range(levels):
        for ref, begin in ((lam, rows), (lat_e, rows), (lat_w, rows), (halo_e, 0), (halo_w, 0), *((f, 0) for f in rest_factors)):
            north, south = ref[level, begin : begin + rows], ref[level, begin + rows : begin + 2 * rows]
            ref[level, begin : begin + rows] = near_rows(plan, north, south)
    lax.fori_loop(wide, STEPS - 1, functools.partial(step, 2 * rows, 2 * rows), 0)
    step(2 * rows, rows, 0, 0)
    flux[...] = flux[...] / STEPS
    for turn in range(plan.devices):
        base = (partner_of(me, turn, plan.devices) if turn else me) * plan.count
        for level in range(plan.count):
            outs[turn][level] = lam[base + level, :rows, : plan.chunk]


def sum_body(plan, *refs):
    buckets, out = refs[:-1], refs[-1]
    count, rows, width = plan.count, plan.rows, plan.width
    cells = jnp.concatenate([bucket[count] for bucket in buckets], axis=0)
    tile = cells.shape[1]
    blocks = width // tile
    lane = lax.broadcasted_iota(jnp.int32, cells.shape, 1)
    place = (lane % rows * blocks + lane // rows).astype(F32)
    hits = jnp.where((cells == place) & (lane < rows * blocks), 1.0, 0.0)
    hits = hits.T[: rows * blocks]
    for level in range(count):
        values = jnp.concatenate([bucket[level] for bucket in buckets], axis=0)
        added = lax.dot_general(
            hits, values, (((1,), (0,)), ((), ())), precision=lax.Precision.HIGHEST, preferred_element_type=F32
        )
        for block in range(blocks):
            out[level, :, block * tile : (block + 1) * tile] = added[block * rows : (block + 1) * rows]


def finish_body(plan, *refs):
    parts, added, out = refs[: plan.devices], refs[plan.devices], refs[-1]
    me = lax.axis_index("lev")
    for level in range(plan.count):
        for q in range(plan.devices):
            piece = parts[0][level]
            for turn in range(1, plan.devices):
                piece = jnp.where(source_of(me, turn, plan.devices) == q, parts[turn][level], piece)
            at = slice(q * plan.chunk, (q + 1) * plan.chunk)
            out[level, :, at] = piece + added[level, :, at]


def bucket_body(regions, values, region_column, region_row, cell_column, *outs):
    count, tiles, tile = values.shape
    capacity = outs[0].shape[1]
    band = lax.axis_index("lat")
    earlier = lax.broadcasted_iota(jnp.int32, (tiles, tiles), 0) < lax.broadcasted_iota(jnp.int32, (tiles, tiles), 1)
    same = (region_column[...] == region_row[...]) & earlier
    rank = jnp.sum(jnp.where(same, 1.0, 0.0), axis=0, keepdims=True).astype(jnp.int32)
    slot = lax.broadcasted_iota(jnp.int32, (capacity, tiles), 0)
    cells = jnp.broadcast_to(cell_column[...].astype(F32), (tiles, tile))
    picks = [
        jnp.where((slot == rank) & (region_row[...] == partner_of(band, s, regions)), 1.0, 0.0) for s in range(regions)
    ]
    picks = jnp.concatenate(picks, axis=0)
    for level in range(count + 1):
        got = lax.dot_general(
            picks,
            cells if level == count else values[level],
            (((1,), (0,)), ((), ())),
            precision=lax.Precision.HIGHEST,
            preferred_element_type=F32,
        )
        for s in range(regions):
            outs[s][level] = got[s * capacity : (s + 1) * capacity]


def bucket_tiles(tile_values, tile_region, tile_cell):
    regions = lax.axis_size("lat")
    count, tiles, tile = tile_values.shape
    return call(
        functools.partial(bucket_body, regions),
        [(count + 1, tiles // 4, tile)] * regions,
        tile_values,
        tile_region,
        tile_region.reshape(1, tiles),
        tile_cell.reshape(tiles, 1),
    )

def local(adjoint_in, courant, diffusion, tile_values, tile_region, tile_cell):
    field = adjoint_in[0]
    count, rows, width = field.shape
    devices = lax.axis_size("lev")
    bands = lax.axis_size("lat")
    plan = Plan(count, rows, width, devices)
    tracers = lax.axis_size("tr")
    swaps_a, swaps_b = band_swaps(bands, tracers, 0), band_swaps(bands, tracers, 1)
    tile = (rows, LANES)

    early = plan.packed(plan.own_size)
    late = plan.packed(plan.sent_size) * (devices - 1)
    own, *sent = call(
        functools.partial(pack_body, plan),
        [(plan.own_size,) + tile] + [(plan.sent_size,) + tile] * (devices - 1),
        field,
        courant,
        diffusion,
        scratch=[field.shape, courant.shape, diffusion.shape],
        semaphores=3,
        inputs=pltpu.HBM,
    )
    got = [lax.ppermute(part, "lev", pairs) for part, pairs in zip(sent, rounds(devices))]
    early_a, early_b = call(functools.partial(pack_rows_body, plan), [(early,) + tile] * 2, own)
    early_b = lax.ppermute(early_b, ("lat", "tr"), swaps_b)
    early_a = lax.ppermute(early_a, ("lat", "tr"), swaps_a)
    (late_b,) = call(functools.partial(forward_rows_body, plan, False), [(late,) + tile], *got)
    (late_a,) = call(functools.partial(forward_rows_body, plan, True), [(late,) + tile], *got)
    late_b = lax.ppermute(late_b, ("lat", "tr"), swaps_b)
    late_a = lax.ppermute(late_a, ("lat", "tr"), swaps_a)
    state = call(
        functools.partial(early_body, plan),
        early_shapes(plan),
        own,
        early_a,
        early_b,
        *got,
        scratch=[(plan.own_size,) + tile],
    )
    buckets = bucket_tiles(tile_values[0], tile_region, tile_cell)
    late_a, late_b, state, buckets = lax.optimization_barrier((late_a, late_b, state, buckets))
    crossing = {}
    for turn in sorted(range(1, bands), key=lambda turn: (turn == bands - 1, -turn)):
        crossing[turn] = lax.ppermute(buckets[turn], "lat", rounds(bands)[turn - 1])
    buckets = [buckets[0]] + [crossing[turn] for turn in range(1, bands)]

    whole, halo = (plan.levels, 3 * rows, plan.window), (plan.levels, 2 * rows, plan.window)
    *outs, flux = call(
        functools.partial(steps_body, plan, bands),
        [(count, rows, plan.chunk)] * devices + [(rows, plan.chunk)],
        *state,
        late_a,
        late_b,
        scratch=[whole, halo, halo, whole, whole]
        + [(plan.levels, 2 * rows, LANES)] * 3
        + [((devices - 1) * plan.sent_size,) + tile],
    )
    parts = [outs[0]] + [lax.ppermute(part, "lev", pairs) for part, pairs in zip(outs[1:], rounds(devices))]
    (added,) = call(functools.partial(sum_body, plan), [(count, rows, width)], *buckets)
    (out,) = call(functools.partial(finish_body, plan), [(count, rows, width)], *parts, added)
    return out[None], flux[None]


def solution(mesh):
    return jax.shard_map(
        local,
        mesh=mesh,
        in_specs=(
            P(("groups", "tr"), "lev", "lat", None),
            P(None, "lev", "lat", None),
            P(None, "lat", "lev"),
            P(("groups", "tr"), "lev", "lat", None),
            P(("groups", "lat"), None),
            P(("groups", "lat")),
        ),
        out_specs=(P(("groups", "tr"), "lev", "lat", None), P(("groups", "tr"), "lat", "lev")),
        check_vma=False,
    )
```
